32 devices in a mesh: gx: 8 (over z, core), gy: 4 (over y, x).
Axes of the slice: x: 2, y: 2, z: 4, core: 2. Of those that a mesh axis runs over, the one named last changes fastest.
Arguments:
- masses: bfloat16 [256, 32, 32, 128], P(None, 'gx', 'gy'), may hold values from 0 to 1
- table: bfloat16 [256, 17], replicated, may hold values from 0.0009994507 to 0.019897461
- star_mask: int32 [32, 32, 128], P('gx', 'gy'), may hold values 0 or 1
- density: float32 [32, 32, 128], P('gx', 'gy'), may hold values from 0.1 to 10
- metals: float32 [16, 32, 32, 128], P(None, 'gx', 'gy'), may hold values from 0.1 to 1
- energy: float32 [32, 32, 128], P('gx', 'gy'), may hold values from 0.5 to 2
- courant_x: float32 [32, 32, 128], P('gx', 'gy'), may hold values from -0.3 to 0.3
- courant_y: float32 [32, 32, 128], P('gx', 'gy'), may hold values from -0.3 to 0.3
- courant_z: float32 [32, 32, 128], P('gx', 'gy'), may hold values from -0.3 to 0.3
Outputs:
- advected: float32 [16, 32, 32, 128], P(None, 'gx', 'gy')
- energy_out: float32 [32, 32, 128], P('gx', 'gy')
The draws below stay inside these ranges and needn't reach their ends.
Inputs may be any that keep to these rules, and one draw needn't show every extreme that they name: `star_mask`: 1 marks a star-forming cell, 0 any other.
All inputs are finite; a program needn't handle non-finite values. No bound on the sum of `star_mask` on one device may be relied on, other than what follows from the above.
Results may differ from the reference program's by a relative error of at most 0.0003.
Values sent between devices are 32-bit elements; how exact they have to be, the bound alone decides.
No kernel may reach another device: no remote copies, remote signals or barrier semaphores. Data moves between devices by JAX's collectives and lax.ppermute only.
A program may use at most 64 MiB of HBM per device.

```python
import math
import jax
import jax.numpy as jnp
from jax import lax

NMET = 16
BINS = 256
COMP = 17
NX = 32
NY = 32
NZ = 128


def place_ends(entries, key, least, largest):
    longest = entries.shape.index(max(entries.shape))
    spots = []
    for shift in (0, 1):
        where = [jax.random.randint(jax.random.fold_in(key, axis), (), 0, length) for axis, length in enumerate(entries.shape)]
        where[longest] = (where[longest] + shift) % entries.shape[longest]
        spots.append(tuple(where))
    return entries.at[spots[0]].set(least).at[spots[1]].set(largest)


def level_of(own_key, dims, split, smallest, high):
    level = 1.0
    for position, shards_of in split:
        draws = jax.random.uniform(jax.random.fold_in(jax.random.fold_in(own_key, 6), position), (shards_of,), jnp.float32, smallest / len(split), high / len(split))
        level = level * jnp.repeat(jnp.exp(draws), dims[position] // shards_of).reshape((-1,) + (1,) * (len(dims) - 1 - position))
    return level


def setup_inputs(seed: int = 0) -> dict:
    arg_keys = jax.random.split(jax.random.key(seed), 10)
    return {
        "masses": jnp.clip(1.0 * jax.random.uniform(arg_keys[0], (BINS, NX, NY, NZ), jnp.float32) ** level_of(arg_keys[0], (BINS, NX, NY, NZ), ((1, 8), (2, 4)), -0.2, 0.2), 0.0, 1.0).astype(jnp.bfloat16),
        "table": jnp.clip(jnp.exp(jax.random.uniform(arg_keys[1], (BINS, COMP), jnp.float32, math.log(0.0009994507), math.log(0.019897461))), 0.0009994507, 0.019897461).astype(jnp.bfloat16),
        "star_mask": place_ends((jax.random.randint(arg_keys[2], (NX, NY, NZ), 0, 2) < 1).astype(jnp.int32), jax.random.fold_in(arg_keys[2], 1), 0, 1),
        "density": jnp.clip(jnp.exp(math.log(10.0) - 4.6051702 * jax.random.uniform(arg_keys[3], (NX, NY, NZ), jnp.float32) ** level_of(arg_keys[3], (NX, NY, NZ), ((0, 8), (1, 4)), -0.2, 0.2)), 0.1, 10.0),
        "metals": jnp.clip(jnp.exp(math.log(1.0) - 2.3025851 * jax.random.uniform(arg_keys[4], (NMET, NX, NY, NZ), jnp.float32) ** level_of(arg_keys[4], (NMET, NX, NY, NZ), ((1, 8), (2, 4)), -0.2, 0.2)), 0.1, 1.0),
        "energy": jnp.clip(jnp.exp(math.log(2.0) - 1.3862944 * jax.random.uniform(arg_keys[5], (NX, NY, NZ), jnp.float32) ** level_of(arg_keys[5], (NX, NY, NZ), ((0, 8), (1, 4)), -0.2, 0.2)), 0.5, 2.0),
        "courant_x": jnp.clip(jax.random.uniform(arg_keys[6], (NX, NY, NZ), jnp.float32, -0.3, 0.3) * level_of(arg_keys[6], (NX, NY, NZ), ((0, 8), (1, 4)), -0.4, 0.0), -0.3, 0.3),
        "courant_y": jnp.clip(jax.random.uniform(arg_keys[7], (NX, NY, NZ), jnp.float32, -0.3, 0.3) * level_of(arg_keys[7], (NX, NY, NZ), ((0, 8), (1, 4)), -0.4, 0.0), -0.3, 0.3),
        "courant_z": jnp.clip(jax.random.uniform(arg_keys[8], (NX, NY, NZ), jnp.float32, -0.3, 0.3) * level_of(arg_keys[8], (NX, NY, NZ), ((0, 8), (1, 4)), -0.4, 0.0), -0.3, 0.3),
    }


def box_valid(padded):
    nx = padded.shape[-3] - 2
    ny = padded.shape[-2] - 2
    nz = padded.shape[-1] - 2
    total = None
    for a in range(3):
        for b in range(3):
            for c in range(3):
                piece = padded[..., a:a + nx, b:b + ny, c:c + nz]
                total = piece if total is None else total + piece
    return total


def take_part(array, axis, offset, shape):
    starts = [1, 1, 1]
    starts[axis] = starts[axis] + offset
    return array[..., starts[0]:starts[0] + shape[0], starts[1]:starts[1] + shape[1], starts[2]:starts[2] + shape[2]]


def advect(values, courant):
    inner = values[:, 1:-1, 1:-1, 1:-1]
    shape = inner.shape[1:]
    result = inner
    for axis in range(3):
        speed = courant[axis:axis + 1]
        lower_val = take_part(values, axis, -1, shape)
        upper_val = take_part(values, axis, 1, shape)
        speed_mid = take_part(speed, axis, 0, shape)
        speed_low = take_part(speed, axis, -1, shape)
        flux_up = jnp.maximum(speed_mid, 0.0) * inner + jnp.minimum(speed_mid, 0.0) * upper_val
        flux_low = jnp.maximum(speed_low, 0.0) * lower_val + jnp.minimum(speed_low, 0.0) * inner
        result = result - (flux_up - flux_low)
    return result


def reference(masses, table, star_mask, density, metals, energy, courant_x, courant_y, courant_z):
    sources = jnp.einsum("bk,bxyz->kxyz", table.astype(jnp.float32), masses.astype(jnp.float32), precision=lax.Precision.HIGHEST)
    sources = sources * star_mask.astype(jnp.float32)
    rim = [(1, 1), (1, 1), (1, 1)]
    weight_sum = box_valid(jnp.pad(density, rim))
    share = sources / weight_sum
    deposit = density * box_valid(jnp.pad(share, [(0, 0)] + rim))
    energy_out = energy + deposit[NMET]
    enriched = metals + deposit[:NMET]
    courant = jnp.stack([courant_x, courant_y, courant_z])
    advected = advect(jnp.pad(enriched, [(0, 0)] + rim), jnp.pad(courant, [(0, 0)] + rim))
    return advected, energy_out
```

```python
import jax
import jax.numpy as jnp
from jax import lax
from jax.experimental import pallas as pl
from jax.experimental.pallas import tpu as pltpu
from jax.sharding import PartitionSpec as P

F32 = jnp.float32
BF16 = jnp.bfloat16
BINS = 256
COMP = 17
NMET = 16
BX = 4
BY = 8
NZ = 128
CHUNKS = 4
YROWS = 216
XROWS = 424
CROWS = 128
PITCH = 24
DPITCH = 40


def rows(start, count, stride=1):
    return pl.ds(start, count) if stride == 1 else pl.ds(start, count, stride)


def sources_kernel(
    even_ref, masses_ref, table_ref, star_ref, dens_ref, metals_ref, cx_ref, cy_ref,
    src_ref, ya_ref, yb_ref, xa_ref, xb_ref,
    mass_buf, expand_ref, wide_ref, sems,
):
    per = BINS // CHUNKS
    copies = []
    for c in range(CHUNKS):
        copy = pltpu.make_async_copy(
            masses_ref.at[pl.ds(c * per, per)], mass_buf.at[pl.ds(c * per, per)], sems.at[c]
        )
        copy.start()
        copies.append(copy)

    width = BINS * 16
    spread = (
        lax.broadcasted_iota(jnp.int32, (BINS, width), 1) // 16
        == lax.broadcasted_iota(jnp.int32, (BINS, width), 0)
    ).astype(F32).astype(BF16)
    wide_ref[0:COMP, :] = lax.dot_general(
        table_ref[...], spread, (((0,), (0,)), ((), ())), preferred_element_type=F32
    )
    same = (
        lax.broadcasted_iota(jnp.int32, (16, width), 1) % 16
        == lax.broadcasted_iota(jnp.int32, (16, width), 0)
    )
    for k in range(COMP):
        line = jnp.broadcast_to(wide_ref[k : k + 1, :], (16, width))
        expand_ref[k * 16 : k * 16 + 16, :] = jnp.where(same, line, 0.0).astype(BF16)

    total = None
    for c in range(CHUNKS):
        copies[c].wait()
        part = mass_buf[c * per : (c + 1) * per]
        right = jnp.concatenate(
            [part[:, 16 * j : 16 * j + 16].reshape(per * 16, NZ) for j in range(2)], axis=1
        )
        left = expand_ref[:, c * per * 16 : (c + 1) * per * 16]
        prod = jnp.dot(left, right, preferred_element_type=F32)
        total = prod if total is None else total + prod
    for j in range(2):
        for s in range(2):
            x = 2 * j + s
            mask = star_ref[x * BY : x * BY + BY, :].astype(F32)
            for k in range(COMP):
                at = (k * BX + x) * BY
                piece = total[k * 16 + s * BY : k * 16 + s * BY + BY, j * NZ : (j + 1) * NZ]
                src_ref[at : at + BY, :] = piece * mask

    even_x = even_ref[0]
    even_y = even_ref[1]
    for out, high in ((ya_ref, even_y), (yb_ref, 1 - even_y)):
        near = jnp.where(high == 1, BY - 1, 0)
        step = jnp.where(high == 1, -1, 1)
        out[0:64, :] = src_ref[rows(near, 64, BY), :]
        out[64:128, :] = src_ref[rows(near + step, 64, BY), :]
        out[128:192, :] = metals_ref[rows(near, 64, BY), :]
        out[192:196, :] = src_ref[rows(NMET * BX * BY + near, 4, BY), :]
        out[196:200, :] = dens_ref[rows(near, 4, BY), :]
        out[200:204, :] = dens_ref[rows(near + step, 4, BY), :]
        out[204:208, :] = dens_ref[rows(near + 2 * step, 4, BY), :]
        out[208:212, :] = cy_ref[rows(near, 4, BY), :]
        out[212:216, :] = jnp.zeros((4, NZ), F32)
    for out, high in ((xa_ref, even_x), (xb_ref, 1 - even_x)):
        near = jnp.where(high == 1, BX - 1, 0) * BY
        step = jnp.where(high == 1, -1, 1) * BY
        tile = 0
        pieces = [(src_ref, k * BX * BY + near) for k in range(COMP)]
        pieces += [(src_ref, k * BX * BY + near + step) for k in range(NMET)]
        pieces += [(metals_ref, k * BX * BY + near) for k in range(NMET)]
        pieces += [(dens_ref, near), (dens_ref, near + step), (dens_ref, near + 2 * step)]
        pieces += [(cx_ref, near)]
        for ref, at in pieces:
            out[tile * BY : tile * BY + BY, :] = ref[pl.ds(pl.multiple_of(at, BY), BY), :]
            tile += 1


def corner_kernel(even_ref, ya_ref, yb_ref, ca_ref, cb_ref):
    even_x = even_ref[0]
    for out, high in ((ca_ref, even_x), (cb_ref, 1 - even_x)):
        near = jnp.where(high == 1, BX - 1, 0)
        step = jnp.where(high == 1, -1, 1)
        for side, y_ref in enumerate((ya_ref, yb_ref)):
            base = side * 64
            out[base : base + 16, :] = y_ref[rows(near, 16, BX), :]
            out[base + 16 : base + 32, :] = y_ref[rows(near + step, 16, BX), :]
            out[base + 32 : base + 48, :] = y_ref[rows(64 + near, 16, BX), :]
            out[base + 48 : base + 64, :] = y_ref[192:208, :]


def finish_kernel(
    even_ref, src_ref, ya_ref, yb_ref, xa_ref, xb_ref, ca_ref, cb_ref,
    dens_ref, metals_ref, energy_ref, cx_ref, cy_ref, cz_ref,
    out_ref, energy_out_ref,
    se_ref, de_ref, rw_ref, ys_ref, ee_ref, mx_ref, my_ref, cxl_ref, cye_ref,
):
    even_x = even_ref[0]
    even_y = even_ref[1]
    lane = lax.broadcasted_iota(jnp.int32, (1, NZ), 1)
    not_first = lane > 0
    not_last = lane < NZ - 1

    def prev_z(v):
        return pltpu.roll(v, 1, 1)

    def next_z(v):
        return pltpu.roll(v, NZ - 1, 1)

    de_ref[...] = jnp.zeros(de_ref.shape, F32)

    for x in range(BX):
        at = x * BY
        d_at = (x + 3) * DPITCH + 16
        de_ref[d_at : d_at + BY, :] = dens_ref[at : at + BY, :]
        cye_ref[x * PITCH + 8 : x * PITCH + 16, :] = cy_ref[at : at + BY, :]
        for k in range(COMP):
            s_at = (k * 8 + x + 2) * PITCH + 8
            se_ref[s_at : s_at + BY, :] = src_ref[(k * BX + x) * BY : (k * BX + x + 1) * BY, :]

    for y_ref, high in ((ya_ref, even_y), (yb_ref, 1 - even_y)):
        is_high = high == 1
        r1 = jnp.where(is_high, 16, 7)
        r2 = jnp.where(is_high, 17, 6)
        for k in range(NMET):
            at = k * BX
            base = (k * 8 + 2) * PITCH
            se_ref[rows(base + r1, BX, PITCH), :] = y_ref[at : at + BX, :]
            se_ref[rows(base + r2, BX, PITCH), :] = y_ref[64 + at : 64 + at + BX, :]
            my_ref[high, k * 8 + 2 : k * 8 + 2 + BX, :] = y_ref[128 + at : 128 + at + BX, :]
        base = (NMET * 8 + 2) * PITCH
        se_ref[rows(base + r1, BX, PITCH), :] = y_ref[192:196, :]
        for w in range(3):
            d_row = jnp.where(is_high, 24 + w, 15 - w)
            de_ref[rows(3 * DPITCH + d_row, BX, DPITCH), :] = y_ref[196 + 4 * w : 200 + 4 * w, :]
        cye_ref[rows(jnp.where(is_high, 16, 7), BX, PITCH), :] = y_ref[208:212, :]

    for x_ref, c_ref, high in ((xa_ref, ca_ref, even_x), (xb_ref, cb_ref, 1 - even_x)):
        is_high = high == 1
        p1 = jnp.where(is_high, 6, 1)
        p2 = jnp.where(is_high, 7, 0)
        for k in range(COMP):
            at = pl.multiple_of((k * 8 + p1) * PITCH + 8, 8)
            se_ref[pl.ds(at, BY), :] = x_ref[k * BY : k * BY + BY, :]
        for k in range(NMET):
            at = pl.multiple_of((k * 8 + p2) * PITCH + 8, 8)
            tile = COMP + k
            se_ref[pl.ds(at, BY), :] = x_ref[tile * BY : tile * BY + BY, :]
            tile = COMP + NMET + k
            mx_ref[high, k * BY : k * BY + BY, :] = x_ref[tile * BY : tile * BY + BY, :]
        for w in range(3):
            tile = COMP + 2 * NMET + w
            plane = jnp.where(is_high, 7 + w, 2 - w)
            at = pl.multiple_of(plane * DPITCH + 16, 8)
            de_ref[pl.ds(at, BY), :] = x_ref[tile * BY : tile * BY + BY, :]
        tile = COMP + 2 * NMET + 3
        cxl_ref[high] = x_ref[tile * BY : tile * BY + BY, :]
        for side, y_high in ((0, even_y), (1, 1 - even_y)):
            y_is_high = y_high == 1
            base = side * 64
            r1 = jnp.where(y_is_high, 16, 7)
            r2 = jnp.where(y_is_high, 17, 6)
            se_ref[rows(p1 * PITCH + r1, NMET, 8 * PITCH), :] = c_ref[base : base + 16, :]
            se_ref[rows(p2 * PITCH + r1, NMET, 8 * PITCH), :] = c_ref[base + 16 : base + 32, :]
            se_ref[rows(p1 * PITCH + r2, NMET, 8 * PITCH), :] = c_ref[base + 32 : base + 48, :]
            from_plane = jnp.where(is_high, 0, BX - 1)
            step = jnp.where(is_high, 1, -1)
            misc = base + 48 + from_plane
            se_ref[pl.ds((NMET * 8 + p1) * PITCH + r1, 1), :] = c_ref[pl.ds(misc, 1), :]
            for w in range(3):
                d_row = jnp.where(y_is_high, 24 + w, 15 - w)
                for q in range(3):
                    plane = jnp.where(is_high, 7 + q, 2 - q)
                    de_ref[pl.ds(plane * DPITCH + d_row, 1), :] = c_ref[
                        pl.ds(misc + 4 + 4 * w + q * step, 1), :
                    ]

    columns = []
    for p in range(10):
        at = p * DPITCH + 8
        columns.append(
            de_ref[at - 1 : at + 23, :] + de_ref[at : at + 24, :] + de_ref[at + 1 : at + 25, :]
        )
    for p in range(8):
        flat = columns[p] + columns[p + 1] + columns[p + 2]
        weight = flat + jnp.where(not_first, prev_z(flat), 0.0) + jnp.where(not_last, next_z(flat), 0.0)
        inside = weight > 0.0
        rw_ref[p * PITCH : (p + 1) * PITCH, :] = jnp.where(
            inside, 1.0 / jnp.where(inside, weight, 1.0), 0.0
        )

    for p in range(8):
        inv = [rw_ref[p * PITCH + 7 + d : p * PITCH + 15 + d, :] for d in range(3)]
        for k in range(COMP if 0 < p < 7 else NMET):
            at = (k * 8 + p) * PITCH + 7
            value = None
            for d in range(3):
                term = se_ref[at + d : at + d + BY, :] * inv[d]
                value = term if value is None else value + term
            ys_ref[(k * 8 + p) * BY : (k * 8 + p) * BY + BY, :] = value

    for p in range(1, 7):
        dens = de_ref[(p + 1) * DPITCH + 16 : (p + 1) * DPITCH + 24, :]
        dens_first = jnp.where(not_first, dens, 0.0)
        dens_last = jnp.where(not_last, dens, 0.0)
        for k in range(COMP if 1 < p < 6 else NMET):
            at = (k * 8 + p) * BY
            flat = ys_ref[at - BY : at, :] + ys_ref[at : at + BY, :] + ys_ref[at + BY : at + 2 * BY, :]
            deposit = dens * flat + dens_first * prev_z(flat) + dens_last * next_z(flat)
            if k == NMET:
                cell = (p - 2) * BY
                energy_out_ref[cell : cell + BY, :] = energy_ref[cell : cell + BY, :] + deposit
                continue
            if p == 1:
                metal = mx_ref[0, k * BY : k * BY + BY, :]
            elif p == 6:
                metal = mx_ref[1, k * BY : k * BY + BY, :]
            else:
                cell = (k * BX + p - 2) * BY
                metal = metals_ref[cell : cell + BY, :]
            e_at = (k * 8 + p) * PITCH + 8
            ee_ref[e_at : e_at + BY, :] = metal + deposit

    for side in range(2):
        row = (7, 16)[side]
        dens = de_ref[rows(DPITCH + row + 8, 8, DPITCH), :]
        dens_first = jnp.where(not_first, dens, 0.0)
        dens_last = jnp.where(not_last, dens, 0.0)
        inv = [rw_ref[rows(row - 1 + d, 8, PITCH), :] for d in range(3)]
        for k in range(NMET):
            value = None
            for d in range(3):
                term = se_ref[rows(k * 8 * PITCH + row - 1 + d, 8, PITCH), :] * inv[d]
                value = term if value is None else value + term
            flat = value + pltpu.roll(value, 1, 0) + pltpu.roll(value, 7, 0)
            deposit = dens * flat + dens_first * prev_z(flat) + dens_last * next_z(flat)
            ee_ref[rows(k * 8 * PITCH + row, 8, PITCH), :] = my_ref[side, k * 8 : k * 8 + 8, :] + deposit

    for x in range(BX):
        at = x * BY
        cx_up = cx_ref[at : at + BY, :]
        cx_low = cxl_ref[0] if x == 0 else cx_ref[at - BY : at, :]
        cy_up = cy_ref[at : at + BY, :]
        cy_low = cye_ref[x * PITCH + 7 : x * PITCH + 15, :]
        cz_up = cz_ref[at : at + BY, :]
        cz_low = jnp.where(not_first, prev_z(cz_up), 0.0)
        to_next = [-jnp.minimum(c, 0.0) for c in (cx_up, cy_up, cz_up)]
        from_prev = [jnp.maximum(c, 0.0) for c in (cx_low, cy_low, cz_low)]
        middle = 1.0
        for up, low in ((cx_up, cx_low), (cy_up, cy_low), (cz_up, cz_low)):
            middle = middle - jnp.maximum(up, 0.0) + jnp.minimum(low, 0.0)
        to_next[2] = jnp.where(not_last, to_next[2], 0.0)
        for k in range(NMET):
            e_at = (k * 8 + x + 2) * PITCH + 8
            own = ee_ref[e_at : e_at + BY, :]
            result = middle * own
            result = result + to_next[0] * ee_ref[e_at + PITCH : e_at + PITCH + BY, :]
            result = result + from_prev[0] * ee_ref[e_at - PITCH : e_at - PITCH + BY, :]
            result = result + to_next[1] * ee_ref[e_at + 1 : e_at + 1 + BY, :]
            result = result + from_prev[1] * ee_ref[e_at - 1 : e_at - 1 + BY, :]
            result = result + to_next[2] * next_z(own)
            result = result + from_prev[2] * prev_z(own)
            cell = (k * BX + x) * BY
            out_ref[cell : cell + BY, :] = result


def swaps(axis):
    count = lax.axis_size(axis)
    rounds = []
    for first in (0, 1):
        pairs = []
        for i in range(first, count - 1, 2):
            pairs += [(i, i + 1), (i + 1, i)]
        rounds.append(pairs)
    return rounds


VM = pl.BlockSpec(memory_space=pltpu.VMEM)
SM = pl.BlockSpec(memory_space=pltpu.SMEM)


def buffer(count):
    return pltpu.VMEM((count, NZ), F32)


def body(masses, table, star_mask, density, metals, energy, courant_x, courant_y, courant_z):
    cells = BX * BY
    even = jnp.stack([1 - lax.axis_index("gx") % 2, 1 - lax.axis_index("gy") % 2]).astype(jnp.int32)
    masses = masses.reshape(BINS, cells, NZ)
    star_mask, density, energy, courant_x, courant_y, courant_z = (
        a.reshape(cells, NZ) for a in (star_mask, density, energy, courant_x, courant_y, courant_z)
    )
    metals = metals.reshape(NMET * cells, NZ)
    src, ya, yb, xa, xb = pl.pallas_call(
        sources_kernel,
        name="sources",
        out_shape=[buffer(COMP * cells), buffer(YROWS), buffer(YROWS), buffer(XROWS), buffer(XROWS)],
        in_specs=[SM, pl.BlockSpec(memory_space=pl.ANY)] + [VM] * 6,
        out_specs=[VM] * 5,
        scratch_shapes=[
            pltpu.VMEM((BINS, cells, NZ), BF16),
            pltpu.VMEM((COMP * 16, BINS * 16), BF16),
            pltpu.VMEM((24, BINS * 16), F32),
            pltpu.SemaphoreType.DMA((CHUNKS,)),
        ],
        compiler_params=pltpu.CompilerParams(vmem_limit_bytes=32 * 1024 * 1024),
    )(even, masses, table, star_mask, density, metals, courant_x, courant_y)
    pairs_y = swaps("gy")
    pairs_x = swaps("gx")
    ya = lax.ppermute(ya, "gy", pairs_y[0])
    yb = lax.ppermute(yb, "gy", pairs_y[1])
    xa = lax.ppermute(xa, "gx", pairs_x[0])
    xb = lax.ppermute(xb, "gx", pairs_x[1])
    ca, cb = pl.pallas_call(
        corner_kernel,
        name="corners",
        out_shape=[buffer(CROWS), buffer(CROWS)],
        in_specs=[SM, VM, VM],
        out_specs=[VM, VM],
    )(even, ya, yb)
    ca = lax.ppermute(ca, "gx", pairs_x[0])
    cb = lax.ppermute(cb, "gx", pairs_x[1])
    advected, energy_out = pl.pallas_call(
        finish_kernel,
        name="finish",
        out_shape=[
            jax.ShapeDtypeStruct((NMET * cells, NZ), F32),
            jax.ShapeDtypeStruct((cells, NZ), F32),
        ],
        in_specs=[SM] + [VM] * 13,
        out_specs=[VM, VM],
        scratch_shapes=[
            pltpu.VMEM((COMP * 8 * PITCH, NZ), F32),
            pltpu.VMEM((10 * DPITCH, NZ), F32),
            pltpu.VMEM((8 * PITCH, NZ), F32),
            pltpu.VMEM((COMP * 8 * BY, NZ), F32),
            pltpu.VMEM((NMET * 8 * PITCH, NZ), F32),
            pltpu.VMEM((2, NMET * BY, NZ), F32),
            pltpu.VMEM((2, NMET * 8, NZ), F32),
            pltpu.VMEM((2, BY, NZ), F32),
            pltpu.VMEM((BX * PITCH, NZ), F32),
        ],
        compiler_params=pltpu.CompilerParams(vmem_limit_bytes=32 * 1024 * 1024),
    )(even, src, ya, yb, xa, xb, ca, cb, density, metals, energy, courant_x, courant_y, courant_z)
    return advected.reshape(NMET, BX, BY, NZ), energy_out.reshape(BX, BY, NZ)


def solution(mesh):
    field = P("gx", "gy", None)
    stack = P(None, "gx", "gy", None)
    in_specs = (stack, P(), field, field, stack, field, field, field, field)
    out_specs = (stack, field)
    return jax.shard_map(body, mesh=mesh, in_specs=in_specs, out_specs=out_specs, check_vma=False)
```

```python
import jax
import jax.numpy as jnp
from jax import lax
from jax.experimental import pallas as pl
from jax.experimental.pallas import tpu as pltpu
from jax.sharding import PartitionSpec as P

F32 = jnp.float32
BF16 = jnp.bfloat16
BINS = 256
COMP = 17
NMET = 16
BX = 4
BY = 8
NZ = 128
CHUNKS = 4
GROUP = 4
YROWS = 216
XROWS = 424
CROWS = 128
PITCH = 24
DPITCH = 40


def rows(start, count, stride=1):
    return pl.ds(start, count) if stride == 1 else pl.ds(start, count, stride)


def place(axis):
    index = lax.axis_index(axis)
    last = index == lax.axis_size(axis) - 1
    odd = index % 2
    alone_a = jnp.logical_and(odd == 0, last)
    alone_b = jnp.logical_or(index == 0, jnp.logical_and(odd == 1, last))
    return 1 - odd, alone_a, alone_b


def sources_kernel(
    masses_hbm, table_hbm, star_hbm, dens_hbm, metals_hbm, energy_hbm, cx_hbm, cy_hbm, cz_hbm,
    src_ref, ya_ref, yb_ref, xa_ref, xb_ref,
    dens_ref, metals_ref, energy_ref, cx_ref, cy_ref, cz_ref,
    mass_buf, table_ref, star_ref, expand_ref, wide_ref, mass_sems, sems,
):
    small = [
        (table_hbm, table_ref), (star_hbm, star_ref), (dens_hbm, dens_ref), (metals_hbm, metals_ref),
        (cx_hbm, cx_ref), (cy_hbm, cy_ref), (cz_hbm, cz_ref), (energy_hbm, energy_ref),
    ]
    small_copies = [
        pltpu.make_async_copy(hbm, ref, sems.at[i]) for i, (hbm, ref) in enumerate(small)
    ]
    per = BINS // CHUNKS
    copies = [
        pltpu.make_async_copy(
            masses_hbm.at[pl.ds(c * per, per)], mass_buf.at[pl.ds(c * per, per)], mass_sems.at[c]
        )
        for c in range(CHUNKS)
    ]
    small_copies[0].start()
    for copy in copies:
        copy.start()
    for copy in small_copies[1:]:
        copy.start()

    width = BINS * 16
    unit = (
        lax.broadcasted_iota(jnp.int32, (BINS, BINS), 0)
        == lax.broadcasted_iota(jnp.int32, (BINS, BINS), 1)
    ).astype(F32).astype(BF16)
    group = lax.broadcasted_iota(jnp.int32, (8, NZ), 1) // 16
    same = (
        lax.broadcasted_iota(jnp.int32, (16, NZ), 1) % 16
        == lax.broadcasted_iota(jnp.int32, (16, NZ), 0)
    )
    small_copies[0].wait()
    turned = lax.dot_general(
        table_ref[...], unit, (((0,), (0,)), ((), ())), preferred_element_type=F32
    )
    turned = jnp.concatenate([turned, jnp.zeros((24 - COMP, BINS), F32)], axis=0)
    for t in range(width // NZ):
        first = 8 * t
        half = first // NZ
        for r in range(3):
            tile = turned[8 * r : 8 * r + 8, half * NZ : (half + 1) * NZ]
            wide_ref[8 * r : 8 * r + 8, t * NZ : (t + 1) * NZ] = jnp.take_along_axis(
                tile, group + first % NZ, axis=1
            )
    for t in range(width // NZ):
        for k in range(COMP):
            line = jnp.broadcast_to(wide_ref[k : k + 1, t * NZ : (t + 1) * NZ], (16, NZ))
            expand_ref[k * 16 : k * 16 + 16, t * NZ : (t + 1) * NZ] = jnp.where(
                same, line, 0.0
            ).astype(BF16)

    total = None
    for c in range(CHUNKS):
        copies[c].wait()
        part = mass_buf[c * per : (c + 1) * per]
        right = jnp.concatenate(
            [part[:, 16 * j : 16 * j + 16].reshape(per * 16, NZ) for j in range(2)], axis=1
        )
        left = expand_ref[:, c * per * 16 : (c + 1) * per * 16]
        prod = jnp.dot(left, right, preferred_element_type=F32)
        total = prod if total is None else total + prod
    for copy in small_copies[1:]:
        copy.wait()
    for j in range(2):
        for s in range(2):
            x = 2 * j + s
            mask = star_ref[x * BY : x * BY + BY, :].astype(F32)
            for k in range(COMP):
                at = (k * BX + x) * BY
                piece = total[k * 16 + s * BY : k * 16 + s * BY + BY, j * NZ : (j + 1) * NZ]
                src_ref[at : at + BY, :] = piece * mask

    even_x, alone_xa, alone_xb = place("gx")
    even_y, alone_ya, alone_yb = place("gy")
    for out, high in ((ya_ref, even_y), (yb_ref, 1 - even_y)):
        near = jnp.where(high == 1, BY - 1, 0)
        step = jnp.where(high == 1, -1, 1)
        out[0:64, :] = src_ref[rows(near, 64, BY), :]
        out[64:128, :] = src_ref[rows(near + step, 64, BY), :]
        out[128:192, :] = metals_ref[rows(near, 64, BY), :]
        out[192:196, :] = src_ref[rows(NMET * BX * BY + near, 4, BY), :]
        out[196:200, :] = dens_ref[rows(near, 4, BY), :]
        out[200:204, :] = dens_ref[rows(near + step, 4, BY), :]
        out[204:208, :] = dens_ref[rows(near + 2 * step, 4, BY), :]
        out[208:212, :] = cy_ref[rows(near, 4, BY), :]
        out[212:216, :] = jnp.zeros((4, NZ), F32)
    for out, high in ((xa_ref, even_x), (xb_ref, 1 - even_x)):
        near = jnp.where(high == 1, BX - 1, 0) * BY
        step = jnp.where(high == 1, -1, 1) * BY
        tile = 0
        pieces = [(src_ref, k * BX * BY + near) for k in range(COMP)]
        pieces += [(src_ref, k * BX * BY + near + step) for k in range(NMET)]
        pieces += [(metals_ref, k * BX * BY + near) for k in range(NMET)]
        pieces += [(dens_ref, near), (dens_ref, near + step), (dens_ref, near + 2 * step)]
        pieces += [(cx_ref, near)]
        for ref, at in pieces:
            out[tile * BY : tile * BY + BY, :] = ref[pl.ds(pl.multiple_of(at, BY), BY), :]
            tile += 1
    for out, alone in ((ya_ref, alone_ya), (yb_ref, alone_yb), (xa_ref, alone_xa), (xb_ref, alone_xb)):
        clear(out, alone)


def clear(ref, alone):
    @pl.when(alone)
    def _():
        ref[...] = jnp.zeros(ref.shape, F32)


def corner_kernel(ya_ref, yb_ref, ca_ref, cb_ref):
    even_x, alone_a, alone_b = place("gx")
    for out, high in ((ca_ref, even_x), (cb_ref, 1 - even_x)):
        near = jnp.where(high == 1, BX - 1, 0)
        step = jnp.where(high == 1, -1, 1)
        for side, y_ref in enumerate((ya_ref, yb_ref)):
            base = side * 64
            out[base : base + 16, :] = y_ref[rows(near, 16, BX), :]
            out[base + 16 : base + 32, :] = y_ref[rows(near + step, 16, BX), :]
            out[base + 32 : base + 48, :] = y_ref[rows(64 + near, 16, BX), :]
            out[base + 48 : base + 64, :] = y_ref[192:208, :]
    clear(ca_ref, alone_a)
    clear(cb_ref, alone_b)


def finish_kernel(
    src_ref, ya_ref, yb_ref, xa_ref, xb_ref, ca_ref, cb_ref,
    dens_ref, metals_ref, energy_ref, cx_ref, cy_ref, cz_ref,
    out_hbm, energy_out_hbm,
    out_ref, energy_out_ref, sems,
    se_ref, de_ref, rw_ref, ys_ref, ee_ref, mx_ref, my_ref, cxl_ref, cye_ref,
):
    even_x = place("gx")[0]
    even_y = place("gy")[0]
    lane = lax.broadcasted_iota(jnp.int32, (1, NZ), 1)
    not_first = lane > 0
    not_last = lane < NZ - 1

    def prev_z(v):
        return pltpu.roll(v, 1, 1)

    def next_z(v):
        return pltpu.roll(v, NZ - 1, 1)

    def masked_prev(v):
        return jnp.where(not_first, prev_z(v), 0.0)

    def masked_next(v):
        return jnp.where(not_last, next_z(v), 0.0)

    de_ref[...] = jnp.zeros(de_ref.shape, F32)

    for x in range(BX):
        at = x * BY
        d_at = (x + 3) * DPITCH + 16
        de_ref[d_at : d_at + BY, :] = dens_ref[at : at + BY, :]
        cye_ref[x * PITCH + 8 : x * PITCH + 16, :] = cy_ref[at : at + BY, :]
        for k in range(COMP):
            s_at = (k * 8 + x + 2) * PITCH + 8
            se_ref[s_at : s_at + BY, :] = src_ref[(k * BX + x) * BY : (k * BX + x + 1) * BY, :]

    for y_ref, high in ((ya_ref, even_y), (yb_ref, 1 - even_y)):
        is_high = high == 1
        r1 = jnp.where(is_high, 16, 7)
        r2 = jnp.where(is_high, 17, 6)
        for k in range(NMET):
            at = k * BX
            base = (k * 8 + 2) * PITCH
            se_ref[rows(base + r1, BX, PITCH), :] = y_ref[at : at + BX, :]
            se_ref[rows(base + r2, BX, PITCH), :] = y_ref[64 + at : 64 + at + BX, :]
            my_ref[high, k * 8 + 2 : k * 8 + 2 + BX, :] = y_ref[128 + at : 128 + at + BX, :]
        base = (NMET * 8 + 2) * PITCH
        se_ref[rows(base + r1, BX, PITCH), :] = y_ref[192:196, :]
        for w in range(3):
            d_row = jnp.where(is_high, 24 + w, 15 - w)
            de_ref[rows(3 * DPITCH + d_row, BX, DPITCH), :] = y_ref[196 + 4 * w : 200 + 4 * w, :]
        cye_ref[rows(jnp.where(is_high, 16, 7), BX, PITCH), :] = y_ref[208:212, :]

    for x_ref, c_ref, high in ((xa_ref, ca_ref, even_x), (xb_ref, cb_ref, 1 - even_x)):
        is_high = high == 1
        p1 = jnp.where(is_high, 6, 1)
        p2 = jnp.where(is_high, 7, 0)
        for k in range(COMP):
            at = pl.multiple_of((k * 8 + p1) * PITCH + 8, 8)
            se_ref[pl.ds(at, BY), :] = x_ref[k * BY : k * BY + BY, :]
        for k in range(NMET):
            at = pl.multiple_of((k * 8 + p2) * PITCH + 8, 8)
            tile = COMP + k
            se_ref[pl.ds(at, BY), :] = x_ref[tile * BY : tile * BY + BY, :]
            tile = COMP + NMET + k
            mx_ref[high, k * BY : k * BY + BY, :] = x_ref[tile * BY : tile * BY + BY, :]
        for w in range(3):
            tile = COMP + 2 * NMET + w
            plane = jnp.where(is_high, 7 + w, 2 - w)
            at = pl.multiple_of(plane * DPITCH + 16, 8)
            de_ref[pl.ds(at, BY), :] = x_ref[tile * BY : tile * BY + BY, :]
        tile = COMP + 2 * NMET + 3
        cxl_ref[high] = x_ref[tile * BY : tile * BY + BY, :]
        for side, y_high in ((0, even_y), (1, 1 - even_y)):
            y_is_high = y_high == 1
            base = side * 64
            r1 = jnp.where(y_is_high, 16, 7)
            r2 = jnp.where(y_is_high, 17, 6)
            se_ref[rows(p1 * PITCH + r1, NMET, 8 * PITCH), :] = c_ref[base : base + 16, :]
            se_ref[rows(p2 * PITCH + r1, NMET, 8 * PITCH), :] = c_ref[base + 16 : base + 32, :]
            se_ref[rows(p1 * PITCH + r2, NMET, 8 * PITCH), :] = c_ref[base + 32 : base + 48, :]
            from_plane = jnp.where(is_high, 0, BX - 1)
            step = jnp.where(is_high, 1, -1)
            misc = base + 48 + from_plane
            se_ref[pl.ds((NMET * 8 + p1) * PITCH + r1, 1), :] = c_ref[pl.ds(misc, 1), :]
            for w in range(3):
                d_row = jnp.where(y_is_high, 24 + w, 15 - w)
                for q in range(3):
                    plane = jnp.where(is_high, 7 + q, 2 - q)
                    de_ref[pl.ds(plane * DPITCH + d_row, 1), :] = c_ref[
                        pl.ds(misc + 4 + 4 * w + q * step, 1), :
                    ]

    columns = []
    for p in range(10):
        at = p * DPITCH + 8
        columns.append(
            de_ref[at - 1 : at + 23, :] + de_ref[at : at + 24, :] + de_ref[at + 1 : at + 25, :]
        )
    for p in range(8):
        flat = columns[p] + columns[p + 1] + columns[p + 2]
        weight = flat + masked_prev(flat) + masked_next(flat)
        inside = weight > 0.0
        rw_ref[p * PITCH : (p + 1) * PITCH, :] = jnp.where(
            inside, 1.0 / jnp.where(inside, weight, 1.0), 0.0
        )

    copies = []
    for first in range(NMET, -1, -GROUP):
        group = [first] if first == NMET else range(first, first + GROUP)
        share_sums(group, se_ref, rw_ref, ys_ref)
        for k in group:
            for p in range(2, 6) if k == NMET else range(1, 7):
                dens = de_ref[(p + 1) * DPITCH + 16 : (p + 1) * DPITCH + 24, :]
                at = (k * 8 + p) * BY
                flat = (
                    ys_ref[at - BY : at, :] + ys_ref[at : at + BY, :] + ys_ref[at + BY : at + 2 * BY, :]
                )
                collected = flat + masked_prev(flat) + masked_next(flat)
                deposit = dens * collected
                if k == NMET:
                    cell = (p - 2) * BY
                    energy_out_ref[cell : cell + BY, :] = energy_ref[cell : cell + BY, :] + deposit
                    continue
                if p == 1:
                    metal = mx_ref[0, k * BY : k * BY + BY, :]
                elif p == 6:
                    metal = mx_ref[1, k * BY : k * BY + BY, :]
                else:
                    cell = (k * BX + p - 2) * BY
                    metal = metals_ref[cell : cell + BY, :]
                e_at = (k * 8 + p) * PITCH + 8
                ee_ref[e_at : e_at + BY, :] = metal + deposit
        if first == NMET:
            copies.append(pltpu.make_async_copy(energy_out_ref, energy_out_hbm, sems.at[0]))
            copies[-1].start()
            continue

        for side in range(2):
            row = (7, 16)[side]
            dens = de_ref[rows(DPITCH + row + 8, 8, DPITCH), :]
            inv = [rw_ref[rows(row - 1 + d, 8, PITCH), :] for d in range(3)]
            for k in group:
                value = None
                for d in range(3):
                    term = se_ref[rows(k * 8 * PITCH + row - 1 + d, 8, PITCH), :] * inv[d]
                    value = term if value is None else value + term
                flat = value + pltpu.roll(value, 1, 0) + pltpu.roll(value, 7, 0)
                deposit = dens * (flat + masked_prev(flat) + masked_next(flat))
                ee_ref[rows(k * 8 * PITCH + row, 8, PITCH), :] = (
                    my_ref[side, k * 8 : k * 8 + 8, :] + deposit
                )

        for x in range(BX):
            at = x * BY
            cx_up = cx_ref[at : at + BY, :]
            cx_low = cxl_ref[0] if x == 0 else cx_ref[at - BY : at, :]
            cy_up = cy_ref[at : at + BY, :]
            cy_low = cye_ref[x * PITCH + 7 : x * PITCH + 15, :]
            cz_up = cz_ref[at : at + BY, :]
            cz_low = masked_prev(cz_up)
            to_next = [-jnp.minimum(c, 0.0) for c in (cx_up, cy_up, cz_up)]
            from_prev = [jnp.maximum(c, 0.0) for c in (cx_low, cy_low, cz_low)]
            middle = 1.0
            for up, low in ((cx_up, cx_low), (cy_up, cy_low), (cz_up, cz_low)):
                middle = middle - jnp.maximum(up, 0.0) + jnp.minimum(low, 0.0)
            to_next[2] = jnp.where(not_last, to_next[2], 0.0)
            for k in group:
                e_at = (k * 8 + x + 2) * PITCH + 8
                own = ee_ref[e_at : e_at + BY, :]
                result = middle * own
                result = result + to_next[0] * ee_ref[e_at + PITCH : e_at + PITCH + BY, :]
                result = result + from_prev[0] * ee_ref[e_at - PITCH : e_at - PITCH + BY, :]
                result = result + to_next[1] * ee_ref[e_at + 1 : e_at + 1 + BY, :]
                result = result + from_prev[1] * ee_ref[e_at - 1 : e_at - 1 + BY, :]
                result = result + to_next[2] * next_z(own)
                result = result + from_prev[2] * prev_z(own)
                cell = (k * BX + x) * BY
                out_ref[cell : cell + BY, :] = result
        piece = pl.ds(first * BX * BY, GROUP * BX * BY)
        copies.append(
            pltpu.make_async_copy(out_ref.at[piece], out_hbm.at[piece], sems.at[len(copies)])
        )
        copies[-1].start()
    for copy in copies:
        copy.wait()


def share_sums(group, se_ref, rw_ref, ys_ref):
    for p in range(8):
        inv = [rw_ref[p * PITCH + 7 + d : p * PITCH + 15 + d, :] for d in range(3)]
        for k in group:
            if k == NMET and p in (0, 7):
                continue
            at = (k * 8 + p) * PITCH + 7
            value = None
            for d in range(3):
                term = se_ref[at + d : at + d + BY, :] * inv[d]
                value = term if value is None else value + term
            ys_ref[(k * 8 + p) * BY : (k * 8 + p) * BY + BY, :] = value


def swaps(axis):
    count = lax.axis_size(axis)
    rounds = []
    for first in (0, 1):
        partner = list(range(count))
        for i in range(first, count - 1, 2):
            partner[i], partner[i + 1] = i + 1, i
        rounds.append(list(enumerate(partner)))
    return rounds


VM = pl.BlockSpec(memory_space=pltpu.VMEM)
HB = pl.BlockSpec(memory_space=pltpu.HBM)


def buffer(count):
    return pltpu.VMEM((count, NZ), F32)


def body(masses, table, star_mask, density, metals, energy, courant_x, courant_y, courant_z):
    cells = BX * BY
    masses = masses.reshape(BINS, cells, NZ)
    star_mask, density, energy, courant_x, courant_y, courant_z = (
        a.reshape(cells, NZ) for a in (star_mask, density, energy, courant_x, courant_y, courant_z)
    )
    metals = metals.reshape(NMET * cells, NZ)
    src, ya, yb, xa, xb, *local = pl.pallas_call(
        sources_kernel,
        name="sources",
        out_shape=[buffer(COMP * cells), buffer(YROWS), buffer(YROWS), buffer(XROWS), buffer(XROWS)]
        + [buffer(cells), buffer(NMET * cells)] + [buffer(cells)] * 4,
        in_specs=[HB] * 9,
        out_specs=[VM] * 11,
        scratch_shapes=[
            pltpu.VMEM((BINS, cells, NZ), BF16),
            pltpu.VMEM((BINS, COMP), BF16),
            pltpu.VMEM((cells, NZ), jnp.int32),
            pltpu.VMEM((COMP * 16, BINS * 16), BF16),
            pltpu.VMEM((24, BINS * 16), F32),
            pltpu.SemaphoreType.DMA((CHUNKS,)),
            pltpu.SemaphoreType.DMA((8,)),
        ],
        compiler_params=pltpu.CompilerParams(vmem_limit_bytes=32 * 1024 * 1024),
    )(masses, table, star_mask, density, metals, energy, courant_x, courant_y, courant_z)
    pairs_y = swaps("gy")
    pairs_x = swaps("gx")
    ya = lax.ppermute(ya, "gy", pairs_y[0])
    yb = lax.ppermute(yb, "gy", pairs_y[1])
    xa = lax.ppermute(xa, "gx", pairs_x[0])
    xb = lax.ppermute(xb, "gx", pairs_x[1])
    ca, cb = pl.pallas_call(
        corner_kernel,
        name="corners",
        out_shape=[buffer(CROWS), buffer(CROWS)],
        in_specs=[VM, VM],
        out_specs=[VM, VM],
    )(ya, yb)
    ca = lax.ppermute(ca, "gx", pairs_x[0])
    cb = lax.ppermute(cb, "gx", pairs_x[1])
    advected, energy_out = pl.pallas_call(
        finish_kernel,
        name="finish",
        out_shape=[
            jax.ShapeDtypeStruct((NMET * cells, NZ), F32),
            jax.ShapeDtypeStruct((cells, NZ), F32),
        ],
        in_specs=[VM] * 13,
        out_specs=[HB, HB],
        scratch_shapes=[
            pltpu.VMEM((NMET * cells, NZ), F32),
            pltpu.VMEM((cells, NZ), F32),
            pltpu.SemaphoreType.DMA((1 + NMET // GROUP,)),
            pltpu.VMEM((COMP * 8 * PITCH, NZ), F32),
            pltpu.VMEM((10 * DPITCH, NZ), F32),
            pltpu.VMEM((8 * PITCH, NZ), F32),
            pltpu.VMEM((COMP * 8 * BY, NZ), F32),
            pltpu.VMEM((NMET * 8 * PITCH, NZ), F32),
            pltpu.VMEM((2, NMET * BY, NZ), F32),
            pltpu.VMEM((2, NMET * 8, NZ), F32),
            pltpu.VMEM((2, BY, NZ), F32),
            pltpu.VMEM((BX * PITCH, NZ), F32),
        ],
        compiler_params=pltpu.CompilerParams(vmem_limit_bytes=32 * 1024 * 1024),
    )(src, ya, yb, xa, xb, ca, cb, *local)
    return advected.reshape(NMET, BX, BY, NZ), energy_out.reshape(BX, BY, NZ)


def solution(mesh):
    field = P("gx", "gy", None)
    stack = P(None, "gx", "gy", None)
    in_specs = (stack, P(), field, field, stack, field, field, field, field)
    out_specs = (stack, field)
    return jax.shard_map(body, mesh=mesh, in_specs=in_specs, out_specs=out_specs, check_vma=False)
```

```python
import jax
import jax.numpy as jnp
from jax import lax
from jax.experimental import pallas as pl
from jax.experimental.pallas import tpu as pltpu
from jax.sharding import PartitionSpec as P

F32 = jnp.float32
BF16 = jnp.bfloat16
BINS = 256
COMP = 17
NMET = 16
BX = 4
BY = 8
NZ = 128
CHUNKS = 4
GROUP = 4
YROWS = 216
XROWS = 424
CROWS = 128
PITCH = 24
DPITCH = 40


def rows(start, count, stride=1):
    return pl.ds(start, count) if stride == 1 else pl.ds(start, count, stride)


def place(axis):
    index = lax.axis_index(axis)
    last = index == lax.axis_size(axis) - 1
    odd = index % 2
    alone_a = jnp.logical_and(odd == 0, last)
    alone_b = jnp.logical_or(index == 0, jnp.logical_and(odd == 1, last))
    return 1 - odd, alone_a, alone_b


def sources_kernel(
    masses_hbm, table_hbm, star_hbm, dens_hbm, metals_hbm, energy_hbm, cx_hbm, cy_hbm, cz_hbm,
    src_ref, ya_ref, yb_ref, xa_ref, xb_ref,
    dens_ref, metals_ref, energy_ref, cx_ref, cy_ref, cz_ref,
    mass_buf, table_ref, star_ref, expand_ref, wide_ref, mass_sems, sems,
):
    small = [
        (table_hbm, table_ref), (star_hbm, star_ref), (dens_hbm, dens_ref), (metals_hbm, metals_ref),
        (cx_hbm, cx_ref), (cy_hbm, cy_ref), (cz_hbm, cz_ref), (energy_hbm, energy_ref),
    ]
    small_copies = [
        pltpu.make_async_copy(hbm, ref, sems.at[i]) for i, (hbm, ref) in enumerate(small)
    ]
    per = BINS // CHUNKS
    copies = [
        pltpu.make_async_copy(
            masses_hbm.at[pl.ds(c * per, per)], mass_buf.at[pl.ds(c * per, per)], mass_sems.at[c]
        )
        for c in range(CHUNKS)
    ]
    small_copies[0].start()
    for copy in copies:
        copy.start()
    for copy in small_copies[1:]:
        copy.start()

    width = BINS * 16
    group = lax.broadcasted_iota(jnp.int32, (8, NZ), 1) // 16
    same = (
        lax.broadcasted_iota(jnp.int32, (16, NZ), 1) % 16
        == lax.broadcasted_iota(jnp.int32, (16, NZ), 0)
    )
    small_copies[0].wait()
    turned = table_ref[...].astype(F32)
    turned = jnp.concatenate([turned, jnp.zeros((24 - COMP, BINS), F32)], axis=0)
    for t in range(width // NZ):
        first = 8 * t
        half = first // NZ
        for r in range(3):
            tile = turned[8 * r : 8 * r + 8, half * NZ : (half + 1) * NZ]
            wide_ref[8 * r : 8 * r + 8, t * NZ : (t + 1) * NZ] = jnp.take_along_axis(
                tile, group + first % NZ, axis=1
            )
    for t in range(width // NZ):
        for k in range(COMP):
            line = jnp.broadcast_to(wide_ref[k : k + 1, t * NZ : (t + 1) * NZ], (16, NZ))
            expand_ref[k * 16 : k * 16 + 16, t * NZ : (t + 1) * NZ] = jnp.where(
                same, line, 0.0
            ).astype(BF16)

    total = None
    for c in range(CHUNKS):
        copies[c].wait()
        part = mass_buf[c * per : (c + 1) * per]
        right = jnp.concatenate(
            [part[:, 16 * j : 16 * j + 16].reshape(per * 16, NZ) for j in range(2)], axis=1
        )
        left = expand_ref[:, c * per * 16 : (c + 1) * per * 16]
        prod = jnp.dot(left, right, preferred_element_type=F32)
        total = prod if total is None else total + prod
    for copy in small_copies[1:]:
        copy.wait()
    for j in range(2):
        for s in range(2):
            x = 2 * j + s
            mask = star_ref[x * BY : x * BY + BY, :].astype(F32)
            for k in range(COMP):
                at = (k * BX + x) * BY
                piece = total[k * 16 + s * BY : k * 16 + s * BY + BY, j * NZ : (j + 1) * NZ]
                src_ref[at : at + BY, :] = piece * mask

    even_x, alone_xa, alone_xb = place("gx")
    even_y, alone_ya, alone_yb = place("gy")
    for out, high in ((ya_ref, even_y), (yb_ref, 1 - even_y)):
        near = jnp.where(high == 1, BY - 1, 0)
        step = jnp.where(high == 1, -1, 1)
        out[0:64, :] = src_ref[rows(near, 64, BY), :]
        out[64:128, :] = src_ref[rows(near + step, 64, BY), :]
        out[128:192, :] = metals_ref[rows(near, 64, BY), :]
        out[192:196, :] = src_ref[rows(NMET * BX * BY + near, 4, BY), :]
        out[196:200, :] = dens_ref[rows(near, 4, BY), :]
        out[200:204, :] = dens_ref[rows(near + step, 4, BY), :]
        out[204:208, :] = dens_ref[rows(near + 2 * step, 4, BY), :]
        out[208:212, :] = cy_ref[rows(near, 4, BY), :]
        out[212:216, :] = jnp.zeros((4, NZ), F32)
    for out, high in ((xa_ref, even_x), (xb_ref, 1 - even_x)):
        near = jnp.where(high == 1, BX - 1, 0) * BY
        step = jnp.where(high == 1, -1, 1) * BY
        tile = 0
        pieces = [(src_ref, k * BX * BY + near) for k in range(COMP)]
        pieces += [(src_ref, k * BX * BY + near + step) for k in range(NMET)]
        pieces += [(metals_ref, k * BX * BY + near) for k in range(NMET)]
        pieces += [(dens_ref, near), (dens_ref, near + step), (dens_ref, near + 2 * step)]
        pieces += [(cx_ref, near)]
        for ref, at in pieces:
            out[tile * BY : tile * BY + BY, :] = ref[pl.ds(pl.multiple_of(at, BY), BY), :]
            tile += 1
    for out, alone in ((ya_ref, alone_ya), (yb_ref, alone_yb), (xa_ref, alone_xa), (xb_ref, alone_xb)):
        clear(out, alone)


def clear(ref, alone):
    @pl.when(alone)
    def _():
        ref[...] = jnp.zeros(ref.shape, F32)


def corner_kernel(ya_ref, yb_ref, ca_ref, cb_ref):
    even_x, alone_a, alone_b = place("gx")
    for out, high in ((ca_ref, even_x), (cb_ref, 1 - even_x)):
        near = jnp.where(high == 1, BX - 1, 0)
        step = jnp.where(high == 1, -1, 1)
        for side, y_ref in enumerate((ya_ref, yb_ref)):
            base = side * 64
            out[base : base + 16, :] = y_ref[rows(near, 16, BX), :]
            out[base + 16 : base + 32, :] = y_ref[rows(near + step, 16, BX), :]
            out[base + 32 : base + 48, :] = y_ref[rows(64 + near, 16, BX), :]
            out[base + 48 : base + 64, :] = y_ref[192:208, :]
    clear(ca_ref, alone_a)
    clear(cb_ref, alone_b)


def finish_kernel(
    src_ref, ya_ref, yb_ref, xa_ref, xb_ref, ca_ref, cb_ref,
    dens_ref, metals_ref, energy_ref, cx_ref, cy_ref, cz_ref,
    out_hbm, energy_out_hbm,
    out_ref, energy_out_ref, sems,
    se_ref, de_ref, rw_ref, ys_ref, ee_ref, mx_ref, my_ref, cxl_ref, cye_ref,
):
    even_x = place("gx")[0]
    even_y = place("gy")[0]
    lane = lax.broadcasted_iota(jnp.int32, (1, NZ), 1)
    not_first = lane > 0
    not_last = lane < NZ - 1

    def prev_z(v):
        return pltpu.roll(v, 1, 1)

    def next_z(v):
        return pltpu.roll(v, NZ - 1, 1)

    def masked_prev(v):
        return jnp.where(not_first, prev_z(v), 0.0)

    def masked_next(v):
        return jnp.where(not_last, next_z(v), 0.0)

    de_ref[...] = jnp.zeros(de_ref.shape, F32)

    for x in range(BX):
        at = x * BY
        d_at = (x + 3) * DPITCH + 16
        de_ref[d_at : d_at + BY, :] = dens_ref[at : at + BY, :]
        cye_ref[x * PITCH + 8 : x * PITCH + 16, :] = cy_ref[at : at + BY, :]
        for k in range(COMP):
            s_at = (k * 8 + x + 2) * PITCH + 8
            se_ref[s_at : s_at + BY, :] = src_ref[(k * BX + x) * BY : (k * BX + x + 1) * BY, :]

    for y_ref, high in ((ya_ref, even_y), (yb_ref, 1 - even_y)):
        is_high = high == 1
        r1 = jnp.where(is_high, 16, 7)
        r2 = jnp.where(is_high, 17, 6)
        for k in range(NMET):
            at = k * BX
            base = (k * 8 + 2) * PITCH
            se_ref[rows(base + r1, BX, PITCH), :] = y_ref[at : at + BX, :]
            se_ref[rows(base + r2, BX, PITCH), :] = y_ref[64 + at : 64 + at + BX, :]
            my_ref[high, k * 8 + 2 : k * 8 + 2 + BX, :] = y_ref[128 + at : 128 + at + BX, :]
        base = (NMET * 8 + 2) * PITCH
        se_ref[rows(base + r1, BX, PITCH), :] = y_ref[192:196, :]
        for w in range(3):
            d_row = jnp.where(is_high, 24 + w, 15 - w)
            de_ref[rows(3 * DPITCH + d_row, BX, DPITCH), :] = y_ref[196 + 4 * w : 200 + 4 * w, :]
        cye_ref[rows(jnp.where(is_high, 16, 7), BX, PITCH), :] = y_ref[208:212, :]

    for x_ref, c_ref, high in ((xa_ref, ca_ref, even_x), (xb_ref, cb_ref, 1 - even_x)):
        is_high = high == 1
        p1 = jnp.where(is_high, 6, 1)
        p2 = jnp.where(is_high, 7, 0)
        for k in range(COMP):
            at = pl.multiple_of((k * 8 + p1) * PITCH + 8, 8)
            se_ref[pl.ds(at, BY), :] = x_ref[k * BY : k * BY + BY, :]
        for k in range(NMET):
            at = pl.multiple_of((k * 8 + p2) * PITCH + 8, 8)
            tile = COMP + k
            se_ref[pl.ds(at, BY), :] = x_ref[tile * BY : tile * BY + BY, :]
            tile = COMP + NMET + k
            mx_ref[high, k * BY : k * BY + BY, :] = x_ref[tile * BY : tile * BY + BY, :]
        for w in range(3):
            tile = COMP + 2 * NMET + w
            plane = jnp.where(is_high, 7 + w, 2 - w)
            at = pl.multiple_of(plane * DPITCH + 16, 8)
            de_ref[pl.ds(at, BY), :] = x_ref[tile * BY : tile * BY + BY, :]
        tile = COMP + 2 * NMET + 3
        cxl_ref[high] = x_ref[tile * BY : tile * BY + BY, :]
        for side, y_high in ((0, even_y), (1, 1 - even_y)):
            y_is_high = y_high == 1
            base = side * 64
            r1 = jnp.where(y_is_high, 16, 7)
            r2 = jnp.where(y_is_high, 17, 6)
            se_ref[rows(p1 * PITCH + r1, NMET, 8 * PITCH), :] = c_ref[base : base + 16, :]
            se_ref[rows(p2 * PITCH + r1, NMET, 8 * PITCH), :] = c_ref[base + 16 : base + 32, :]
            se_ref[rows(p1 * PITCH + r2, NMET, 8 * PITCH), :] = c_ref[base + 32 : base + 48, :]
            from_plane = jnp.where(is_high, 0, BX - 1)
            step = jnp.where(is_high, 1, -1)
            misc = base + 48 + from_plane
            se_ref[pl.ds((NMET * 8 + p1) * PITCH + r1, 1), :] = c_ref[pl.ds(misc, 1), :]
            for w in range(3):
                d_row = jnp.where(y_is_high, 24 + w, 15 - w)
                for q in range(3):
                    plane = jnp.where(is_high, 7 + q, 2 - q)
                    de_ref[pl.ds(plane * DPITCH + d_row, 1), :] = c_ref[
                        pl.ds(misc + 4 + 4 * w + q * step, 1), :
                    ]

    columns = []
    for p in range(10):
        at = p * DPITCH + 8
        columns.append(
            de_ref[at - 1 : at + 23, :] + de_ref[at : at + 24, :] + de_ref[at + 1 : at + 25, :]
        )
    for p in range(8):
        flat = columns[p] + columns[p + 1] + columns[p + 2]
        weight = flat + masked_prev(flat) + masked_next(flat)
        inside = weight > 0.0
        rw_ref[p * PITCH : (p + 1) * PITCH, :] = jnp.where(
            inside, 1.0 / jnp.where(inside, weight, 1.0), 0.0
        )

    copies = []
    for first in range(NMET, -1, -GROUP):
        group = [first] if first == NMET else range(first, first + GROUP)
        share_sums(group, se_ref, rw_ref, ys_ref)
        for k in group:
            for p in range(2, 6) if k == NMET else range(1, 7):
                dens = de_ref[(p + 1) * DPITCH + 16 : (p + 1) * DPITCH + 24, :]
                at = (k * 8 + p) * BY
                flat = (
                    ys_ref[at - BY : at, :] + ys_ref[at : at + BY, :] + ys_ref[at + BY : at + 2 * BY, :]
                )
                collected = flat + masked_prev(flat) + masked_next(flat)
                deposit = dens * collected
                if k == NMET:
                    cell = (p - 2) * BY
                    energy_out_ref[cell : cell + BY, :] = energy_ref[cell : cell + BY, :] + deposit
                    continue
                if p == 1:
                    metal = mx_ref[0, k * BY : k * BY + BY, :]
                elif p == 6:
                    metal = mx_ref[1, k * BY : k * BY + BY, :]
                else:
                    cell = (k * BX + p - 2) * BY
                    metal = metals_ref[cell : cell + BY, :]
                e_at = (k * 8 + p) * PITCH + 8
                ee_ref[e_at : e_at + BY, :] = metal + deposit
        if first == NMET:
            copies.append(pltpu.make_async_copy(energy_out_ref, energy_out_hbm, sems.at[0]))
            copies[-1].start()
            continue

        for side in range(2):
            row = (7, 16)[side]
            dens = de_ref[rows(DPITCH + row + 8, 8, DPITCH), :]
            inv = [rw_ref[rows(row - 1 + d, 8, PITCH), :] for d in range(3)]
            for k in group:
                value = None
                for d in range(3):
                    term = se_ref[rows(k * 8 * PITCH + row - 1 + d, 8, PITCH), :] * inv[d]
                    value = term if value is None else value + term
                flat = value + pltpu.roll(value, 1, 0) + pltpu.roll(value, 7, 0)
                deposit = dens * (flat + masked_prev(flat) + masked_next(flat))
                ee_ref[rows(k * 8 * PITCH + row, 8, PITCH), :] = (
                    my_ref[side, k * 8 : k * 8 + 8, :] + deposit
                )

        for x in range(BX):
            at = x * BY
            cx_up = cx_ref[at : at + BY, :]
            cx_low = cxl_ref[0] if x == 0 else cx_ref[at - BY : at, :]
            cy_up = cy_ref[at : at + BY, :]
            cy_low = cye_ref[x * PITCH + 7 : x * PITCH + 15, :]
            cz_up = cz_ref[at : at + BY, :]
            cz_low = masked_prev(cz_up)
            to_next = [-jnp.minimum(c, 0.0) for c in (cx_up, cy_up, cz_up)]
            from_prev = [jnp.maximum(c, 0.0) for c in (cx_low, cy_low, cz_low)]
            middle = 1.0
            for up, low in ((cx_up, cx_low), (cy_up, cy_low), (cz_up, cz_low)):
                middle = middle - jnp.maximum(up, 0.0) + jnp.minimum(low, 0.0)
            to_next[2] = jnp.where(not_last, to_next[2], 0.0)
            for k in group:
                e_at = (k * 8 + x + 2) * PITCH + 8
                own = ee_ref[e_at : e_at + BY, :]
                result = middle * own
                result = result + to_next[0] * ee_ref[e_at + PITCH : e_at + PITCH + BY, :]
                result = result + from_prev[0] * ee_ref[e_at - PITCH : e_at - PITCH + BY, :]
                result = result + to_next[1] * ee_ref[e_at + 1 : e_at + 1 + BY, :]
                result = result + from_prev[1] * ee_ref[e_at - 1 : e_at - 1 + BY, :]
                result = result + to_next[2] * next_z(own)
                result = result + from_prev[2] * prev_z(own)
                cell = (k * BX + x) * BY
                out_ref[cell : cell + BY, :] = result
        piece = pl.ds(first * BX * BY, GROUP * BX * BY)
        copies.append(
            pltpu.make_async_copy(out_ref.at[piece], out_hbm.at[piece], sems.at[len(copies)])
        )
        copies[-1].start()
    for copy in copies:
        copy.wait()


def share_sums(group, se_ref, rw_ref, ys_ref):
    for p in range(8):
        inv = [rw_ref[p * PITCH + 7 + d : p * PITCH + 15 + d, :] for d in range(3)]
        for k in group:
            if k == NMET and p in (0, 7):
                continue
            at = (k * 8 + p) * PITCH + 7
            value = None
            for d in range(3):
                term = se_ref[at + d : at + d + BY, :] * inv[d]
                value = term if value is None else value + term
            ys_ref[(k * 8 + p) * BY : (k * 8 + p) * BY + BY, :] = value


def swaps():
    nx = lax.axis_size("gx")
    ny = lax.axis_size("gy")
    rounds = []
    for along_x in (True, False):
        for first in (0, 1):
            pairs = []
            for x in range(nx):
                for y in range(ny):
                    place_, count = (x, nx) if along_x else (y, ny)
                    mate = place_ + 1 if place_ % 2 == first else place_ - 1
                    if 0 <= mate < count:
                        to = (mate, y) if along_x else (x, mate)
                    elif along_x and ny % 2 == 0:
                        to = (x, (y + ny // 2) % ny)
                    elif not along_x and nx % 2 == 0:
                        to = (x + 1 - 2 * (x % 2), y)
                    else:
                        to = (x, y)
                    pairs.append((x * ny + y, to[0] * ny + to[1]))
            rounds.append(pairs)
    return rounds


def swap(value, pairs):
    return lax.ppermute(value, ("gx", "gy"), pairs)


VM = pl.BlockSpec(memory_space=pltpu.VMEM)
HB = pl.BlockSpec(memory_space=pltpu.HBM)


def buffer(count):
    return pltpu.VMEM((count, NZ), F32)


def body(masses, table, star_mask, density, metals, energy, courant_x, courant_y, courant_z):
    cells = BX * BY
    masses = masses.reshape(BINS, cells, NZ)
    star_mask, density, energy, courant_x, courant_y, courant_z = (
        a.reshape(cells, NZ) for a in (star_mask, density, energy, courant_x, courant_y, courant_z)
    )
    metals = metals.reshape(NMET * cells, NZ)
    src, ya, yb, xa, xb, *local = pl.pallas_call(
        sources_kernel,
        name="sources",
        out_shape=[buffer(COMP * cells), buffer(YROWS), buffer(YROWS), buffer(XROWS), buffer(XROWS)]
        + [buffer(cells), buffer(NMET * cells)] + [buffer(cells)] * 4,
        in_specs=[HB] * 9,
        out_specs=[VM] * 11,
        scratch_shapes=[
            pltpu.VMEM((BINS, cells, NZ), BF16),
            pltpu.VMEM((COMP, BINS), BF16),
            pltpu.VMEM((cells, NZ), jnp.int32),
            pltpu.VMEM((COMP * 16, BINS * 16), BF16),
            pltpu.VMEM((24, BINS * 16), F32),
            pltpu.SemaphoreType.DMA((CHUNKS,)),
            pltpu.SemaphoreType.DMA((8,)),
        ],
        compiler_params=pltpu.CompilerParams(vmem_limit_bytes=32 * 1024 * 1024),
    )(
        *(
            pltpu.with_memory_space_constraint(a, pltpu.HBM)
            for a in (
                masses, table.T, star_mask, density, metals, energy, courant_x, courant_y, courant_z
            )
        )
    )
    pairs_xa, pairs_xb, pairs_ya, pairs_yb = swaps()
    ya = swap(ya, pairs_ya)
    yb = swap(yb, pairs_yb)
    xa = swap(xa, pairs_xa)
    xb = swap(xb, pairs_xb)
    ca, cb = pl.pallas_call(
        corner_kernel,
        name="corners",
        out_shape=[buffer(CROWS), buffer(CROWS)],
        in_specs=[VM, VM],
        out_specs=[VM, VM],
        compiler_params=pltpu.CompilerParams(vmem_limit_bytes=4 * 1024 * 1024),
    )(*(pltpu.with_memory_space_constraint(a, pltpu.VMEM) for a in (ya, yb)))
    ca = swap(ca, pairs_xa)
    cb = swap(cb, pairs_xb)
    advected, energy_out = pl.pallas_call(
        finish_kernel,
        name="finish",
        out_shape=[
            jax.ShapeDtypeStruct((NMET * cells, NZ), F32),
            jax.ShapeDtypeStruct((cells, NZ), F32),
        ],
        in_specs=[VM] * 13,
        out_specs=[HB, HB],
        scratch_shapes=[
            pltpu.VMEM((NMET * cells, NZ), F32),
            pltpu.VMEM((cells, NZ), F32),
            pltpu.SemaphoreType.DMA((1 + NMET // GROUP,)),
            pltpu.VMEM((COMP * 8 * PITCH, NZ), F32),
            pltpu.VMEM((10 * DPITCH, NZ), F32),
            pltpu.VMEM((8 * PITCH, NZ), F32),
            pltpu.VMEM((COMP * 8 * BY, NZ), F32),
            pltpu.VMEM((NMET * 8 * PITCH, NZ), F32),
            pltpu.VMEM((2, NMET * BY, NZ), F32),
            pltpu.VMEM((2, NMET * 8, NZ), F32),
            pltpu.VMEM((2, BY, NZ), F32),
            pltpu.VMEM((BX * PITCH, NZ), F32),
        ],
        compiler_params=pltpu.CompilerParams(vmem_limit_bytes=32 * 1024 * 1024),
    )(
        *(
            pltpu.with_memory_space_constraint(a, pltpu.VMEM)
            for a in (src, ya, yb, xa, xb, ca, cb, *local)
        )
    )
    return advected.reshape(NMET, BX, BY, NZ), energy_out.reshape(BX, BY, NZ)


def solution(mesh):
    field = P("gx", "gy", None)
    stack = P(None, "gx", "gy", None)
    in_specs = (stack, P(), field, field, stack, field, field, field, field)
    out_specs = (stack, field)
    return jax.shard_map(body, mesh=mesh, in_specs=in_specs, out_specs=out_specs, check_vma=False)
```

```python
import jax
import jax.numpy as jnp
from jax import lax
from jax.experimental import pallas as pl
from jax.experimental.pallas import tpu as pltpu
from jax.sharding import PartitionSpec as P

F32 = jnp.float32
BF16 = jnp.bfloat16
BINS = 256
COMP = 17
NMET = 16
BX = 4
BY = 8
NZ = 128
CHUNKS = 4
GROUP = 4
YROWS = 112
ZROWS = 104
XROWS = 424
CROWS = 128
PITCH = 24
DPITCH = 40


def rows(start, count, stride=1):
    return pl.ds(start, count) if stride == 1 else pl.ds(start, count, stride)


def place(axis):
    index = lax.axis_index(axis)
    last = index == lax.axis_size(axis) - 1
    odd = index % 2
    alone_a = jnp.logical_and(odd == 0, last)
    alone_b = jnp.logical_or(index == 0, jnp.logical_and(odd == 1, last))
    return 1 - odd, alone_a, alone_b


def sources_kernel(
    masses_hbm, table_hbm, star_hbm, dens_hbm, metals_hbm, energy_hbm, cx_hbm, cy_hbm, cz_hbm,
    src_ref, ya_ref, yb_ref, xa_ref, xb_ref, za_ref, zb_ref,
    dens_ref, metals_ref, energy_ref, cx_ref, cy_ref, cz_ref,
    mass_buf, table_ref, star_ref, expand_ref, wide_ref, mass_sems, sems,
):
    small = [
        (table_hbm, table_ref), (star_hbm, star_ref), (dens_hbm, dens_ref), (metals_hbm, metals_ref),
        (cx_hbm, cx_ref), (cy_hbm, cy_ref), (cz_hbm, cz_ref), (energy_hbm, energy_ref),
    ]
    small_copies = [
        pltpu.make_async_copy(hbm, ref, sems.at[i]) for i, (hbm, ref) in enumerate(small)
    ]
    per = BINS // CHUNKS
    copies = [
        pltpu.make_async_copy(
            masses_hbm.at[pl.ds(c * per, per)], mass_buf.at[pl.ds(c * per, per)], mass_sems.at[c]
        )
        for c in range(CHUNKS)
    ]
    small_copies[0].start()
    for copy in copies:
        copy.start()
    for copy in small_copies[1:]:
        copy.start()

    width = BINS * 16
    group = lax.broadcasted_iota(jnp.int32, (8, NZ), 1) // 16
    same = (
        lax.broadcasted_iota(jnp.int32, (16, NZ), 1) % 16
        == lax.broadcasted_iota(jnp.int32, (16, NZ), 0)
    )
    small_copies[0].wait()
    turned = table_ref[...].astype(F32)
    turned = jnp.concatenate([turned, jnp.zeros((24 - COMP, BINS), F32)], axis=0)
    for t in range(width // NZ):
        first = 8 * t
        half = first // NZ
        for r in range(3):
            tile = turned[8 * r : 8 * r + 8, half * NZ : (half + 1) * NZ]
            wide_ref[8 * r : 8 * r + 8, t * NZ : (t + 1) * NZ] = jnp.take_along_axis(
                tile, group + first % NZ, axis=1
            )
    for t in range(width // NZ):
        for k in range(COMP):
            line = jnp.broadcast_to(wide_ref[k : k + 1, t * NZ : (t + 1) * NZ], (16, NZ))
            expand_ref[k * 16 : k * 16 + 16, t * NZ : (t + 1) * NZ] = jnp.where(
                same, line, 0.0
            ).astype(BF16)

    total = None
    for c in range(CHUNKS):
        copies[c].wait()
        part = mass_buf[c * per : (c + 1) * per]
        right = jnp.concatenate(
            [part[:, 16 * j : 16 * j + 16].reshape(per * 16, NZ) for j in range(2)], axis=1
        )
        left = expand_ref[:, c * per * 16 : (c + 1) * per * 16]
        prod = jnp.dot(left, right, preferred_element_type=F32)
        total = prod if total is None else total + prod
    for copy in small_copies[1:]:
        copy.wait()
    for j in range(2):
        for s in range(2):
            x = 2 * j + s
            mask = star_ref[x * BY : x * BY + BY, :].astype(F32)
            for k in range(COMP):
                at = (k * BX + x) * BY
                piece = total[k * 16 + s * BY : k * 16 + s * BY + BY, j * NZ : (j + 1) * NZ]
                src_ref[at : at + BY, :] = piece * mask

    even_x, alone_xa, alone_xb = place("gx")
    even_y, alone_ya, alone_yb = place("gy")
    plane = BX * BY
    for out, rest, high in ((ya_ref, za_ref, even_y), (yb_ref, zb_ref, 1 - even_y)):
        near = jnp.where(high == 1, BY - 1, 0)
        step = jnp.where(high == 1, -1, 1)
        out[0:64, :] = src_ref[rows(near, 64, BY), :]
        for i, x in enumerate((0, BX - 1)):
            out[64 + 16 * i : 80 + 16 * i, :] = src_ref[rows(x * BY + near + step, 16, plane), :]
        out[96:100, :] = src_ref[rows(NMET * plane + near, 4, BY), :]
        out[100:104, :] = dens_ref[rows(near, 4, BY), :]
        out[104:108, :] = dens_ref[rows(near + step, 4, BY), :]
        out[108:112, :] = dens_ref[rows(near + 2 * step, 4, BY), :]
        rest[0:64, :] = metals_ref[rows(near, 64, BY), :]
        for x in range(1, BX - 1):
            at = 64 + 16 * (x - 1)
            rest[at : at + 16, :] = src_ref[rows(x * BY + near + step, 16, plane), :]
        rest[96:100, :] = cy_ref[rows(near, 4, BY), :]
        rest[100:104, :] = jnp.zeros((4, NZ), F32)
    for out, high in ((xa_ref, even_x), (xb_ref, 1 - even_x)):
        near = jnp.where(high == 1, BX - 1, 0) * BY
        step = jnp.where(high == 1, -1, 1) * BY
        tile = 0
        pieces = [(src_ref, k * BX * BY + near) for k in range(COMP)]
        pieces += [(src_ref, k * BX * BY + near + step) for k in range(NMET)]
        pieces += [(metals_ref, k * BX * BY + near) for k in range(NMET)]
        pieces += [(dens_ref, near), (dens_ref, near + step), (dens_ref, near + 2 * step)]
        pieces += [(cx_ref, near)]
        for ref, at in pieces:
            out[tile * BY : tile * BY + BY, :] = ref[pl.ds(pl.multiple_of(at, BY), BY), :]
            tile += 1
    for out, alone in (
        (ya_ref, alone_ya), (yb_ref, alone_yb), (za_ref, alone_ya), (zb_ref, alone_yb),
        (xa_ref, alone_xa), (xb_ref, alone_xb),
    ):
        clear(out, alone)


def clear(ref, alone):
    @pl.when(alone)
    def _():
        ref[...] = jnp.zeros(ref.shape, F32)


def corner_kernel(ya_ref, yb_ref, xa_ref, xb_ref, ca_ref, cb_ref):
    del xa_ref, xb_ref
    even_x, alone_a, alone_b = place("gx")
    for out, high in ((ca_ref, even_x), (cb_ref, 1 - even_x)):
        near = jnp.where(high == 1, BX - 1, 0)
        step = jnp.where(high == 1, -1, 1)
        for side, y_ref in enumerate((ya_ref, yb_ref)):
            base = side * 64
            out[base : base + 16, :] = y_ref[rows(near, 16, BX), :]
            out[base + 16 : base + 32, :] = y_ref[rows(near + step, 16, BX), :]
            at = pl.multiple_of(jnp.where(high == 1, 80, 64), 16)
            out[base + 32 : base + 48, :] = y_ref[pl.ds(at, 16), :]
            out[base + 48 : base + 64, :] = y_ref[96:112, :]
    clear(ca_ref, alone_a)
    clear(cb_ref, alone_b)


def finish_kernel(
    src_ref, ya_ref, yb_ref, xa_ref, xb_ref, za_ref, zb_ref, ca_ref, cb_ref,
    dens_ref, metals_ref, energy_ref, cx_ref, cy_ref, cz_ref,
    out_hbm, energy_out_hbm,
    out_ref, energy_out_ref, sems,
    se_ref, de_ref, rw_ref, ys_ref, ee_ref, mx_ref, my_ref, cxl_ref, cye_ref,
):
    even_x = place("gx")[0]
    even_y = place("gy")[0]
    lane = lax.broadcasted_iota(jnp.int32, (1, NZ), 1)
    not_first = lane > 0
    not_last = lane < NZ - 1

    def prev_z(v):
        return pltpu.roll(v, 1, 1)

    def next_z(v):
        return pltpu.roll(v, NZ - 1, 1)

    def masked_prev(v):
        return jnp.where(not_first, prev_z(v), 0.0)

    def masked_next(v):
        return jnp.where(not_last, next_z(v), 0.0)

    de_ref[...] = jnp.zeros(de_ref.shape, F32)

    for x in range(BX):
        at = x * BY
        d_at = (x + 3) * DPITCH + 16
        de_ref[d_at : d_at + BY, :] = dens_ref[at : at + BY, :]
        cye_ref[x * PITCH + 8 : x * PITCH + 16, :] = cy_ref[at : at + BY, :]
        for k in range(COMP):
            s_at = (k * 8 + x + 2) * PITCH + 8
            se_ref[s_at : s_at + BY, :] = src_ref[(k * BX + x) * BY : (k * BX + x + 1) * BY, :]

    for y_ref, z_ref, high in ((ya_ref, za_ref, even_y), (yb_ref, zb_ref, 1 - even_y)):
        is_high = high == 1
        r1 = jnp.where(is_high, 16, 7)
        r2 = jnp.where(is_high, 17, 6)
        for k in range(NMET):
            at = k * BX
            base = (k * 8 + 2) * PITCH
            se_ref[rows(base + r1, BX, PITCH), :] = y_ref[at : at + BX, :]
            my_ref[high, k * 8 + 2 : k * 8 + 2 + BX, :] = z_ref[at : at + BX, :]
        for x in range(BX):
            if x in (0, BX - 1):
                value = y_ref[64 + 16 * (x > 0) : 80 + 16 * (x > 0), :]
            else:
                value = z_ref[48 + 16 * x : 64 + 16 * x, :]
            se_ref[rows((x + 2) * PITCH + r2, NMET, 8 * PITCH), :] = value
        base = (NMET * 8 + 2) * PITCH
        se_ref[rows(base + r1, BX, PITCH), :] = y_ref[96:100, :]
        for w in range(3):
            d_row = jnp.where(is_high, 24 + w, 15 - w)
            de_ref[rows(3 * DPITCH + d_row, BX, DPITCH), :] = y_ref[100 + 4 * w : 104 + 4 * w, :]
        cye_ref[rows(jnp.where(is_high, 16, 7), BX, PITCH), :] = z_ref[96:100, :]

    for x_ref, c_ref, high in ((xa_ref, ca_ref, even_x), (xb_ref, cb_ref, 1 - even_x)):
        is_high = high == 1
        p1 = jnp.where(is_high, 6, 1)
        p2 = jnp.where(is_high, 7, 0)
        for k in range(COMP):
            at = pl.multiple_of((k * 8 + p1) * PITCH + 8, 8)
            se_ref[pl.ds(at, BY), :] = x_ref[k * BY : k * BY + BY, :]
        for k in range(NMET):
            at = pl.multiple_of((k * 8 + p2) * PITCH + 8, 8)
            tile = COMP + k
            se_ref[pl.ds(at, BY), :] = x_ref[tile * BY : tile * BY + BY, :]
            tile = COMP + NMET + k
            mx_ref[high, k * BY : k * BY + BY, :] = x_ref[tile * BY : tile * BY + BY, :]
        for w in range(3):
            tile = COMP + 2 * NMET + w
            plane = jnp.where(is_high, 7 + w, 2 - w)
            at = pl.multiple_of(plane * DPITCH + 16, 8)
            de_ref[pl.ds(at, BY), :] = x_ref[tile * BY : tile * BY + BY, :]
        tile = COMP + 2 * NMET + 3
        cxl_ref[high] = x_ref[tile * BY : tile * BY + BY, :]
        for side, y_high in ((0, even_y), (1, 1 - even_y)):
            y_is_high = y_high == 1
            base = side * 64
            r1 = jnp.where(y_is_high, 16, 7)
            r2 = jnp.where(y_is_high, 17, 6)
            se_ref[rows(p1 * PITCH + r1, NMET, 8 * PITCH), :] = c_ref[base : base + 16, :]
            se_ref[rows(p2 * PITCH + r1, NMET, 8 * PITCH), :] = c_ref[base + 16 : base + 32, :]
            se_ref[rows(p1 * PITCH + r2, NMET, 8 * PITCH), :] = c_ref[base + 32 : base + 48, :]
            from_plane = jnp.where(is_high, 0, BX - 1)
            step = jnp.where(is_high, 1, -1)
            misc = base + 48 + from_plane
            se_ref[pl.ds((NMET * 8 + p1) * PITCH + r1, 1), :] = c_ref[pl.ds(misc, 1), :]
            for w in range(3):
                d_row = jnp.where(y_is_high, 24 + w, 15 - w)
                for q in range(3):
                    plane = jnp.where(is_high, 7 + q, 2 - q)
                    de_ref[pl.ds(plane * DPITCH + d_row, 1), :] = c_ref[
                        pl.ds(misc + 4 + 4 * w + q * step, 1), :
                    ]

    columns = []
    for p in range(10):
        at = p * DPITCH + 8
        columns.append(
            de_ref[at - 1 : at + 23, :] + de_ref[at : at + 24, :] + de_ref[at + 1 : at + 25, :]
        )
    for p in range(8):
        flat = columns[p] + columns[p + 1] + columns[p + 2]
        weight = flat + masked_prev(flat) + masked_next(flat)
        inside = weight > 0.0
        rw_ref[p * PITCH : (p + 1) * PITCH, :] = jnp.where(
            inside, 1.0 / jnp.where(inside, weight, 1.0), 0.0
        )

    copies = []
    for first in range(NMET, -1, -GROUP):
        group = [first] if first == NMET else range(first, first + GROUP)
        share_sums(group, se_ref, rw_ref, ys_ref)
        for k in group:
            for p in range(2, 6) if k == NMET else range(1, 7):
                dens = de_ref[(p + 1) * DPITCH + 16 : (p + 1) * DPITCH + 24, :]
                at = (k * 8 + p) * BY
                flat = (
                    ys_ref[at - BY : at, :] + ys_ref[at : at + BY, :] + ys_ref[at + BY : at + 2 * BY, :]
                )
                collected = flat + masked_prev(flat) + masked_next(flat)
                deposit = dens * collected
                if k == NMET:
                    cell = (p - 2) * BY
                    energy_out_ref[cell : cell + BY, :] = energy_ref[cell : cell + BY, :] + deposit
                    continue
                if p == 1:
                    metal = mx_ref[0, k * BY : k * BY + BY, :]
                elif p == 6:
                    metal = mx_ref[1, k * BY : k * BY + BY, :]
                else:
                    cell = (k * BX + p - 2) * BY
                    metal = metals_ref[cell : cell + BY, :]
                e_at = (k * 8 + p) * PITCH + 8
                ee_ref[e_at : e_at + BY, :] = metal + deposit
        if first == NMET:
            copies.append(pltpu.make_async_copy(energy_out_ref, energy_out_hbm, sems.at[0]))
            copies[-1].start()
            continue

        for side in range(2):
            row = (7, 16)[side]
            dens = de_ref[rows(DPITCH + row + 8, 8, DPITCH), :]
            inv = [rw_ref[rows(row - 1 + d, 8, PITCH), :] for d in range(3)]
            for k in group:
                value = None
                for d in range(3):
                    term = se_ref[rows(k * 8 * PITCH + row - 1 + d, 8, PITCH), :] * inv[d]
                    value = term if value is None else value + term
                flat = value + pltpu.roll(value, 1, 0) + pltpu.roll(value, 7, 0)
                deposit = dens * (flat + masked_prev(flat) + masked_next(flat))
                ee_ref[rows(k * 8 * PITCH + row, 8, PITCH), :] = (
                    my_ref[side, k * 8 : k * 8 + 8, :] + deposit
                )

        for x in range(BX):
            at = x * BY
            cx_up = cx_ref[at : at + BY, :]
            cx_low = cxl_ref[0] if x == 0 else cx_ref[at - BY : at, :]
            cy_up = cy_ref[at : at + BY, :]
            cy_low = cye_ref[x * PITCH + 7 : x * PITCH + 15, :]
            cz_up = cz_ref[at : at + BY, :]
            cz_low = masked_prev(cz_up)
            to_next = [-jnp.minimum(c, 0.0) for c in (cx_up, cy_up, cz_up)]
            from_prev = [jnp.maximum(c, 0.0) for c in (cx_low, cy_low, cz_low)]
            middle = 1.0
            for up, low in ((cx_up, cx_low), (cy_up, cy_low), (cz_up, cz_low)):
                middle = middle - jnp.maximum(up, 0.0) + jnp.minimum(low, 0.0)
            to_next[2] = jnp.where(not_last, to_next[2], 0.0)
            for k in group:
                e_at = (k * 8 + x + 2) * PITCH + 8
                own = ee_ref[e_at : e_at + BY, :]
                result = middle * own
                result = result + to_next[0] * ee_ref[e_at + PITCH : e_at + PITCH + BY, :]
                result = result + from_prev[0] * ee_ref[e_at - PITCH : e_at - PITCH + BY, :]
                result = result + to_next[1] * ee_ref[e_at + 1 : e_at + 1 + BY, :]
                result = result + from_prev[1] * ee_ref[e_at - 1 : e_at - 1 + BY, :]
                result = result + to_next[2] * next_z(own)
                result = result + from_prev[2] * prev_z(own)
                cell = (k * BX + x) * BY
                out_ref[cell : cell + BY, :] = result
        piece = pl.ds(first * BX * BY, GROUP * BX * BY)
        copies.append(
            pltpu.make_async_copy(out_ref.at[piece], out_hbm.at[piece], sems.at[len(copies)])
        )
        copies[-1].start()
    for copy in copies:
        copy.wait()


def share_sums(group, se_ref, rw_ref, ys_ref):
    for p in range(8):
        inv = [rw_ref[p * PITCH + 7 + d : p * PITCH + 15 + d, :] for d in range(3)]
        for k in group:
            if k == NMET and p in (0, 7):
                continue
            at = (k * 8 + p) * PITCH + 7
            value = None
            for d in range(3):
                term = se_ref[at + d : at + d + BY, :] * inv[d]
                value = term if value is None else value + term
            ys_ref[(k * 8 + p) * BY : (k * 8 + p) * BY + BY, :] = value


def swaps():
    nx = lax.axis_size("gx")
    ny = lax.axis_size("gy")
    rounds = []
    for along_x in (True, False):
        for first in (0, 1):
            pairs = []
            for x in range(nx):
                for y in range(ny):
                    place_, count = (x, nx) if along_x else (y, ny)
                    mate = place_ + 1 if place_ % 2 == first else place_ - 1
                    if 0 <= mate < count:
                        to = (mate, y) if along_x else (x, mate)
                    elif along_x and ny % 2 == 0:
                        to = (x, (y + ny // 2) % ny)
                    elif not along_x and nx % 2 == 0:
                        to = (x + 1 - 2 * (x % 2), y)
                    else:
                        to = (x, y)
                    pairs.append((x * ny + y, to[0] * ny + to[1]))
            rounds.append(pairs)
    return rounds


def swap(value, pairs):
    return lax.ppermute(value, ("gx", "gy"), pairs)


VM = pl.BlockSpec(memory_space=pltpu.VMEM)
HB = pl.BlockSpec(memory_space=pltpu.HBM)


def buffer(count):
    return pltpu.VMEM((count, NZ), F32)


def body(masses, table, star_mask, density, metals, energy, courant_x, courant_y, courant_z):
    cells = BX * BY
    masses = masses.reshape(BINS, cells, NZ)
    star_mask, density, energy, courant_x, courant_y, courant_z = (
        a.reshape(cells, NZ) for a in (star_mask, density, energy, courant_x, courant_y, courant_z)
    )
    metals = metals.reshape(NMET * cells, NZ)
    src, ya, yb, xa, xb, za, zb, *local = pl.pallas_call(
        sources_kernel,
        name="sources",
        out_shape=[buffer(COMP * cells)]
        + [buffer(count) for count in (YROWS, YROWS, XROWS, XROWS, ZROWS, ZROWS)]
        + [buffer(cells), buffer(NMET * cells)] + [buffer(cells)] * 4,
        in_specs=[HB] * 9,
        out_specs=[VM] * 13,
        scratch_shapes=[
            pltpu.VMEM((BINS, cells, NZ), BF16),
            pltpu.VMEM((COMP, BINS), BF16),
            pltpu.VMEM((cells, NZ), jnp.int32),
            pltpu.VMEM((COMP * 16, BINS * 16), BF16),
            pltpu.VMEM((24, BINS * 16), F32),
            pltpu.SemaphoreType.DMA((CHUNKS,)),
            pltpu.SemaphoreType.DMA((8,)),
        ],
        compiler_params=pltpu.CompilerParams(vmem_limit_bytes=32 * 1024 * 1024),
    )(
        *(
            pltpu.with_memory_space_constraint(a, pltpu.HBM)
            for a in (
                masses, table.T, star_mask, density, metals, energy, courant_x, courant_y, courant_z
            )
        )
    )
    pairs_xa, pairs_xb, pairs_ya, pairs_yb = swaps()
    ya = swap(ya, pairs_ya)
    yb = swap(yb, pairs_yb)
    xa = swap(xa, pairs_xa)
    xb = swap(xb, pairs_xb)
    za = swap(za, pairs_ya)
    zb = swap(zb, pairs_yb)
    ca, cb = pl.pallas_call(
        corner_kernel,
        name="corners",
        out_shape=[buffer(CROWS), buffer(CROWS)],
        in_specs=[VM] * 4,
        out_specs=[VM, VM],
        compiler_params=pltpu.CompilerParams(vmem_limit_bytes=4 * 1024 * 1024),
    )(*(pltpu.with_memory_space_constraint(a, pltpu.VMEM) for a in (ya, yb, xa, xb)))
    ca = swap(ca, pairs_xa)
    cb = swap(cb, pairs_xb)
    advected, energy_out = pl.pallas_call(
        finish_kernel,
        name="finish",
        out_shape=[
            jax.ShapeDtypeStruct((NMET * cells, NZ), F32),
            jax.ShapeDtypeStruct((cells, NZ), F32),
        ],
        in_specs=[VM] * 15,
        out_specs=[HB, HB],
        scratch_shapes=[
            pltpu.VMEM((NMET * cells, NZ), F32),
            pltpu.VMEM((cells, NZ), F32),
            pltpu.SemaphoreType.DMA((1 + NMET // GROUP,)),
            pltpu.VMEM((COMP * 8 * PITCH, NZ), F32),
            pltpu.VMEM((10 * DPITCH, NZ), F32),
            pltpu.VMEM((8 * PITCH, NZ), F32),
            pltpu.VMEM((COMP * 8 * BY, NZ), F32),
            pltpu.VMEM((NMET * 8 * PITCH, NZ), F32),
            pltpu.VMEM((2, NMET * BY, NZ), F32),
            pltpu.VMEM((2, NMET * 8, NZ), F32),
            pltpu.VMEM((2, BY, NZ), F32),
            pltpu.VMEM((BX * PITCH, NZ), F32),
        ],
        compiler_params=pltpu.CompilerParams(vmem_limit_bytes=32 * 1024 * 1024),
    )(
        *(
            pltpu.with_memory_space_constraint(a, pltpu.VMEM)
            for a in (src, ya, yb, xa, xb, za, zb, ca, cb, *local)
        )
    )
    return advected.reshape(NMET, BX, BY, NZ), energy_out.reshape(BX, BY, NZ)


def solution(mesh):
    field = P("gx", "gy", None)
    stack = P(None, "gx", "gy", None)
    in_specs = (stack, P(), field, field, stack, field, field, field, field)
    out_specs = (stack, field)
    return jax.shard_map(body, mesh=mesh, in_specs=in_specs, out_specs=out_specs, check_vma=False)
```

```python
import jax
import jax.numpy as jnp
from jax import lax
from jax.experimental import pallas as pl
from jax.experimental.pallas import tpu as pltpu
from jax.sharding import PartitionSpec as P

F32 = jnp.float32
BF16 = jnp.bfloat16
BINS = 256
COMP = 17
NMET = 16
BX = 4
BY = 8
NZ = 128
CHUNKS = 4
GROUP = 4
YROWS = 112
ZROWS = 104
XROWS = 424
CROWS = 64
PITCH = 24
DPITCH = 40


def rows(start, count, stride=1):
    return pl.ds(start, count) if stride == 1 else pl.ds(start, count, stride)


def place(axis):
    index = lax.axis_index(axis)
    last = index == lax.axis_size(axis) - 1
    odd = index % 2
    alone_a = jnp.logical_and(odd == 0, last)
    alone_b = jnp.logical_or(index == 0, jnp.logical_and(odd == 1, last))
    return 1 - odd, alone_a, alone_b


def sources_kernel(
    masses_hbm, table_hbm, star_hbm, dens_hbm, metals_hbm, energy_hbm, cx_hbm, cy_hbm, cz_hbm,
    src_ref, ya_ref, yb_ref, xa_ref, xb_ref, za_ref, zb_ref,
    dens_ref, metals_ref, energy_ref, cx_ref, cy_ref, cz_ref,
    mass_buf, table_ref, star_ref, expand_ref, wide_ref, mass_sems, sems,
):
    small = [
        (table_hbm, table_ref), (star_hbm, star_ref), (dens_hbm, dens_ref), (metals_hbm, metals_ref),
        (cx_hbm, cx_ref), (cy_hbm, cy_ref), (cz_hbm, cz_ref), (energy_hbm, energy_ref),
    ]
    small_copies = [
        pltpu.make_async_copy(hbm, ref, sems.at[i]) for i, (hbm, ref) in enumerate(small)
    ]
    per = BINS // CHUNKS
    copies = [
        pltpu.make_async_copy(
            masses_hbm.at[pl.ds(c * per, per)], mass_buf.at[pl.ds(c * per, per)], mass_sems.at[c]
        )
        for c in range(CHUNKS)
    ]
    small_copies[0].start()
    for copy in copies:
        copy.start()
    for copy in small_copies[1:]:
        copy.start()

    width = BINS * 16
    group = lax.broadcasted_iota(jnp.int32, (8, NZ), 1) // 16
    same = (
        lax.broadcasted_iota(jnp.int32, (16, NZ), 1) % 16
        == lax.broadcasted_iota(jnp.int32, (16, NZ), 0)
    )
    small_copies[0].wait()
    turned = table_ref[...].astype(F32)
    turned = jnp.concatenate([turned, jnp.zeros((24 - COMP, BINS), F32)], axis=0)
    for t in range(width // NZ):
        first = 8 * t
        half = first // NZ
        for r in range(3):
            tile = turned[8 * r : 8 * r + 8, half * NZ : (half + 1) * NZ]
            wide_ref[8 * r : 8 * r + 8, t * NZ : (t + 1) * NZ] = jnp.take_along_axis(
                tile, group + first % NZ, axis=1
            )
    for t in range(width // NZ):
        for k in range(COMP):
            line = jnp.broadcast_to(wide_ref[k : k + 1, t * NZ : (t + 1) * NZ], (16, NZ))
            expand_ref[k * 16 : k * 16 + 16, t * NZ : (t + 1) * NZ] = jnp.where(
                same, line, 0.0
            ).astype(BF16)

    total = None
    for c in range(CHUNKS):
        copies[c].wait()
        part = mass_buf[c * per : (c + 1) * per]
        right = jnp.concatenate(
            [part[:, 16 * j : 16 * j + 16].reshape(per * 16, NZ) for j in range(2)], axis=1
        )
        left = expand_ref[:, c * per * 16 : (c + 1) * per * 16]
        prod = jnp.dot(left, right, preferred_element_type=F32)
        total = prod if total is None else total + prod
    for copy in small_copies[1:]:
        copy.wait()
    for j in range(2):
        for s in range(2):
            x = 2 * j + s
            mask = star_ref[x * BY : x * BY + BY, :].astype(F32)
            for k in range(COMP):
                at = (k * BX + x) * BY
                piece = total[k * 16 + s * BY : k * 16 + s * BY + BY, j * NZ : (j + 1) * NZ]
                src_ref[at : at + BY, :] = piece * mask

    even_x, alone_xa, alone_xb = place("gx")
    even_y, alone_ya, alone_yb = place("gy")
    plane = BX * BY
    for out, rest, high in ((ya_ref, za_ref, even_y), (yb_ref, zb_ref, 1 - even_y)):
        near = jnp.where(high == 1, BY - 1, 0)
        step = jnp.where(high == 1, -1, 1)
        out[0:64, :] = src_ref[rows(near, 64, BY), :]
        for i, x in enumerate((0, BX - 1)):
            out[64 + 16 * i : 80 + 16 * i, :] = src_ref[rows(x * BY + near + step, 16, plane), :]
        out[96:100, :] = src_ref[rows(NMET * plane + near, 4, BY), :]
        out[100:104, :] = dens_ref[rows(near, 4, BY), :]
        out[104:108, :] = dens_ref[rows(near + step, 4, BY), :]
        out[108:112, :] = dens_ref[rows(near + 2 * step, 4, BY), :]
        rest[0:64, :] = metals_ref[rows(near, 64, BY), :]
        for x in range(1, BX - 1):
            at = 64 + 16 * (x - 1)
            rest[at : at + 16, :] = src_ref[rows(x * BY + near + step, 16, plane), :]
        rest[96:100, :] = cy_ref[rows(near, 4, BY), :]
        rest[100:104, :] = jnp.zeros((4, NZ), F32)
    for out, high in ((xa_ref, even_x), (xb_ref, 1 - even_x)):
        near = jnp.where(high == 1, BX - 1, 0) * BY
        step = jnp.where(high == 1, -1, 1) * BY
        tile = 0
        pieces = [(src_ref, k * BX * BY + near) for k in range(COMP)]
        pieces += [(src_ref, k * BX * BY + near + step) for k in range(NMET)]
        pieces += [(metals_ref, k * BX * BY + near) for k in range(NMET)]
        pieces += [(dens_ref, near), (dens_ref, near + step), (dens_ref, near + 2 * step)]
        pieces += [(cx_ref, near)]
        for ref, at in pieces:
            out[tile * BY : tile * BY + BY, :] = ref[pl.ds(pl.multiple_of(at, BY), BY), :]
            tile += 1
    for out, alone in (
        (ya_ref, alone_ya), (yb_ref, alone_yb), (za_ref, alone_ya), (zb_ref, alone_yb),
        (xa_ref, alone_xa), (xb_ref, alone_xb),
    ):
        clear(out, alone)


def clear(ref, alone):
    @pl.when(alone)
    def _():
        ref[...] = jnp.zeros(ref.shape, F32)


def corner_kernel(y_ref, xa_ref, xb_ref, ca_ref, cb_ref):
    del xa_ref, xb_ref
    even_x, alone_a, alone_b = place("gx")
    for out, high in ((ca_ref, even_x), (cb_ref, 1 - even_x)):
        near = jnp.where(high == 1, BX - 1, 0)
        step = jnp.where(high == 1, -1, 1)
        out[0:16, :] = y_ref[rows(near, 16, BX), :]
        out[16:32, :] = y_ref[rows(near + step, 16, BX), :]
        at = pl.multiple_of(jnp.where(high == 1, 80, 64), 16)
        out[32:48, :] = y_ref[pl.ds(at, 16), :]
        out[48:64, :] = y_ref[96:112, :]
    clear(ca_ref, alone_a)
    clear(cb_ref, alone_b)


def sort_kernel(za_ref, zb_ref, zlow_ref, zhigh_ref):
    a_is_high = place("gy")[0] == 1
    a = za_ref[...]
    b = zb_ref[...]
    zlow_ref[...] = jnp.where(a_is_high, b, a)
    zhigh_ref[...] = jnp.where(a_is_high, a, b)


def finish_kernel(
    src_ref, ya_ref, yb_ref, xa_ref, xb_ref, zlow_ref, zhigh_ref, cbb_ref, cab_ref, cba_ref, caa_ref,
    dens_ref, metals_ref, energy_ref, cx_ref, cy_ref, cz_ref,
    out_hbm, energy_out_hbm,
    out_ref, energy_out_ref, sems,
    se_ref, de_ref, rw_ref, ys_ref, ee_ref, mx_ref, my_ref, cxl_ref, cye_ref,
):
    even_x = place("gx")[0]
    even_y = place("gy")[0]
    lane = lax.broadcasted_iota(jnp.int32, (1, NZ), 1)
    not_first = lane > 0
    not_last = lane < NZ - 1

    def prev_z(v):
        return pltpu.roll(v, 1, 1)

    def next_z(v):
        return pltpu.roll(v, NZ - 1, 1)

    def masked_prev(v):
        return jnp.where(not_first, prev_z(v), 0.0)

    def masked_next(v):
        return jnp.where(not_last, next_z(v), 0.0)

    de_ref[...] = jnp.zeros(de_ref.shape, F32)

    for x in range(BX):
        at = x * BY
        d_at = (x + 3) * DPITCH + 16
        de_ref[d_at : d_at + BY, :] = dens_ref[at : at + BY, :]
        cye_ref[x * PITCH + 8 : x * PITCH + 16, :] = cy_ref[at : at + BY, :]
        for k in range(COMP):
            s_at = (k * 8 + x + 2) * PITCH + 8
            se_ref[s_at : s_at + BY, :] = src_ref[(k * BX + x) * BY : (k * BX + x + 1) * BY, :]

    for y_ref, high in ((ya_ref, even_y), (yb_ref, 1 - even_y)):
        is_high = high == 1
        r1 = jnp.where(is_high, 16, 7)
        r2 = jnp.where(is_high, 17, 6)
        for k in range(NMET):
            at = k * BX
            base = (k * 8 + 2) * PITCH
            se_ref[rows(base + r1, BX, PITCH), :] = y_ref[at : at + BX, :]
        for i, x in enumerate((0, BX - 1)):
            se_ref[rows((x + 2) * PITCH + r2, NMET, 8 * PITCH), :] = y_ref[64 + 16 * i : 80 + 16 * i, :]
        base = (NMET * 8 + 2) * PITCH
        se_ref[rows(base + r1, BX, PITCH), :] = y_ref[96:100, :]
        for w in range(3):
            d_row = jnp.where(is_high, 24 + w, 15 - w)
            de_ref[rows(3 * DPITCH + d_row, BX, DPITCH), :] = y_ref[100 + 4 * w : 104 + 4 * w, :]
    for side, z_ref in enumerate((zlow_ref, zhigh_ref)):
        for k in range(NMET):
            my_ref[side, k * 8 + 2 : k * 8 + 2 + BX, :] = z_ref[k * BX : k * BX + BX, :]
        for x in range(1, BX - 1):
            r2 = (6, 17)[side]
            se_ref[rows((x + 2) * PITCH + r2, NMET, 8 * PITCH), :] = z_ref[48 + 16 * x : 64 + 16 * x, :]
    cye_ref[rows(7, BX, PITCH), :] = zlow_ref[96:100, :]

    for x_ref, corners, high in (
        (xa_ref, (caa_ref, cab_ref), even_x),
        (xb_ref, (cba_ref, cbb_ref), 1 - even_x),
    ):
        is_high = high == 1
        p1 = jnp.where(is_high, 6, 1)
        p2 = jnp.where(is_high, 7, 0)
        for k in range(COMP):
            at = pl.multiple_of((k * 8 + p1) * PITCH + 8, 8)
            se_ref[pl.ds(at, BY), :] = x_ref[k * BY : k * BY + BY, :]
        for k in range(NMET):
            at = pl.multiple_of((k * 8 + p2) * PITCH + 8, 8)
            tile = COMP + k
            se_ref[pl.ds(at, BY), :] = x_ref[tile * BY : tile * BY + BY, :]
            tile = COMP + NMET + k
            mx_ref[high, k * BY : k * BY + BY, :] = x_ref[tile * BY : tile * BY + BY, :]
        for w in range(3):
            tile = COMP + 2 * NMET + w
            plane = jnp.where(is_high, 7 + w, 2 - w)
            at = pl.multiple_of(plane * DPITCH + 16, 8)
            de_ref[pl.ds(at, BY), :] = x_ref[tile * BY : tile * BY + BY, :]
        tile = COMP + 2 * NMET + 3
        cxl_ref[high] = x_ref[tile * BY : tile * BY + BY, :]
        for c_ref, y_high in zip(corners, (even_y, 1 - even_y)):
            y_is_high = y_high == 1
            r1 = jnp.where(y_is_high, 16, 7)
            r2 = jnp.where(y_is_high, 17, 6)
            se_ref[rows(p1 * PITCH + r1, NMET, 8 * PITCH), :] = c_ref[0:16, :]
            se_ref[rows(p2 * PITCH + r1, NMET, 8 * PITCH), :] = c_ref[16:32, :]
            se_ref[rows(p1 * PITCH + r2, NMET, 8 * PITCH), :] = c_ref[32:48, :]
            from_plane = jnp.where(is_high, 0, BX - 1)
            step = jnp.where(is_high, 1, -1)
            misc = 48 + from_plane
            se_ref[pl.ds((NMET * 8 + p1) * PITCH + r1, 1), :] = c_ref[pl.ds(misc, 1), :]
            for w in range(3):
                d_row = jnp.where(y_is_high, 24 + w, 15 - w)
                for q in range(3):
                    plane = jnp.where(is_high, 7 + q, 2 - q)
                    de_ref[pl.ds(plane * DPITCH + d_row, 1), :] = c_ref[
                        pl.ds(misc + 4 + 4 * w + q * step, 1), :
                    ]

    columns = []
    for p in range(10):
        at = p * DPITCH + 8
        columns.append(
            de_ref[at - 1 : at + 23, :] + de_ref[at : at + 24, :] + de_ref[at + 1 : at + 25, :]
        )
    for p in range(8):
        flat = columns[p] + columns[p + 1] + columns[p + 2]
        weight = flat + masked_prev(flat) + masked_next(flat)
        inside = weight > 0.0
        rw_ref[p * PITCH : (p + 1) * PITCH, :] = jnp.where(
            inside, 1.0 / jnp.where(inside, weight, 1.0), 0.0
        )

    copies = []
    for first in range(NMET, -1, -GROUP):
        group = [first] if first == NMET else range(first, first + GROUP)
        share_sums(group, se_ref, rw_ref, ys_ref)
        for k in group:
            for p in range(2, 6) if k == NMET else range(1, 7):
                dens = de_ref[(p + 1) * DPITCH + 16 : (p + 1) * DPITCH + 24, :]
                at = (k * 8 + p) * BY
                flat = (
                    ys_ref[at - BY : at, :] + ys_ref[at : at + BY, :] + ys_ref[at + BY : at + 2 * BY, :]
                )
                collected = flat + masked_prev(flat) + masked_next(flat)
                deposit = dens * collected
                if k == NMET:
                    cell = (p - 2) * BY
                    energy_out_ref[cell : cell + BY, :] = energy_ref[cell : cell + BY, :] + deposit
                    continue
                if p == 1:
                    metal = mx_ref[0, k * BY : k * BY + BY, :]
                elif p == 6:
                    metal = mx_ref[1, k * BY : k * BY + BY, :]
                else:
                    cell = (k * BX + p - 2) * BY
                    metal = metals_ref[cell : cell + BY, :]
                e_at = (k * 8 + p) * PITCH + 8
                ee_ref[e_at : e_at + BY, :] = metal + deposit
        if first == NMET:
            copies.append(pltpu.make_async_copy(energy_out_ref, energy_out_hbm, sems.at[0]))
            copies[-1].start()
            continue

        for side in range(2):
            row = (7, 16)[side]
            dens = de_ref[rows(DPITCH + row + 8, 8, DPITCH), :]
            inv = [rw_ref[rows(row - 1 + d, 8, PITCH), :] for d in range(3)]
            for k in group:
                value = None
                for d in range(3):
                    term = se_ref[rows(k * 8 * PITCH + row - 1 + d, 8, PITCH), :] * inv[d]
                    value = term if value is None else value + term
                flat = value + pltpu.roll(value, 1, 0) + pltpu.roll(value, 7, 0)
                deposit = dens * (flat + masked_prev(flat) + masked_next(flat))
                ee_ref[rows(k * 8 * PITCH + row, 8, PITCH), :] = (
                    my_ref[side, k * 8 : k * 8 + 8, :] + deposit
                )

        for x in range(BX):
            at = x * BY
            cx_up = cx_ref[at : at + BY, :]
            cx_low = cxl_ref[0] if x == 0 else cx_ref[at - BY : at, :]
            cy_up = cy_ref[at : at + BY, :]
            cy_low = cye_ref[x * PITCH + 7 : x * PITCH + 15, :]
            cz_up = cz_ref[at : at + BY, :]
            cz_low = masked_prev(cz_up)
            to_next = [-jnp.minimum(c, 0.0) for c in (cx_up, cy_up, cz_up)]
            from_prev = [jnp.maximum(c, 0.0) for c in (cx_low, cy_low, cz_low)]
            middle = 1.0
            for up, low in ((cx_up, cx_low), (cy_up, cy_low), (cz_up, cz_low)):
                middle = middle - jnp.maximum(up, 0.0) + jnp.minimum(low, 0.0)
            to_next[2] = jnp.where(not_last, to_next[2], 0.0)
            for k in group:
                e_at = (k * 8 + x + 2) * PITCH + 8
                own = ee_ref[e_at : e_at + BY, :]
                result = middle * own
                result = result + to_next[0] * ee_ref[e_at + PITCH : e_at + PITCH + BY, :]
                result = result + from_prev[0] * ee_ref[e_at - PITCH : e_at - PITCH + BY, :]
                result = result + to_next[1] * ee_ref[e_at + 1 : e_at + 1 + BY, :]
                result = result + from_prev[1] * ee_ref[e_at - 1 : e_at - 1 + BY, :]
                result = result + to_next[2] * next_z(own)
                result = result + from_prev[2] * prev_z(own)
                cell = (k * BX + x) * BY
                out_ref[cell : cell + BY, :] = result
        piece = pl.ds(first * BX * BY, GROUP * BX * BY)
        copies.append(
            pltpu.make_async_copy(out_ref.at[piece], out_hbm.at[piece], sems.at[len(copies)])
        )
        copies[-1].start()
    for copy in copies:
        copy.wait()


def share_sums(group, se_ref, rw_ref, ys_ref):
    for p in range(8):
        inv = [rw_ref[p * PITCH + 7 + d : p * PITCH + 15 + d, :] for d in range(3)]
        for k in group:
            if k == NMET and p in (0, 7):
                continue
            at = (k * 8 + p) * PITCH + 7
            value = None
            for d in range(3):
                term = se_ref[at + d : at + d + BY, :] * inv[d]
                value = term if value is None else value + term
            ys_ref[(k * 8 + p) * BY : (k * 8 + p) * BY + BY, :] = value


def swaps():
    nx = lax.axis_size("gx")
    ny = lax.axis_size("gy")
    rounds = []
    for along_x in (True, False):
        for first in (0, 1):
            pairs = []
            for x in range(nx):
                for y in range(ny):
                    place_, count = (x, nx) if along_x else (y, ny)
                    mate = place_ + 1 if place_ % 2 == first else place_ - 1
                    if 0 <= mate < count:
                        to = (mate, y) if along_x else (x, mate)
                    elif along_x and ny % 2 == 0:
                        to = (x, (y + ny // 2) % ny)
                    elif not along_x and nx % 2 == 0:
                        to = (x + 1 - 2 * (x % 2), y)
                    else:
                        to = (x, y)
                    pairs.append((x * ny + y, to[0] * ny + to[1]))
            rounds.append(pairs)
    return rounds


def swap(value, pairs):
    return lax.ppermute(value, ("gx", "gy"), pairs)


VM = pl.BlockSpec(memory_space=pltpu.VMEM)
HB = pl.BlockSpec(memory_space=pltpu.HBM)


def buffer(count):
    return pltpu.VMEM((count, NZ), F32)


def body(masses, table, star_mask, density, metals, energy, courant_x, courant_y, courant_z):
    cells = BX * BY
    masses = masses.reshape(BINS, cells, NZ)
    star_mask, density, energy, courant_x, courant_y, courant_z = (
        a.reshape(cells, NZ) for a in (star_mask, density, energy, courant_x, courant_y, courant_z)
    )
    metals = metals.reshape(NMET * cells, NZ)
    src, ya, yb, xa, xb, za, zb, *local = pl.pallas_call(
        sources_kernel,
        name="sources",
        out_shape=[buffer(COMP * cells)]
        + [buffer(count) for count in (YROWS, YROWS, XROWS, XROWS, ZROWS, ZROWS)]
        + [buffer(cells), buffer(NMET * cells)] + [buffer(cells)] * 4,
        in_specs=[HB] * 9,
        out_specs=[VM] * 13,
        scratch_shapes=[
            pltpu.VMEM((BINS, cells, NZ), BF16),
            pltpu.VMEM((COMP, BINS), BF16),
            pltpu.VMEM((cells, NZ), jnp.int32),
            pltpu.VMEM((COMP * 16, BINS * 16), BF16),
            pltpu.VMEM((24, BINS * 16), F32),
            pltpu.SemaphoreType.DMA((CHUNKS,)),
            pltpu.SemaphoreType.DMA((8,)),
        ],
        compiler_params=pltpu.CompilerParams(vmem_limit_bytes=32 * 1024 * 1024),
    )(
        *(
            pltpu.with_memory_space_constraint(a, pltpu.HBM)
            for a in (
                masses, table.T, star_mask, density, metals, energy, courant_x, courant_y, courant_z
            )
        )
    )
    pairs_xa, pairs_xb, pairs_ya, pairs_yb = swaps()
    ya = swap(ya, pairs_ya)
    yb = swap(yb, pairs_yb)
    xa = swap(xa, pairs_xa)
    xb = swap(xb, pairs_xb)
    za = swap(za, pairs_ya)
    zb = swap(zb, pairs_yb)
    corners = []
    for y in (ya, yb):
        ca, cb = pl.pallas_call(
            corner_kernel,
            name="corners",
            out_shape=[buffer(CROWS), buffer(CROWS)],
            in_specs=[VM] * 3,
            out_specs=[VM, VM],
            compiler_params=pltpu.CompilerParams(vmem_limit_bytes=4 * 1024 * 1024),
        )(*(pltpu.with_memory_space_constraint(a, pltpu.VMEM) for a in (y, xa, xb)))
        corners += [swap(ca, pairs_xa), swap(cb, pairs_xb)]
    z = pl.pallas_call(
        sort_kernel,
        name="sort",
        out_shape=[buffer(ZROWS), buffer(ZROWS)],
        in_specs=[VM] * 2,
        out_specs=[VM] * 2,
        compiler_params=pltpu.CompilerParams(vmem_limit_bytes=4 * 1024 * 1024),
    )(*(pltpu.with_memory_space_constraint(a, pltpu.VMEM) for a in (za, zb)))
    advected, energy_out = pl.pallas_call(
        finish_kernel,
        name="finish",
        out_shape=[
            jax.ShapeDtypeStruct((NMET * cells, NZ), F32),
            jax.ShapeDtypeStruct((cells, NZ), F32),
        ],
        in_specs=[VM] * 17,
        out_specs=[HB, HB],
        scratch_shapes=[
            pltpu.VMEM((NMET * cells, NZ), F32),
            pltpu.VMEM((cells, NZ), F32),
            pltpu.SemaphoreType.DMA((1 + NMET // GROUP,)),
            pltpu.VMEM((COMP * 8 * PITCH, NZ), F32),
            pltpu.VMEM((10 * DPITCH, NZ), F32),
            pltpu.VMEM((8 * PITCH, NZ), F32),
            pltpu.VMEM((COMP * 8 * BY, NZ), F32),
            pltpu.VMEM((NMET * 8 * PITCH, NZ), F32),
            pltpu.VMEM((2, NMET * BY, NZ), F32),
            pltpu.VMEM((2, NMET * 8, NZ), F32),
            pltpu.VMEM((2, BY, NZ), F32),
            pltpu.VMEM((BX * PITCH, NZ), F32),
        ],
        compiler_params=pltpu.CompilerParams(vmem_limit_bytes=32 * 1024 * 1024),
    )(
        *(
            pltpu.with_memory_space_constraint(a, pltpu.VMEM)
            for a in (src, ya, yb, xa, xb, *z, *corners[::-1], *local)
        )
    )
    return advected.reshape(NMET, BX, BY, NZ), energy_out.reshape(BX, BY, NZ)


def solution(mesh):
    field = P("gx", "gy", None)
    stack = P(None, "gx", "gy", None)
    in_specs = (stack, P(), field, field, stack, field, field, field, field)
    out_specs = (stack, field)
    return jax.shard_map(body, mesh=mesh, in_specs=in_specs, out_specs=out_specs, check_vma=False)
```

```python
import jax
import jax.numpy as jnp
from jax import lax
from jax.experimental import pallas as pl
from jax.experimental.pallas import tpu as pltpu
from jax.sharding import PartitionSpec as P

F32 = jnp.float32
BF16 = jnp.bfloat16
BINS = 256
COMP = 17
NMET = 16
BX = 4
BY = 8
NZ = 128
CHUNKS = 4
GROUP = 4
YROWS = 112
ZROWS = 114
XROWS = 424
CROWS = 114
PITCH = 24
DENSITIES = [(w, q) for w in range(3) for q in range(3) if w + q < 4]
DPITCH = 40


def rows(start, count, stride=1):
    return pl.ds(start, count) if stride == 1 else pl.ds(start, count, stride)


def place(axis):
    index = lax.axis_index(axis)
    last = index == lax.axis_size(axis) - 1
    odd = index % 2
    alone_a = jnp.logical_and(odd == 0, last)
    alone_b = jnp.logical_or(index == 0, jnp.logical_and(odd == 1, last))
    return 1 - odd, alone_a, alone_b


def sources_kernel(
    masses_hbm, table_hbm, star_hbm, dens_hbm, metals_hbm, energy_hbm, cx_hbm, cy_hbm, cz_hbm,
    src_ref, ya_ref, yb_ref, xa_ref, xb_ref, za_ref, zb_ref,
    dens_ref, metals_ref, energy_ref, cx_ref, cy_ref, cz_ref,
    mass_buf, table_ref, star_ref, expand_ref, wide_ref, mass_sems, sems,
):
    small = [
        (table_hbm, table_ref), (star_hbm, star_ref), (dens_hbm, dens_ref), (metals_hbm, metals_ref),
        (cx_hbm, cx_ref), (cy_hbm, cy_ref), (cz_hbm, cz_ref), (energy_hbm, energy_ref),
    ]
    small_copies = [
        pltpu.make_async_copy(hbm, ref, sems.at[i]) for i, (hbm, ref) in enumerate(small)
    ]
    per = BINS // CHUNKS
    copies = [
        pltpu.make_async_copy(
            masses_hbm.at[pl.ds(c * per, per)], mass_buf.at[pl.ds(c * per, per)], mass_sems.at[c]
        )
        for c in range(CHUNKS)
    ]
    small_copies[0].start()
    for copy in copies:
        copy.start()
    for copy in small_copies[1:]:
        copy.start()

    width = BINS * 16
    group = lax.broadcasted_iota(jnp.int32, (8, NZ), 1) // 16
    same = (
        lax.broadcasted_iota(jnp.int32, (16, NZ), 1) % 16
        == lax.broadcasted_iota(jnp.int32, (16, NZ), 0)
    )
    small_copies[0].wait()
    turned = table_ref[...].astype(F32)
    turned = jnp.concatenate([turned, jnp.zeros((24 - COMP, BINS), F32)], axis=0)
    for t in range(width // NZ):
        first = 8 * t
        half = first // NZ
        for r in range(3):
            tile = turned[8 * r : 8 * r + 8, half * NZ : (half + 1) * NZ]
            wide_ref[8 * r : 8 * r + 8, t * NZ : (t + 1) * NZ] = jnp.take_along_axis(
                tile, group + first % NZ, axis=1
            )
    for t in range(width // NZ):
        for k in range(COMP):
            line = jnp.broadcast_to(wide_ref[k : k + 1, t * NZ : (t + 1) * NZ], (16, NZ))
            expand_ref[k * 16 : k * 16 + 16, t * NZ : (t + 1) * NZ] = jnp.where(
                same, line, 0.0
            ).astype(BF16)

    total = None
    for c in range(CHUNKS):
        copies[c].wait()
        part = mass_buf[c * per : (c + 1) * per]
        right = jnp.concatenate(
            [part[:, 16 * j : 16 * j + 16].reshape(per * 16, NZ) for j in range(2)], axis=1
        )
        left = expand_ref[:, c * per * 16 : (c + 1) * per * 16]
        prod = jnp.dot(left, right, preferred_element_type=F32)
        total = prod if total is None else total + prod
    for copy in small_copies[1:]:
        copy.wait()
    for j in range(2):
        for s in range(2):
            x = 2 * j + s
            mask = star_ref[x * BY : x * BY + BY, :].astype(F32)
            for k in range(COMP):
                at = (k * BX + x) * BY
                piece = total[k * 16 + s * BY : k * 16 + s * BY + BY, j * NZ : (j + 1) * NZ]
                src_ref[at : at + BY, :] = piece * mask

    even_x, alone_xa, alone_xb = place("gx")
    even_y, alone_ya, alone_yb = place("gy")
    plane = BX * BY
    for out, rest, high in ((ya_ref, za_ref, even_y), (yb_ref, zb_ref, 1 - even_y)):
        near = jnp.where(high == 1, BY - 1, 0)
        step = jnp.where(high == 1, -1, 1)
        out[0:64, :] = src_ref[rows(near, 64, BY), :]
        for i, x in enumerate((0, BX - 1)):
            out[64 + 16 * i : 80 + 16 * i, :] = src_ref[rows(x * BY + near + step, 16, plane), :]
        out[96:100, :] = src_ref[rows(NMET * plane + near, 4, BY), :]
        out[100:104, :] = dens_ref[rows(near, 4, BY), :]
        out[104:108, :] = dens_ref[rows(near + step, 4, BY), :]
        out[108:112, :] = dens_ref[rows(near + 2 * step, 4, BY), :]
        rest[0:64, :] = metals_ref[rows(near, 64, BY), :]
        for x in range(1, BX - 1):
            at = 64 + 16 * (x - 1)
            rest[at : at + 16, :] = src_ref[rows(x * BY + near + step, 16, plane), :]
        rest[96:100, :] = cy_ref[rows(near, 4, BY), :]
        rest[100:ZROWS, :] = jnp.zeros((ZROWS - 100, NZ), F32)
    for out, high in ((xa_ref, even_x), (xb_ref, 1 - even_x)):
        near = jnp.where(high == 1, BX - 1, 0) * BY
        step = jnp.where(high == 1, -1, 1) * BY
        tile = 0
        pieces = [(src_ref, k * BX * BY + near) for k in range(COMP)]
        pieces += [(src_ref, k * BX * BY + near + step) for k in range(NMET)]
        pieces += [(metals_ref, k * BX * BY + near) for k in range(NMET)]
        pieces += [(dens_ref, near), (dens_ref, near + step), (dens_ref, near + 2 * step)]
        pieces += [(cx_ref, near)]
        for ref, at in pieces:
            out[tile * BY : tile * BY + BY, :] = ref[pl.ds(pl.multiple_of(at, BY), BY), :]
            tile += 1
    for out, alone in (
        (ya_ref, alone_ya), (yb_ref, alone_yb), (za_ref, alone_ya), (zb_ref, alone_yb),
        (xa_ref, alone_xa), (xb_ref, alone_xb),
    ):
        clear(out, alone)


def clear(ref, alone):
    @pl.when(alone)
    def _():
        ref[...] = jnp.zeros(ref.shape, F32)


def corner_kernel(ya_ref, yb_ref, xa_ref, xb_ref, ca_ref, cb_ref):
    del xa_ref, xb_ref
    even_x, alone_a, alone_b = place("gx")
    for out, high in ((ca_ref, even_x), (cb_ref, 1 - even_x)):
        near = jnp.where(high == 1, BX - 1, 0)
        step = jnp.where(high == 1, -1, 1)
        at = pl.multiple_of(jnp.where(high == 1, 80, 64), 16)
        for side, y_ref in enumerate((ya_ref, yb_ref)):
            base = side * 48
            out[base : base + 16, :] = y_ref[rows(near, 16, BX), :]
            out[base + 16 : base + 32, :] = y_ref[rows(near + step, 16, BX), :]
            out[base + 32 : base + 48, :] = y_ref[pl.ds(at, 16), :]
            base = 96 + side * 9
            out[base : base + 1, :] = y_ref[pl.ds(96 + near, 1), :]
            for i, (w, q) in enumerate(DENSITIES):
                out[base + 1 + i : base + 2 + i, :] = y_ref[pl.ds(100 + 4 * w + near + q * step, 1), :]
    clear(ca_ref, alone_a)
    clear(cb_ref, alone_b)


def sort_kernel(za_ref, zb_ref, zlow_ref, zhigh_ref):
    a_is_high = place("gy")[0] == 1
    a = za_ref[...]
    b = zb_ref[...]
    zlow_ref[...] = jnp.where(a_is_high, b, a)
    zhigh_ref[...] = jnp.where(a_is_high, a, b)


def finish_kernel(
    src_ref, ya_ref, yb_ref, xa_ref, xb_ref, zlow_ref, zhigh_ref, ca_ref, cb_ref,
    dens_ref, metals_ref, energy_ref, cx_ref, cy_ref, cz_ref,
    out_hbm, energy_out_hbm,
    out_ref, energy_out_ref, sems,
    se_ref, de_ref, rw_ref, ys_ref, ee_ref, mx_ref, my_ref, cxl_ref, cye_ref,
):
    even_x = place("gx")[0]
    even_y = place("gy")[0]
    lane = lax.broadcasted_iota(jnp.int32, (1, NZ), 1)
    not_first = lane > 0
    not_last = lane < NZ - 1

    def prev_z(v):
        return pltpu.roll(v, 1, 1)

    def next_z(v):
        return pltpu.roll(v, NZ - 1, 1)

    def masked_prev(v):
        return jnp.where(not_first, prev_z(v), 0.0)

    def masked_next(v):
        return jnp.where(not_last, next_z(v), 0.0)

    de_ref[...] = jnp.zeros(de_ref.shape, F32)

    for x in range(BX):
        at = x * BY
        d_at = (x + 3) * DPITCH + 16
        de_ref[d_at : d_at + BY, :] = dens_ref[at : at + BY, :]
        cye_ref[x * PITCH + 8 : x * PITCH + 16, :] = cy_ref[at : at + BY, :]
        for k in range(COMP):
            s_at = (k * 8 + x + 2) * PITCH + 8
            se_ref[s_at : s_at + BY, :] = src_ref[(k * BX + x) * BY : (k * BX + x + 1) * BY, :]

    for y_ref, high in ((ya_ref, even_y), (yb_ref, 1 - even_y)):
        is_high = high == 1
        r1 = jnp.where(is_high, 16, 7)
        r2 = jnp.where(is_high, 17, 6)
        for k in range(NMET):
            at = k * BX
            base = (k * 8 + 2) * PITCH
            se_ref[rows(base + r1, BX, PITCH), :] = y_ref[at : at + BX, :]
        for i, x in enumerate((0, BX - 1)):
            se_ref[rows((x + 2) * PITCH + r2, NMET, 8 * PITCH), :] = y_ref[64 + 16 * i : 80 + 16 * i, :]
        base = (NMET * 8 + 2) * PITCH
        se_ref[rows(base + r1, BX, PITCH), :] = y_ref[96:100, :]
        for w in range(3):
            d_row = jnp.where(is_high, 24 + w, 15 - w)
            de_ref[rows(3 * DPITCH + d_row, BX, DPITCH), :] = y_ref[100 + 4 * w : 104 + 4 * w, :]
    for side, z_ref in enumerate((zlow_ref, zhigh_ref)):
        for k in range(NMET):
            my_ref[side, k * 8 + 2 : k * 8 + 2 + BX, :] = z_ref[k * BX : k * BX + BX, :]
        for x in range(1, BX - 1):
            r2 = (6, 17)[side]
            se_ref[rows((x + 2) * PITCH + r2, NMET, 8 * PITCH), :] = z_ref[48 + 16 * x : 64 + 16 * x, :]
    cye_ref[rows(7, BX, PITCH), :] = zlow_ref[96:100, :]

    for x_ref, c_ref, high in ((xa_ref, ca_ref, even_x), (xb_ref, cb_ref, 1 - even_x)):
        is_high = high == 1
        p1 = jnp.where(is_high, 6, 1)
        p2 = jnp.where(is_high, 7, 0)
        for k in range(COMP):
            at = pl.multiple_of((k * 8 + p1) * PITCH + 8, 8)
            se_ref[pl.ds(at, BY), :] = x_ref[k * BY : k * BY + BY, :]
        for k in range(NMET):
            at = pl.multiple_of((k * 8 + p2) * PITCH + 8, 8)
            tile = COMP + k
            se_ref[pl.ds(at, BY), :] = x_ref[tile * BY : tile * BY + BY, :]
            tile = COMP + NMET + k
            mx_ref[high, k * BY : k * BY + BY, :] = x_ref[tile * BY : tile * BY + BY, :]
        for w in range(3):
            tile = COMP + 2 * NMET + w
            plane = jnp.where(is_high, 7 + w, 2 - w)
            at = pl.multiple_of(plane * DPITCH + 16, 8)
            de_ref[pl.ds(at, BY), :] = x_ref[tile * BY : tile * BY + BY, :]
        tile = COMP + 2 * NMET + 3
        cxl_ref[high] = x_ref[tile * BY : tile * BY + BY, :]
        for side, y_high in enumerate((even_y, 1 - even_y)):
            base = 48 * side
            y_is_high = y_high == 1
            r1 = jnp.where(y_is_high, 16, 7)
            r2 = jnp.where(y_is_high, 17, 6)
            se_ref[rows(p1 * PITCH + r1, NMET, 8 * PITCH), :] = c_ref[base : base + 16, :]
            se_ref[rows(p2 * PITCH + r1, NMET, 8 * PITCH), :] = c_ref[base + 16 : base + 32, :]
            se_ref[rows(p1 * PITCH + r2, NMET, 8 * PITCH), :] = c_ref[base + 32 : base + 48, :]
            base = 96 + 9 * side
            se_ref[pl.ds((NMET * 8 + p1) * PITCH + r1, 1), :] = c_ref[base : base + 1, :]
            for i, (w, q) in enumerate(DENSITIES):
                d_row = jnp.where(y_is_high, 24 + w, 15 - w)
                plane = jnp.where(is_high, 7 + q, 2 - q)
                de_ref[pl.ds(plane * DPITCH + d_row, 1), :] = c_ref[base + 1 + i : base + 2 + i, :]

    columns = []
    for p in range(10):
        at = p * DPITCH + 8
        columns.append(
            de_ref[at - 1 : at + 23, :] + de_ref[at : at + 24, :] + de_ref[at + 1 : at + 25, :]
        )
    for p in range(8):
        flat = columns[p] + columns[p + 1] + columns[p + 2]
        weight = flat + masked_prev(flat) + masked_next(flat)
        inside = weight > 0.0
        rw_ref[p * PITCH : (p + 1) * PITCH, :] = jnp.where(
            inside, 1.0 / jnp.where(inside, weight, 1.0), 0.0
        )

    copies = []
    for first in range(NMET, -1, -GROUP):
        group = [first] if first == NMET else range(first, first + GROUP)
        share_sums(group, se_ref, rw_ref, ys_ref)
        for k in group:
            for p in range(2, 6) if k == NMET else range(1, 7):
                dens = de_ref[(p + 1) * DPITCH + 16 : (p + 1) * DPITCH + 24, :]
                at = (k * 8 + p) * BY
                flat = (
                    ys_ref[at - BY : at, :] + ys_ref[at : at + BY, :] + ys_ref[at + BY : at + 2 * BY, :]
                )
                collected = flat + masked_prev(flat) + masked_next(flat)
                deposit = dens * collected
                if k == NMET:
                    cell = (p - 2) * BY
                    energy_out_ref[cell : cell + BY, :] = energy_ref[cell : cell + BY, :] + deposit
                    continue
                if p == 1:
                    metal = mx_ref[0, k * BY : k * BY + BY, :]
                elif p == 6:
                    metal = mx_ref[1, k * BY : k * BY + BY, :]
                else:
                    cell = (k * BX + p - 2) * BY
                    metal = metals_ref[cell : cell + BY, :]
                e_at = (k * 8 + p) * PITCH + 8
                ee_ref[e_at : e_at + BY, :] = metal + deposit
        if first == NMET:
            copies.append(pltpu.make_async_copy(energy_out_ref, energy_out_hbm, sems.at[0]))
            copies[-1].start()
            continue

        for side in range(2):
            row = (7, 16)[side]
            dens = de_ref[rows(DPITCH + row + 8, 8, DPITCH), :]
            inv = [rw_ref[rows(row - 1 + d, 8, PITCH), :] for d in range(3)]
            for k in group:
                value = None
                for d in range(3):
                    term = se_ref[rows(k * 8 * PITCH + row - 1 + d, 8, PITCH), :] * inv[d]
                    value = term if value is None else value + term
                flat = value + pltpu.roll(value, 1, 0) + pltpu.roll(value, 7, 0)
                deposit = dens * (flat + masked_prev(flat) + masked_next(flat))
                ee_ref[rows(k * 8 * PITCH + row, 8, PITCH), :] = (
                    my_ref[side, k * 8 : k * 8 + 8, :] + deposit
                )

        for x in range(BX):
            at = x * BY
            cx_up = cx_ref[at : at + BY, :]
            cx_low = cxl_ref[0] if x == 0 else cx_ref[at - BY : at, :]
            cy_up = cy_ref[at : at + BY, :]
            cy_low = cye_ref[x * PITCH + 7 : x * PITCH + 15, :]
            cz_up = cz_ref[at : at + BY, :]
            cz_low = masked_prev(cz_up)
            to_next = [-jnp.minimum(c, 0.0) for c in (cx_up, cy_up, cz_up)]
            from_prev = [jnp.maximum(c, 0.0) for c in (cx_low, cy_low, cz_low)]
            middle = 1.0
            for up, low in ((cx_up, cx_low), (cy_up, cy_low), (cz_up, cz_low)):
                middle = middle - jnp.maximum(up, 0.0) + jnp.minimum(low, 0.0)
            to_next[2] = jnp.where(not_last, to_next[2], 0.0)
            for k in group:
                e_at = (k * 8 + x + 2) * PITCH + 8
                own = ee_ref[e_at : e_at + BY, :]
                result = middle * own
                result = result + to_next[0] * ee_ref[e_at + PITCH : e_at + PITCH + BY, :]
                result = result + from_prev[0] * ee_ref[e_at - PITCH : e_at - PITCH + BY, :]
                result = result + to_next[1] * ee_ref[e_at + 1 : e_at + 1 + BY, :]
                result = result + from_prev[1] * ee_ref[e_at - 1 : e_at - 1 + BY, :]
                result = result + to_next[2] * next_z(own)
                result = result + from_prev[2] * prev_z(own)
                cell = (k * BX + x) * BY
                out_ref[cell : cell + BY, :] = result
        piece = pl.ds(first * BX * BY, GROUP * BX * BY)
        copies.append(
            pltpu.make_async_copy(out_ref.at[piece], out_hbm.at[piece], sems.at[len(copies)])
        )
        copies[-1].start()
    for copy in copies:
        copy.wait()


def share_sums(group, se_ref, rw_ref, ys_ref):
    for p in range(8):
        inv = [rw_ref[p * PITCH + 7 + d : p * PITCH + 15 + d, :] for d in range(3)]
        for k in group:
            if k == NMET and p in (0, 7):
                continue
            at = (k * 8 + p) * PITCH + 7
            value = None
            for d in range(3):
                term = se_ref[at + d : at + d + BY, :] * inv[d]
                value = term if value is None else value + term
            ys_ref[(k * 8 + p) * BY : (k * 8 + p) * BY + BY, :] = value


def swaps():
    nx = lax.axis_size("gx")
    ny = lax.axis_size("gy")
    rounds = []
    for along_x in (True, False):
        for first in (0, 1):
            pairs = []
            for x in range(nx):
                for y in range(ny):
                    place_, count = (x, nx) if along_x else (y, ny)
                    mate = place_ + 1 if place_ % 2 == first else place_ - 1
                    if 0 <= mate < count:
                        to = (mate, y) if along_x else (x, mate)
                    elif along_x and ny % 2 == 0:
                        to = (x, (y + ny // 2) % ny)
                    elif not along_x and nx % 2 == 0:
                        to = (x + 1 - 2 * (x % 2), y)
                    else:
                        to = (x, y)
                    pairs.append((x * ny + y, to[0] * ny + to[1]))
            rounds.append(pairs)
    return rounds


def swap(value, pairs):
    return lax.ppermute(value, ("gx", "gy"), pairs)


VM = pl.BlockSpec(memory_space=pltpu.VMEM)
HB = pl.BlockSpec(memory_space=pltpu.HBM)


def buffer(count):
    return pltpu.VMEM((count, NZ), F32)


def body(masses, table, star_mask, density, metals, energy, courant_x, courant_y, courant_z):
    cells = BX * BY
    masses = masses.reshape(BINS, cells, NZ)
    star_mask, density, energy, courant_x, courant_y, courant_z = (
        a.reshape(cells, NZ) for a in (star_mask, density, energy, courant_x, courant_y, courant_z)
    )
    metals = metals.reshape(NMET * cells, NZ)
    src, ya, yb, xa, xb, za, zb, *local = pl.pallas_call(
        sources_kernel,
        name="sources",
        out_shape=[buffer(COMP * cells)]
        + [buffer(count) for count in (YROWS, YROWS, XROWS, XROWS, ZROWS, ZROWS)]
        + [buffer(cells), buffer(NMET * cells)] + [buffer(cells)] * 4,
        in_specs=[HB] * 9,
        out_specs=[VM] * 13,
        scratch_shapes=[
            pltpu.VMEM((BINS, cells, NZ), BF16),
            pltpu.VMEM((COMP, BINS), BF16),
            pltpu.VMEM((cells, NZ), jnp.int32),
            pltpu.VMEM((COMP * 16, BINS * 16), BF16),
            pltpu.VMEM((24, BINS * 16), F32),
            pltpu.SemaphoreType.DMA((CHUNKS,)),
            pltpu.SemaphoreType.DMA((8,)),
        ],
        compiler_params=pltpu.CompilerParams(vmem_limit_bytes=32 * 1024 * 1024),
    )(
        *(
            pltpu.with_memory_space_constraint(a, pltpu.HBM)
            for a in (
                masses, table.T, star_mask, density, metals, energy, courant_x, courant_y, courant_z
            )
        )
    )
    pairs_xa, pairs_xb, pairs_ya, pairs_yb = swaps()
    ya = swap(ya, pairs_ya)
    yb = swap(yb, pairs_yb)
    xa = swap(xa, pairs_xa)
    xb = swap(xb, pairs_xb)
    za = swap(za, pairs_ya)
    zb = swap(zb, pairs_yb)
    ca, cb = pl.pallas_call(
        corner_kernel,
        name="corners",
        out_shape=[buffer(CROWS), buffer(CROWS)],
        in_specs=[VM] * 4,
        out_specs=[VM, VM],
        compiler_params=pltpu.CompilerParams(vmem_limit_bytes=4 * 1024 * 1024),
    )(*(pltpu.with_memory_space_constraint(a, pltpu.VMEM) for a in (ya, yb, xa, xb)))
    ca = swap(ca, pairs_xa)
    cb = swap(cb, pairs_xb)
    z = pl.pallas_call(
        sort_kernel,
        name="sort",
        out_shape=[buffer(ZROWS), buffer(ZROWS)],
        in_specs=[VM] * 2,
        out_specs=[VM] * 2,
        compiler_params=pltpu.CompilerParams(vmem_limit_bytes=4 * 1024 * 1024),
    )(*(pltpu.with_memory_space_constraint(a, pltpu.VMEM) for a in (za, zb)))
    advected, energy_out = pl.pallas_call(
        finish_kernel,
        name="finish",
        out_shape=[
            jax.ShapeDtypeStruct((NMET * cells, NZ), F32),
            jax.ShapeDtypeStruct((cells, NZ), F32),
        ],
        in_specs=[VM] * 15,
        out_specs=[HB, HB],
        scratch_shapes=[
            pltpu.VMEM((NMET * cells, NZ), F32),
            pltpu.VMEM((cells, NZ), F32),
            pltpu.SemaphoreType.DMA((1 + NMET // GROUP,)),
            pltpu.VMEM((COMP * 8 * PITCH, NZ), F32),
            pltpu.VMEM((10 * DPITCH, NZ), F32),
            pltpu.VMEM((8 * PITCH, NZ), F32),
            pltpu.VMEM((COMP * 8 * BY, NZ), F32),
            pltpu.VMEM((NMET * 8 * PITCH, NZ), F32),
            pltpu.VMEM((2, NMET * BY, NZ), F32),
            pltpu.VMEM((2, NMET * 8, NZ), F32),
            pltpu.VMEM((2, BY, NZ), F32),
            pltpu.VMEM((BX * PITCH, NZ), F32),
        ],
        compiler_params=pltpu.CompilerParams(vmem_limit_bytes=32 * 1024 * 1024),
    )(
        *(
            pltpu.with_memory_space_constraint(a, pltpu.VMEM)
            for a in (src, ya, yb, xa, xb, *z, ca, cb, *local)
        )
    )
    return advected.reshape(NMET, BX, BY, NZ), energy_out.reshape(BX, BY, NZ)


def solution(mesh):
    field = P("gx", "gy", None)
    stack = P(None, "gx", "gy", None)
    in_specs = (stack, P(), field, field, stack, field, field, field, field)
    out_specs = (stack, field)
    return jax.shard_map(body, mesh=mesh, in_specs=in_specs, out_specs=out_specs, check_vma=False)
```

```python
import jax
import jax.numpy as jnp
from jax import lax
from jax.experimental import pallas as pl
from jax.experimental.pallas import tpu as pltpu
from jax.sharding import PartitionSpec as P

F32 = jnp.float32
BF16 = jnp.bfloat16
BINS = 256
COMP = 17
NMET = 16
BX = 4
BY = 8
NZ = 128
CHUNKS = 4
GROUP = 4
YROWS = 112
ZROWS = 114
XROWS = 424
CROWS = 114
PITCH = 24
DENSITIES = [(w, q) for w in range(3) for q in range(3) if w + q < 4]
DPITCH = 40


def rows(start, count, stride=1):
    return pl.ds(start, count) if stride == 1 else pl.ds(start, count, stride)


def place(axis):
    index = lax.axis_index(axis)
    last = index == lax.axis_size(axis) - 1
    odd = index % 2
    alone_a = jnp.logical_and(odd == 0, last)
    alone_b = jnp.logical_or(index == 0, jnp.logical_and(odd == 1, last))
    return 1 - odd, alone_a, alone_b


def sources_kernel(
    masses_hbm, table_hbm, star_hbm, dens_hbm, metals_hbm, energy_hbm, cx_hbm, cy_hbm, cz_hbm,
    src_ref, ya_ref, yb_ref, xa_ref, xb_ref, za_ref, zb_ref,
    dens_ref, metals_ref, energy_ref, cx_ref, cy_ref, cz_ref,
    mass_buf, table_ref, star_ref, expand_ref, wide_ref, mass_sems, sems,
):
    small = [
        (table_hbm, table_ref), (star_hbm, star_ref), (dens_hbm, dens_ref), (metals_hbm, metals_ref),
        (cx_hbm, cx_ref), (cy_hbm, cy_ref), (cz_hbm, cz_ref), (energy_hbm, energy_ref),
    ]
    small_copies = [
        pltpu.make_async_copy(hbm, ref, sems.at[i]) for i, (hbm, ref) in enumerate(small)
    ]
    per = BINS // CHUNKS
    copies = [
        pltpu.make_async_copy(
            masses_hbm.at[pl.ds(c * per, per)], mass_buf.at[pl.ds(c * per, per)], mass_sems.at[c]
        )
        for c in range(CHUNKS)
    ]
    small_copies[0].start()
    for copy in copies:
        copy.start()
    for copy in small_copies[1:]:
        copy.start()

    width = BINS * 16
    group = lax.broadcasted_iota(jnp.int32, (8, NZ), 1) // 16
    same = (
        lax.broadcasted_iota(jnp.int32, (16, NZ), 1) % 16
        == lax.broadcasted_iota(jnp.int32, (16, NZ), 0)
    )
    small_copies[0].wait()
    turned = table_ref[...].astype(F32)
    turned = jnp.concatenate([turned, jnp.zeros((24 - COMP, BINS), F32)], axis=0)
    def expand(c):
        tiles = width // NZ // CHUNKS
        for t in range(c * tiles, (c + 1) * tiles):
            first = 8 * t
            half = first // NZ
            columns = slice(t * NZ, (t + 1) * NZ)
            for r in range(3):
                tile = turned[8 * r : 8 * r + 8, half * NZ : (half + 1) * NZ]
                wide_ref[8 * r : 8 * r + 8, columns] = jnp.take_along_axis(
                    tile, group + first % NZ, axis=1
                )
            for k in range(COMP):
                line = jnp.broadcast_to(wide_ref[k : k + 1, columns], (16, NZ))
                expand_ref[k * 16 : k * 16 + 16, columns] = jnp.where(same, line, 0.0).astype(BF16)

    expand(0)
    total = None
    for c in range(CHUNKS):
        copies[c].wait()
        part = mass_buf[c * per : (c + 1) * per]
        right = jnp.concatenate(
            [part[:, 16 * j : 16 * j + 16].reshape(per * 16, NZ) for j in range(2)], axis=1
        )
        left = expand_ref[:, c * per * 16 : (c + 1) * per * 16]
        prod = jnp.dot(left, right, preferred_element_type=F32)
        total = prod if total is None else total + prod
        if c + 1 < CHUNKS:
            expand(c + 1)
    for copy in small_copies[1:]:
        copy.wait()
    for j in range(2):
        for s in range(2):
            x = 2 * j + s
            mask = star_ref[x * BY : x * BY + BY, :].astype(F32)
            for k in range(COMP):
                at = (k * BX + x) * BY
                piece = total[k * 16 + s * BY : k * 16 + s * BY + BY, j * NZ : (j + 1) * NZ]
                src_ref[at : at + BY, :] = piece * mask

    even_x, alone_xa, alone_xb = place("gx")
    even_y, alone_ya, alone_yb = place("gy")
    plane = BX * BY
    for out, rest, high in ((ya_ref, za_ref, even_y), (yb_ref, zb_ref, 1 - even_y)):
        near = jnp.where(high == 1, BY - 1, 0)
        step = jnp.where(high == 1, -1, 1)
        out[0:64, :] = src_ref[rows(near, 64, BY), :]
        for i, x in enumerate((0, BX - 1)):
            out[64 + 16 * i : 80 + 16 * i, :] = src_ref[rows(x * BY + near + step, 16, plane), :]
        out[96:100, :] = src_ref[rows(NMET * plane + near, 4, BY), :]
        out[100:104, :] = dens_ref[rows(near, 4, BY), :]
        out[104:108, :] = dens_ref[rows(near + step, 4, BY), :]
        out[108:112, :] = dens_ref[rows(near + 2 * step, 4, BY), :]
        rest[0:64, :] = metals_ref[rows(near, 64, BY), :]
        for x in range(1, BX - 1):
            at = 64 + 16 * (x - 1)
            rest[at : at + 16, :] = src_ref[rows(x * BY + near + step, 16, plane), :]
        rest[96:100, :] = cy_ref[rows(near, 4, BY), :]
        rest[100:ZROWS, :] = jnp.zeros((ZROWS - 100, NZ), F32)
    for out, high in ((xa_ref, even_x), (xb_ref, 1 - even_x)):
        near = jnp.where(high == 1, BX - 1, 0) * BY
        step = jnp.where(high == 1, -1, 1) * BY
        tile = 0
        pieces = [(src_ref, k * BX * BY + near) for k in range(COMP)]
        pieces += [(src_ref, k * BX * BY + near + step) for k in range(NMET)]
        pieces += [(metals_ref, k * BX * BY + near) for k in range(NMET)]
        pieces += [(dens_ref, near), (dens_ref, near + step), (dens_ref, near + 2 * step)]
        pieces += [(cx_ref, near)]
        for ref, at in pieces:
            out[tile * BY : tile * BY + BY, :] = ref[pl.ds(pl.multiple_of(at, BY), BY), :]
            tile += 1
    for out, alone in (
        (ya_ref, alone_ya), (yb_ref, alone_yb), (za_ref, alone_ya), (zb_ref, alone_yb),
        (xa_ref, alone_xa), (xb_ref, alone_xb),
    ):
        clear(out, alone)


def clear(ref, alone):
    @pl.when(alone)
    def _():
        ref[...] = jnp.zeros(ref.shape, F32)


def corner_kernel(ya_ref, yb_ref, xa_ref, xb_ref, ca_ref, cb_ref):
    del xa_ref, xb_ref
    even_x, alone_a, alone_b = place("gx")
    for out, high in ((ca_ref, even_x), (cb_ref, 1 - even_x)):
        near = jnp.where(high == 1, BX - 1, 0)
        step = jnp.where(high == 1, -1, 1)
        at = pl.multiple_of(jnp.where(high == 1, 80, 64), 16)
        for side, y_ref in enumerate((ya_ref, yb_ref)):
            base = side * 48
            out[base : base + 16, :] = y_ref[rows(near, 16, BX), :]
            out[base + 16 : base + 32, :] = y_ref[rows(near + step, 16, BX), :]
            out[base + 32 : base + 48, :] = y_ref[pl.ds(at, 16), :]
            base = 96 + side * 9
            out[base : base + 1, :] = y_ref[pl.ds(96 + near, 1), :]
            for i, (w, q) in enumerate(DENSITIES):
                out[base + 1 + i : base + 2 + i, :] = y_ref[pl.ds(100 + 4 * w + near + q * step, 1), :]
    clear(ca_ref, alone_a)
    clear(cb_ref, alone_b)


def sort_kernel(za_ref, zb_ref, zlow_ref, zhigh_ref):
    a_is_high = place("gy")[0] == 1
    a = za_ref[...]
    b = zb_ref[...]
    zlow_ref[...] = jnp.where(a_is_high, b, a)
    zhigh_ref[...] = jnp.where(a_is_high, a, b)


def finish_kernel(
    src_ref, ya_ref, yb_ref, xa_ref, xb_ref, zlow_ref, zhigh_ref, ca_ref, cb_ref,
    dens_ref, metals_ref, energy_ref, cx_ref, cy_ref, cz_ref,
    out_hbm, energy_out_hbm,
    out_ref, energy_out_ref, sems,
    se_ref, de_ref, rw_ref, ys_ref, ee_ref, mx_ref, my_ref, cxl_ref, cye_ref,
):
    even_x = place("gx")[0]
    even_y = place("gy")[0]
    lane = lax.broadcasted_iota(jnp.int32, (1, NZ), 1)
    not_first = lane > 0
    not_last = lane < NZ - 1

    def prev_z(v):
        return pltpu.roll(v, 1, 1)

    def next_z(v):
        return pltpu.roll(v, NZ - 1, 1)

    def masked_prev(v):
        return jnp.where(not_first, prev_z(v), 0.0)

    def masked_next(v):
        return jnp.where(not_last, next_z(v), 0.0)

    de_ref[...] = jnp.zeros(de_ref.shape, F32)

    for x in range(BX):
        at = x * BY
        d_at = (x + 3) * DPITCH + 16
        de_ref[d_at : d_at + BY, :] = dens_ref[at : at + BY, :]
        cye_ref[x * PITCH + 8 : x * PITCH + 16, :] = cy_ref[at : at + BY, :]
        for k in range(COMP):
            s_at = (k * 8 + x + 2) * PITCH + 8
            se_ref[s_at : s_at + BY, :] = src_ref[(k * BX + x) * BY : (k * BX + x + 1) * BY, :]

    for y_ref, high in ((ya_ref, even_y), (yb_ref, 1 - even_y)):
        is_high = high == 1
        r1 = jnp.where(is_high, 16, 7)
        r2 = jnp.where(is_high, 17, 6)
        for k in range(NMET):
            at = k * BX
            base = (k * 8 + 2) * PITCH
            se_ref[rows(base + r1, BX, PITCH), :] = y_ref[at : at + BX, :]
        for i, x in enumerate((0, BX - 1)):
            se_ref[rows((x + 2) * PITCH + r2, NMET, 8 * PITCH), :] = y_ref[64 + 16 * i : 80 + 16 * i, :]
        base = (NMET * 8 + 2) * PITCH
        se_ref[rows(base + r1, BX, PITCH), :] = y_ref[96:100, :]
        for w in range(3):
            d_row = jnp.where(is_high, 24 + w, 15 - w)
            de_ref[rows(3 * DPITCH + d_row, BX, DPITCH), :] = y_ref[100 + 4 * w : 104 + 4 * w, :]
    for side, z_ref in enumerate((zlow_ref, zhigh_ref)):
        for k in range(NMET):
            my_ref[side, k * 8 + 2 : k * 8 + 2 + BX, :] = z_ref[k * BX : k * BX + BX, :]
        for x in range(1, BX - 1):
            r2 = (6, 17)[side]
            se_ref[rows((x + 2) * PITCH + r2, NMET, 8 * PITCH), :] = z_ref[48 + 16 * x : 64 + 16 * x, :]
    cye_ref[rows(7, BX, PITCH), :] = zlow_ref[96:100, :]

    for x_ref, c_ref, high in ((xa_ref, ca_ref, even_x), (xb_ref, cb_ref, 1 - even_x)):
        is_high = high == 1
        p1 = jnp.where(is_high, 6, 1)
        p2 = jnp.where(is_high, 7, 0)
        for k in range(COMP):
            at = pl.multiple_of((k * 8 + p1) * PITCH + 8, 8)
            se_ref[pl.ds(at, BY), :] = x_ref[k * BY : k * BY + BY, :]
        for k in range(NMET):
            at = pl.multiple_of((k * 8 + p2) * PITCH + 8, 8)
            tile = COMP + k
            se_ref[pl.ds(at, BY), :] = x_ref[tile * BY : tile * BY + BY, :]
            tile = COMP + NMET + k
            mx_ref[high, k * BY : k * BY + BY, :] = x_ref[tile * BY : tile * BY + BY, :]
        for w in range(3):
            tile = COMP + 2 * NMET + w
            plane = jnp.where(is_high, 7 + w, 2 - w)
            at = pl.multiple_of(plane * DPITCH + 16, 8)
            de_ref[pl.ds(at, BY), :] = x_ref[tile * BY : tile * BY + BY, :]
        tile = COMP + 2 * NMET + 3
        cxl_ref[high] = x_ref[tile * BY : tile * BY + BY, :]
        for side, y_high in enumerate((even_y, 1 - even_y)):
            base = 48 * side
            y_is_high = y_high == 1
            r1 = jnp.where(y_is_high, 16, 7)
            r2 = jnp.where(y_is_high, 17, 6)
            se_ref[rows(p1 * PITCH + r1, NMET, 8 * PITCH), :] = c_ref[base : base + 16, :]
            se_ref[rows(p2 * PITCH + r1, NMET, 8 * PITCH), :] = c_ref[base + 16 : base + 32, :]
            se_ref[rows(p1 * PITCH + r2, NMET, 8 * PITCH), :] = c_ref[base + 32 : base + 48, :]
            base = 96 + 9 * side
            se_ref[pl.ds((NMET * 8 + p1) * PITCH + r1, 1), :] = c_ref[base : base + 1, :]
            for i, (w, q) in enumerate(DENSITIES):
                d_row = jnp.where(y_is_high, 24 + w, 15 - w)
                plane = jnp.where(is_high, 7 + q, 2 - q)
                de_ref[pl.ds(plane * DPITCH + d_row, 1), :] = c_ref[base + 1 + i : base + 2 + i, :]

    columns = []
    for p in range(10):
        at = p * DPITCH + 8
        columns.append(
            de_ref[at - 1 : at + 23, :] + de_ref[at : at + 24, :] + de_ref[at + 1 : at + 25, :]
        )
    for p in range(8):
        flat = columns[p] + columns[p + 1] + columns[p + 2]
        weight = flat + masked_prev(flat) + masked_next(flat)
        inside = weight > 0.0
        rw_ref[p * PITCH : (p + 1) * PITCH, :] = jnp.where(
            inside, 1.0 / jnp.where(inside, weight, 1.0), 0.0
        )

    copies = []
    for first in range(NMET, -1, -GROUP):
        group = [first] if first == NMET else range(first, first + GROUP)
        share_sums(group, se_ref, rw_ref, ys_ref)
        for k in group:
            for p in range(2, 6) if k == NMET else range(1, 7):
                dens = de_ref[(p + 1) * DPITCH + 16 : (p + 1) * DPITCH + 24, :]
                at = (k * 8 + p) * BY
                flat = (
                    ys_ref[at - BY : at, :] + ys_ref[at : at + BY, :] + ys_ref[at + BY : at + 2 * BY, :]
                )
                collected = flat + masked_prev(flat) + masked_next(flat)
                deposit = dens * collected
                if k == NMET:
                    cell = (p - 2) * BY
                    energy_out_ref[cell : cell + BY, :] = energy_ref[cell : cell + BY, :] + deposit
                    continue
                if p == 1:
                    metal = mx_ref[0, k * BY : k * BY + BY, :]
                elif p == 6:
                    metal = mx_ref[1, k * BY : k * BY + BY, :]
                else:
                    cell = (k * BX + p - 2) * BY
                    metal = metals_ref[cell : cell + BY, :]
                e_at = (k * 8 + p) * PITCH + 8
                ee_ref[e_at : e_at + BY, :] = metal + deposit
        if first == NMET:
            copies.append(pltpu.make_async_copy(energy_out_ref, energy_out_hbm, sems.at[0]))
            copies[-1].start()
            continue

        for side in range(2):
            row = (7, 16)[side]
            dens = de_ref[rows(DPITCH + row + 8, 8, DPITCH), :]
            inv = [rw_ref[rows(row - 1 + d, 8, PITCH), :] for d in range(3)]
            for k in group:
                value = None
                for d in range(3):
                    term = se_ref[rows(k * 8 * PITCH + row - 1 + d, 8, PITCH), :] * inv[d]
                    value = term if value is None else value + term
                flat = value + pltpu.roll(value, 1, 0) + pltpu.roll(value, 7, 0)
                deposit = dens * (flat + masked_prev(flat) + masked_next(flat))
                ee_ref[rows(k * 8 * PITCH + row, 8, PITCH), :] = (
                    my_ref[side, k * 8 : k * 8 + 8, :] + deposit
                )

        for x in range(BX):
            at = x * BY
            cx_up = cx_ref[at : at + BY, :]
            cx_low = cxl_ref[0] if x == 0 else cx_ref[at - BY : at, :]
            cy_up = cy_ref[at : at + BY, :]
            cy_low = cye_ref[x * PITCH + 7 : x * PITCH + 15, :]
            cz_up = cz_ref[at : at + BY, :]
            cz_low = masked_prev(cz_up)
            to_next = [-jnp.minimum(c, 0.0) for c in (cx_up, cy_up, cz_up)]
            from_prev = [jnp.maximum(c, 0.0) for c in (cx_low, cy_low, cz_low)]
            middle = 1.0
            for up, low in ((cx_up, cx_low), (cy_up, cy_low), (cz_up, cz_low)):
                middle = middle - jnp.maximum(up, 0.0) + jnp.minimum(low, 0.0)
            to_next[2] = jnp.where(not_last, to_next[2], 0.0)
            for k in group:
                e_at = (k * 8 + x + 2) * PITCH + 8
                own = ee_ref[e_at : e_at + BY, :]
                result = middle * own
                result = result + to_next[0] * ee_ref[e_at + PITCH : e_at + PITCH + BY, :]
                result = result + from_prev[0] * ee_ref[e_at - PITCH : e_at - PITCH + BY, :]
                result = result + to_next[1] * ee_ref[e_at + 1 : e_at + 1 + BY, :]
                result = result + from_prev[1] * ee_ref[e_at - 1 : e_at - 1 + BY, :]
                result = result + to_next[2] * next_z(own)
                result = result + from_prev[2] * prev_z(own)
                cell = (k * BX + x) * BY
                out_ref[cell : cell + BY, :] = result
        piece = pl.ds(first * BX * BY, GROUP * BX * BY)
        copies.append(
            pltpu.make_async_copy(out_ref.at[piece], out_hbm.at[piece], sems.at[len(copies)])
        )
        copies[-1].start()
    for copy in copies:
        copy.wait()


def share_sums(group, se_ref, rw_ref, ys_ref):
    for p in range(8):
        inv = [rw_ref[p * PITCH + 7 + d : p * PITCH + 15 + d, :] for d in range(3)]
        for k in group:
            if k == NMET and p in (0, 7):
                continue
            at = (k * 8 + p) * PITCH + 7
            value = None
            for d in range(3):
                term = se_ref[at + d : at + d + BY, :] * inv[d]
                value = term if value is None else value + term
            ys_ref[(k * 8 + p) * BY : (k * 8 + p) * BY + BY, :] = value


def swaps():
    nx = lax.axis_size("gx")
    ny = lax.axis_size("gy")
    rounds = []
    for along_x in (True, False):
        for first in (0, 1):
            pairs = []
            for x in range(nx):
                for y in range(ny):
                    place_, count = (x, nx) if along_x else (y, ny)
                    mate = place_ + 1 if place_ % 2 == first else place_ - 1
                    if 0 <= mate < count:
                        to = (mate, y) if along_x else (x, mate)
                    elif along_x and ny % 2 == 0:
                        to = (x, (y + ny // 2) % ny)
                    elif not along_x and nx % 2 == 0:
                        to = (x + 1 - 2 * (x % 2), y)
                    else:
                        to = (x, y)
                    pairs.append((x * ny + y, to[0] * ny + to[1]))
            rounds.append(pairs)
    return rounds


def swap(value, pairs):
    return lax.ppermute(value, ("gx", "gy"), pairs)


VM = pl.BlockSpec(memory_space=pltpu.VMEM)
HB = pl.BlockSpec(memory_space=pltpu.HBM)


def buffer(count):
    return pltpu.VMEM((count, NZ), F32)


def body(masses, table, star_mask, density, metals, energy, courant_x, courant_y, courant_z):
    cells = BX * BY
    masses = masses.reshape(BINS, cells, NZ)
    star_mask, density, energy, courant_x, courant_y, courant_z = (
        a.reshape(cells, NZ) for a in (star_mask, density, energy, courant_x, courant_y, courant_z)
    )
    metals = metals.reshape(NMET * cells, NZ)
    src, ya, yb, xa, xb, za, zb, *local = pl.pallas_call(
        sources_kernel,
        name="sources",
        out_shape=[buffer(COMP * cells)]
        + [buffer(count) for count in (YROWS, YROWS, XROWS, XROWS, ZROWS, ZROWS)]
        + [buffer(cells), buffer(NMET * cells)] + [buffer(cells)] * 4,
        in_specs=[HB] * 9,
        out_specs=[VM] * 13,
        scratch_shapes=[
            pltpu.VMEM((BINS, cells, NZ), BF16),
            pltpu.VMEM((COMP, BINS), BF16),
            pltpu.VMEM((cells, NZ), jnp.int32),
            pltpu.VMEM((COMP * 16, BINS * 16), BF16),
            pltpu.VMEM((24, BINS * 16), F32),
            pltpu.SemaphoreType.DMA((CHUNKS,)),
            pltpu.SemaphoreType.DMA((8,)),
        ],
        compiler_params=pltpu.CompilerParams(vmem_limit_bytes=32 * 1024 * 1024),
    )(
        *(
            pltpu.with_memory_space_constraint(a, pltpu.HBM)
            for a in (
                masses, table.T, star_mask, density, metals, energy, courant_x, courant_y, courant_z
            )
        )
    )
    pairs_xa, pairs_xb, pairs_ya, pairs_yb = swaps()
    ya = swap(ya, pairs_ya)
    yb = swap(yb, pairs_yb)
    xa = swap(xa, pairs_xa)
    xb = swap(xb, pairs_xb)
    za = swap(za, pairs_ya)
    zb = swap(zb, pairs_yb)
    ca, cb = pl.pallas_call(
        corner_kernel,
        name="corners",
        out_shape=[buffer(CROWS), buffer(CROWS)],
        in_specs=[VM] * 4,
        out_specs=[VM, VM],
        compiler_params=pltpu.CompilerParams(vmem_limit_bytes=4 * 1024 * 1024),
    )(*(pltpu.with_memory_space_constraint(a, pltpu.VMEM) for a in (ya, yb, xa, xb)))
    ca = swap(ca, pairs_xa)
    cb = swap(cb, pairs_xb)
    z = pl.pallas_call(
        sort_kernel,
        name="sort",
        out_shape=[buffer(ZROWS), buffer(ZROWS)],
        in_specs=[VM] * 2,
        out_specs=[VM] * 2,
        compiler_params=pltpu.CompilerParams(vmem_limit_bytes=4 * 1024 * 1024),
    )(*(pltpu.with_memory_space_constraint(a, pltpu.VMEM) for a in (za, zb)))
    advected, energy_out = pl.pallas_call(
        finish_kernel,
        name="finish",
        out_shape=[
            jax.ShapeDtypeStruct((NMET * cells, NZ), F32),
            jax.ShapeDtypeStruct((cells, NZ), F32),
        ],
        in_specs=[VM] * 15,
        out_specs=[HB, HB],
        scratch_shapes=[
            pltpu.VMEM((NMET * cells, NZ), F32),
            pltpu.VMEM((cells, NZ), F32),
            pltpu.SemaphoreType.DMA((1 + NMET // GROUP,)),
            pltpu.VMEM((COMP * 8 * PITCH, NZ), F32),
            pltpu.VMEM((10 * DPITCH, NZ), F32),
            pltpu.VMEM((8 * PITCH, NZ), F32),
            pltpu.VMEM((COMP * 8 * BY, NZ), F32),
            pltpu.VMEM((NMET * 8 * PITCH, NZ), F32),
            pltpu.VMEM((2, NMET * BY, NZ), F32),
            pltpu.VMEM((2, NMET * 8, NZ), F32),
            pltpu.VMEM((2, BY, NZ), F32),
            pltpu.VMEM((BX * PITCH, NZ), F32),
        ],
        compiler_params=pltpu.CompilerParams(vmem_limit_bytes=32 * 1024 * 1024),
    )(
        *(
            pltpu.with_memory_space_constraint(a, pltpu.VMEM)
            for a in (src, ya, yb, xa, xb, *z, ca, cb, *local)
        )
    )
    return advected.reshape(NMET, BX, BY, NZ), energy_out.reshape(BX, BY, NZ)


def solution(mesh):
    field = P("gx", "gy", None)
    stack = P(None, "gx", "gy", None)
    in_specs = (stack, P(), field, field, stack, field, field, field, field)
    out_specs = (stack, field)
    return jax.shard_map(body, mesh=mesh, in_specs=in_specs, out_specs=out_specs, check_vma=False)
```

```python
import jax
import jax.numpy as jnp
from jax import lax
from jax.experimental import pallas as pl
from jax.experimental.pallas import tpu as pltpu
from jax.sharding import PartitionSpec as P

F32 = jnp.float32
BF16 = jnp.bfloat16
BINS = 256
COMP = 17
NMET = 16
BX = 4
BY = 8
NZ = 128
PIECES = 16
GROUPS = (5, 5, 4, 2)
GROUP = 4
YROWS = 112
ZROWS = 114
XROWS = 424
CROWS = 114
PITCH = 24
DENSITIES = [(w, q) for w in range(3) for q in range(3) if w + q < 4]
DPITCH = 40


def rows(start, count, stride=1):
    return pl.ds(start, count) if stride == 1 else pl.ds(start, count, stride)


def place(axis):
    index = lax.axis_index(axis)
    last = index == lax.axis_size(axis) - 1
    odd = index % 2
    alone_a = jnp.logical_and(odd == 0, last)
    alone_b = jnp.logical_or(index == 0, jnp.logical_and(odd == 1, last))
    return 1 - odd, alone_a, alone_b


def sources_kernel(
    masses_hbm, table_hbm, star_hbm, dens_hbm, metals_hbm, energy_hbm, cx_hbm, cy_hbm, cz_hbm,
    src_ref, ya_ref, yb_ref, xa_ref, xb_ref, za_ref, zb_ref,
    dens_ref, metals_ref, energy_ref, cx_ref, cy_ref, cz_ref,
    mass_buf, table_ref, star_ref, expand_ref, wide_ref, mass_sems, sems,
):
    small = [
        (table_hbm, table_ref), (star_hbm, star_ref), (dens_hbm, dens_ref), (metals_hbm, metals_ref),
        (cx_hbm, cx_ref), (cy_hbm, cy_ref), (cz_hbm, cz_ref), (energy_hbm, energy_ref),
    ]
    small_copies = [
        pltpu.make_async_copy(hbm, ref, sems.at[i]) for i, (hbm, ref) in enumerate(small)
    ]
    per = BINS // PIECES
    copies = [
        pltpu.make_async_copy(
            masses_hbm.at[pl.ds(c * per, per)], mass_buf.at[pl.ds(c * per, per)], mass_sems.at[c]
        )
        for c in range(PIECES)
    ]
    small_copies[0].start()
    for copy in copies:
        copy.start()
    for copy in small_copies[1:]:
        copy.start()

    width = BINS * 16
    group = lax.broadcasted_iota(jnp.int32, (8, NZ), 1) // 16
    same = (
        lax.broadcasted_iota(jnp.int32, (16, NZ), 1) % 16
        == lax.broadcasted_iota(jnp.int32, (16, NZ), 0)
    )
    small_copies[0].wait()
    turned = table_ref[...].astype(F32)
    turned = jnp.concatenate([turned, jnp.zeros((24 - COMP, BINS), F32)], axis=0)
    def expand(begin, end):
        tiles = width // NZ // PIECES
        for t in range(begin * tiles, end * tiles):
            first = 8 * t
            half = first // NZ
            columns = slice(t * NZ, (t + 1) * NZ)
            for r in range(3):
                tile = turned[8 * r : 8 * r + 8, half * NZ : (half + 1) * NZ]
                wide_ref[8 * r : 8 * r + 8, columns] = jnp.take_along_axis(
                    tile, group + first % NZ, axis=1
                )
            for k in range(COMP):
                line = jnp.broadcast_to(wide_ref[k : k + 1, columns], (16, NZ))
                expand_ref[k * 16 : k * 16 + 16, columns] = jnp.where(same, line, 0.0).astype(BF16)

    total = None
    begin = 0
    expand(0, GROUPS[0])
    for i, count in enumerate(GROUPS):
        end = begin + count
        for copy in copies[begin:end]:
            copy.wait()
        part = mass_buf[begin * per : end * per]
        right = jnp.concatenate(
            [part[:, 16 * j : 16 * j + 16].reshape(count * per * 16, NZ) for j in range(2)], axis=1
        )
        left = expand_ref[:, begin * per * 16 : end * per * 16]
        prod = jnp.dot(left, right, preferred_element_type=F32)
        total = prod if total is None else total + prod
        if i + 1 < len(GROUPS):
            expand(end, end + GROUPS[i + 1])
        begin = end
    for copy in small_copies[1:]:
        copy.wait()
    for j in range(2):
        for s in range(2):
            x = 2 * j + s
            mask = star_ref[x * BY : x * BY + BY, :].astype(F32)
            for k in range(COMP):
                at = (k * BX + x) * BY
                piece = total[k * 16 + s * BY : k * 16 + s * BY + BY, j * NZ : (j + 1) * NZ]
                src_ref[at : at + BY, :] = piece * mask

    even_x, alone_xa, alone_xb = place("gx")
    even_y, alone_ya, alone_yb = place("gy")
    plane = BX * BY
    for out, rest, high in ((ya_ref, za_ref, even_y), (yb_ref, zb_ref, 1 - even_y)):
        near = jnp.where(high == 1, BY - 1, 0)
        step = jnp.where(high == 1, -1, 1)
        out[0:64, :] = src_ref[rows(near, 64, BY), :]
        for i, x in enumerate((0, BX - 1)):
            out[64 + 16 * i : 80 + 16 * i, :] = src_ref[rows(x * BY + near + step, 16, plane), :]
        out[96:100, :] = src_ref[rows(NMET * plane + near, 4, BY), :]
        out[100:104, :] = dens_ref[rows(near, 4, BY), :]
        out[104:108, :] = dens_ref[rows(near + step, 4, BY), :]
        out[108:112, :] = dens_ref[rows(near + 2 * step, 4, BY), :]
        rest[0:64, :] = metals_ref[rows(near, 64, BY), :]
        for x in range(1, BX - 1):
            at = 64 + 16 * (x - 1)
            rest[at : at + 16, :] = src_ref[rows(x * BY + near + step, 16, plane), :]
        rest[96:100, :] = cy_ref[rows(near, 4, BY), :]
        rest[100:ZROWS, :] = jnp.zeros((ZROWS - 100, NZ), F32)
    for out, high in ((xa_ref, even_x), (xb_ref, 1 - even_x)):
        near = jnp.where(high == 1, BX - 1, 0) * BY
        step = jnp.where(high == 1, -1, 1) * BY
        tile = 0
        pieces = [(src_ref, k * BX * BY + near) for k in range(COMP)]
        pieces += [(src_ref, k * BX * BY + near + step) for k in range(NMET)]
        pieces += [(metals_ref, k * BX * BY + near) for k in range(NMET)]
        pieces += [(dens_ref, near), (dens_ref, near + step), (dens_ref, near + 2 * step)]
        pieces += [(cx_ref, near)]
        for ref, at in pieces:
            out[tile * BY : tile * BY + BY, :] = ref[pl.ds(pl.multiple_of(at, BY), BY), :]
            tile += 1
    for out, alone in (
        (ya_ref, alone_ya), (yb_ref, alone_yb), (za_ref, alone_ya), (zb_ref, alone_yb),
        (xa_ref, alone_xa), (xb_ref, alone_xb),
    ):
        clear(out, alone)


def clear(ref, alone):
    @pl.when(alone)
    def _():
        ref[...] = jnp.zeros(ref.shape, F32)


def corner_kernel(ya_ref, yb_ref, xa_ref, xb_ref, ca_ref, cb_ref):
    del xa_ref, xb_ref
    even_x, alone_a, alone_b = place("gx")
    for out, high in ((ca_ref, even_x), (cb_ref, 1 - even_x)):
        near = jnp.where(high == 1, BX - 1, 0)
        step = jnp.where(high == 1, -1, 1)
        at = pl.multiple_of(jnp.where(high == 1, 80, 64), 16)
        for side, y_ref in enumerate((ya_ref, yb_ref)):
            base = side * 48
            out[base : base + 16, :] = y_ref[rows(near, 16, BX), :]
            out[base + 16 : base + 32, :] = y_ref[rows(near + step, 16, BX), :]
            out[base + 32 : base + 48, :] = y_ref[pl.ds(at, 16), :]
            base = 96 + side * 9
            out[base : base + 1, :] = y_ref[pl.ds(96 + near, 1), :]
            for i, (w, q) in enumerate(DENSITIES):
                out[base + 1 + i : base + 2 + i, :] = y_ref[pl.ds(100 + 4 * w + near + q * step, 1), :]
    clear(ca_ref, alone_a)
    clear(cb_ref, alone_b)


def sort_kernel(za_ref, zb_ref, zlow_ref, zhigh_ref):
    a_is_high = place("gy")[0] == 1
    a = za_ref[...]
    b = zb_ref[...]
    zlow_ref[...] = jnp.where(a_is_high, b, a)
    zhigh_ref[...] = jnp.where(a_is_high, a, b)


def finish_kernel(
    src_ref, ya_ref, yb_ref, xa_ref, xb_ref, zlow_ref, zhigh_ref, ca_ref, cb_ref,
    dens_ref, metals_ref, energy_ref, cx_ref, cy_ref, cz_ref,
    out_hbm, energy_out_hbm,
    out_ref, energy_out_ref, sems,
    se_ref, de_ref, rw_ref, ys_ref, ee_ref, mx_ref, my_ref, cxl_ref, cye_ref,
):
    even_x = place("gx")[0]
    even_y = place("gy")[0]
    lane = lax.broadcasted_iota(jnp.int32, (1, NZ), 1)
    not_first = lane > 0
    not_last = lane < NZ - 1

    def prev_z(v):
        return pltpu.roll(v, 1, 1)

    def next_z(v):
        return pltpu.roll(v, NZ - 1, 1)

    def masked_prev(v):
        return jnp.where(not_first, prev_z(v), 0.0)

    def masked_next(v):
        return jnp.where(not_last, next_z(v), 0.0)

    de_ref[...] = jnp.zeros(de_ref.shape, F32)

    for x in range(BX):
        at = x * BY
        d_at = (x + 3) * DPITCH + 16
        de_ref[d_at : d_at + BY, :] = dens_ref[at : at + BY, :]
        cye_ref[x * PITCH + 8 : x * PITCH + 16, :] = cy_ref[at : at + BY, :]
        for k in range(COMP):
            s_at = (k * 8 + x + 2) * PITCH + 8
            se_ref[s_at : s_at + BY, :] = src_ref[(k * BX + x) * BY : (k * BX + x + 1) * BY, :]

    for y_ref, high in ((ya_ref, even_y), (yb_ref, 1 - even_y)):
        is_high = high == 1
        r1 = jnp.where(is_high, 16, 7)
        r2 = jnp.where(is_high, 17, 6)
        for k in range(NMET):
            at = k * BX
            base = (k * 8 + 2) * PITCH
            se_ref[rows(base + r1, BX, PITCH), :] = y_ref[at : at + BX, :]
        for i, x in enumerate((0, BX - 1)):
            se_ref[rows((x + 2) * PITCH + r2, NMET, 8 * PITCH), :] = y_ref[64 + 16 * i : 80 + 16 * i, :]
        base = (NMET * 8 + 2) * PITCH
        se_ref[rows(base + r1, BX, PITCH), :] = y_ref[96:100, :]
        for w in range(3):
            d_row = jnp.where(is_high, 24 + w, 15 - w)
            de_ref[rows(3 * DPITCH + d_row, BX, DPITCH), :] = y_ref[100 + 4 * w : 104 + 4 * w, :]
    for side, z_ref in enumerate((zlow_ref, zhigh_ref)):
        for k in range(NMET):
            my_ref[side, k * 8 + 2 : k * 8 + 2 + BX, :] = z_ref[k * BX : k * BX + BX, :]
        for x in range(1, BX - 1):
            r2 = (6, 17)[side]
            se_ref[rows((x + 2) * PITCH + r2, NMET, 8 * PITCH), :] = z_ref[48 + 16 * x : 64 + 16 * x, :]
    cye_ref[rows(7, BX, PITCH), :] = zlow_ref[96:100, :]

    for x_ref, c_ref, high in ((xa_ref, ca_ref, even_x), (xb_ref, cb_ref, 1 - even_x)):
        is_high = high == 1
        p1 = jnp.where(is_high, 6, 1)
        p2 = jnp.where(is_high, 7, 0)
        for k in range(COMP):
            at = pl.multiple_of((k * 8 + p1) * PITCH + 8, 8)
            se_ref[pl.ds(at, BY), :] = x_ref[k * BY : k * BY + BY, :]
        for k in range(NMET):
            at = pl.multiple_of((k * 8 + p2) * PITCH + 8, 8)
            tile = COMP + k
            se_ref[pl.ds(at, BY), :] = x_ref[tile * BY : tile * BY + BY, :]
            tile = COMP + NMET + k
            mx_ref[high, k * BY : k * BY + BY, :] = x_ref[tile * BY : tile * BY + BY, :]
        for w in range(3):
            tile = COMP + 2 * NMET + w
            plane = jnp.where(is_high, 7 + w, 2 - w)
            at = pl.multiple_of(plane * DPITCH + 16, 8)
            de_ref[pl.ds(at, BY), :] = x_ref[tile * BY : tile * BY + BY, :]
        tile = COMP + 2 * NMET + 3
        cxl_ref[high] = x_ref[tile * BY : tile * BY + BY, :]
        for side, y_high in enumerate((even_y, 1 - even_y)):
            base = 48 * side
            y_is_high = y_high == 1
            r1 = jnp.where(y_is_high, 16, 7)
            r2 = jnp.where(y_is_high, 17, 6)
            se_ref[rows(p1 * PITCH + r1, NMET, 8 * PITCH), :] = c_ref[base : base + 16, :]
            se_ref[rows(p2 * PITCH + r1, NMET, 8 * PITCH), :] = c_ref[base + 16 : base + 32, :]
            se_ref[rows(p1 * PITCH + r2, NMET, 8 * PITCH), :] = c_ref[base + 32 : base + 48, :]
            base = 96 + 9 * side
            se_ref[pl.ds((NMET * 8 + p1) * PITCH + r1, 1), :] = c_ref[base : base + 1, :]
            for i, (w, q) in enumerate(DENSITIES):
                d_row = jnp.where(y_is_high, 24 + w, 15 - w)
                plane = jnp.where(is_high, 7 + q, 2 - q)
                de_ref[pl.ds(plane * DPITCH + d_row, 1), :] = c_ref[base + 1 + i : base + 2 + i, :]

    columns = []
    for p in range(10):
        at = p * DPITCH + 8
        columns.append(
            de_ref[at - 1 : at + 23, :] + de_ref[at : at + 24, :] + de_ref[at + 1 : at + 25, :]
        )
    for p in range(8):
        flat = columns[p] + columns[p + 1] + columns[p + 2]
        weight = flat + masked_prev(flat) + masked_next(flat)
        inside = weight > 0.0
        rw_ref[p * PITCH : (p + 1) * PITCH, :] = jnp.where(
            inside, 1.0 / jnp.where(inside, weight, 1.0), 0.0
        )

    copies = []
    for first in range(NMET, -1, -GROUP):
        group = [first] if first == NMET else range(first, first + GROUP)
        share_sums(group, se_ref, rw_ref, ys_ref)
        for k in group:
            for p in range(2, 6) if k == NMET else range(1, 7):
                dens = de_ref[(p + 1) * DPITCH + 16 : (p + 1) * DPITCH + 24, :]
                at = (k * 8 + p) * BY
                flat = (
                    ys_ref[at - BY : at, :] + ys_ref[at : at + BY, :] + ys_ref[at + BY : at + 2 * BY, :]
                )
                collected = flat + masked_prev(flat) + masked_next(flat)
                deposit = dens * collected
                if k == NMET:
                    cell = (p - 2) * BY
                    energy_out_ref[cell : cell + BY, :] = energy_ref[cell : cell + BY, :] + deposit
                    continue
                if p == 1:
                    metal = mx_ref[0, k * BY : k * BY + BY, :]
                elif p == 6:
                    metal = mx_ref[1, k * BY : k * BY + BY, :]
                else:
                    cell = (k * BX + p - 2) * BY
                    metal = metals_ref[cell : cell + BY, :]
                e_at = (k * 8 + p) * PITCH + 8
                ee_ref[e_at : e_at + BY, :] = metal + deposit
        if first == NMET:
            copies.append(pltpu.make_async_copy(energy_out_ref, energy_out_hbm, sems.at[0]))
            copies[-1].start()
            continue

        for side in range(2):
            row = (7, 16)[side]
            dens = de_ref[rows(DPITCH + row + 8, 8, DPITCH), :]
            inv = [rw_ref[rows(row - 1 + d, 8, PITCH), :] for d in range(3)]
            for k in group:
                value = None
                for d in range(3):
                    term = se_ref[rows(k * 8 * PITCH + row - 1 + d, 8, PITCH), :] * inv[d]
                    value = term if value is None else value + term
                flat = value + pltpu.roll(value, 1, 0) + pltpu.roll(value, 7, 0)
                deposit = dens * (flat + masked_prev(flat) + masked_next(flat))
                ee_ref[rows(k * 8 * PITCH + row, 8, PITCH), :] = (
                    my_ref[side, k * 8 : k * 8 + 8, :] + deposit
                )

        for x in range(BX):
            at = x * BY
            cx_up = cx_ref[at : at + BY, :]
            cx_low = cxl_ref[0] if x == 0 else cx_ref[at - BY : at, :]
            cy_up = cy_ref[at : at + BY, :]
            cy_low = cye_ref[x * PITCH + 7 : x * PITCH + 15, :]
            cz_up = cz_ref[at : at + BY, :]
            cz_low = masked_prev(cz_up)
            to_next = [-jnp.minimum(c, 0.0) for c in (cx_up, cy_up, cz_up)]
            from_prev = [jnp.maximum(c, 0.0) for c in (cx_low, cy_low, cz_low)]
            middle = 1.0
            for up, low in ((cx_up, cx_low), (cy_up, cy_low), (cz_up, cz_low)):
                middle = middle - jnp.maximum(up, 0.0) + jnp.minimum(low, 0.0)
            to_next[2] = jnp.where(not_last, to_next[2], 0.0)
            for k in group:
                e_at = (k * 8 + x + 2) * PITCH + 8
                own = ee_ref[e_at : e_at + BY, :]
                result = middle * own
                result = result + to_next[0] * ee_ref[e_at + PITCH : e_at + PITCH + BY, :]
                result = result + from_prev[0] * ee_ref[e_at - PITCH : e_at - PITCH + BY, :]
                result = result + to_next[1] * ee_ref[e_at + 1 : e_at + 1 + BY, :]
                result = result + from_prev[1] * ee_ref[e_at - 1 : e_at - 1 + BY, :]
                result = result + to_next[2] * next_z(own)
                result = result + from_prev[2] * prev_z(own)
                cell = (k * BX + x) * BY
                out_ref[cell : cell + BY, :] = result
        piece = pl.ds(first * BX * BY, GROUP * BX * BY)
        copies.append(
            pltpu.make_async_copy(out_ref.at[piece], out_hbm.at[piece], sems.at[len(copies)])
        )
        copies[-1].start()
    for copy in copies:
        copy.wait()


def share_sums(group, se_ref, rw_ref, ys_ref):
    for p in range(8):
        inv = [rw_ref[p * PITCH + 7 + d : p * PITCH + 15 + d, :] for d in range(3)]
        for k in group:
            if k == NMET and p in (0, 7):
                continue
            at = (k * 8 + p) * PITCH + 7
            value = None
            for d in range(3):
                term = se_ref[at + d : at + d + BY, :] * inv[d]
                value = term if value is None else value + term
            ys_ref[(k * 8 + p) * BY : (k * 8 + p) * BY + BY, :] = value


def swaps():
    nx = lax.axis_size("gx")
    ny = lax.axis_size("gy")
    rounds = []
    for along_x, mirrored in ((True, False), (True, True), (False, False)):
        for first in (1,) if mirrored else (0, 1):
            pairs = []
            for x in range(nx):
                for y in range(ny):
                    place_, count = (x, nx) if along_x else (y, ny)
                    mate = place_ + 1 if place_ % 2 == first else place_ - 1
                    if 0 <= mate < count:
                        to = (mate, y) if along_x else (x, mate)
                    elif mirrored:
                        to = (x, ny - 1 - y)
                    elif along_x and ny % 2 == 0:
                        to = (x, (y + ny // 2) % ny)
                    elif not along_x and nx % 2 == 0:
                        to = (x + 1 - 2 * (x % 2), y)
                    else:
                        to = (x, y)
                    pairs.append((x * ny + y, to[0] * ny + to[1]))
            rounds.append(pairs)
    return rounds


def swap(value, pairs):
    return lax.ppermute(value, ("gx", "gy"), pairs)


VM = pl.BlockSpec(memory_space=pltpu.VMEM)
HB = pl.BlockSpec(memory_space=pltpu.HBM)


def buffer(count):
    return pltpu.VMEM((count, NZ), F32)


def body(masses, table, star_mask, density, metals, energy, courant_x, courant_y, courant_z):
    cells = BX * BY
    masses = masses.reshape(BINS, cells, NZ)
    star_mask, density, energy, courant_x, courant_y, courant_z = (
        a.reshape(cells, NZ) for a in (star_mask, density, energy, courant_x, courant_y, courant_z)
    )
    metals = metals.reshape(NMET * cells, NZ)
    src, ya, yb, xa, xb, za, zb, *local = pl.pallas_call(
        sources_kernel,
        name="sources",
        out_shape=[buffer(COMP * cells)]
        + [buffer(count) for count in (YROWS, YROWS, XROWS, XROWS, ZROWS, ZROWS)]
        + [buffer(cells), buffer(NMET * cells)] + [buffer(cells)] * 4,
        in_specs=[HB] * 9,
        out_specs=[VM] * 13,
        scratch_shapes=[
            pltpu.VMEM((BINS, cells, NZ), BF16),
            pltpu.VMEM((COMP, BINS), BF16),
            pltpu.VMEM((cells, NZ), jnp.int32),
            pltpu.VMEM((COMP * 16, BINS * 16), BF16),
            pltpu.VMEM((24, BINS * 16), F32),
            pltpu.SemaphoreType.DMA((PIECES,)),
            pltpu.SemaphoreType.DMA((8,)),
        ],
        compiler_params=pltpu.CompilerParams(vmem_limit_bytes=32 * 1024 * 1024),
    )(
        *(
            pltpu.with_memory_space_constraint(a, pltpu.HBM)
            for a in (
                masses, table.T, star_mask, density, metals, energy, courant_x, courant_y, courant_z
            )
        )
    )
    pairs_xa, pairs_xb, pairs_corner_b, pairs_ya, pairs_yb = swaps()
    ya = swap(ya, pairs_ya)
    yb = swap(yb, pairs_yb)
    xa = swap(xa, pairs_xa)
    xb = swap(xb, pairs_xb)
    za = swap(za, pairs_ya)
    zb = swap(zb, pairs_yb)
    ca, cb = pl.pallas_call(
        corner_kernel,
        name="corners",
        out_shape=[buffer(CROWS), buffer(CROWS)],
        in_specs=[VM] * 4,
        out_specs=[VM, VM],
        compiler_params=pltpu.CompilerParams(vmem_limit_bytes=4 * 1024 * 1024),
    )(*(pltpu.with_memory_space_constraint(a, pltpu.VMEM) for a in (ya, yb, xa, xb)))
    ca = swap(ca, pairs_xa)
    cb = swap(cb, pairs_corner_b)
    z = pl.pallas_call(
        sort_kernel,
        name="sort",
        out_shape=[buffer(ZROWS), buffer(ZROWS)],
        in_specs=[VM] * 2,
        out_specs=[VM] * 2,
        compiler_params=pltpu.CompilerParams(vmem_limit_bytes=4 * 1024 * 1024),
    )(*(pltpu.with_memory_space_constraint(a, pltpu.VMEM) for a in (za, zb)))
    advected, energy_out = pl.pallas_call(
        finish_kernel,
        name="finish",
        out_shape=[
            jax.ShapeDtypeStruct((NMET * cells, NZ), F32),
            jax.ShapeDtypeStruct((cells, NZ), F32),
        ],
        in_specs=[VM] * 15,
        out_specs=[HB, HB],
        scratch_shapes=[
            pltpu.VMEM((NMET * cells, NZ), F32),
            pltpu.VMEM((cells, NZ), F32),
            pltpu.SemaphoreType.DMA((1 + NMET // GROUP,)),
            pltpu.VMEM((COMP * 8 * PITCH, NZ), F32),
            pltpu.VMEM((10 * DPITCH, NZ), F32),
            pltpu.VMEM((8 * PITCH, NZ), F32),
            pltpu.VMEM((COMP * 8 * BY, NZ), F32),
            pltpu.VMEM((NMET * 8 * PITCH, NZ), F32),
            pltpu.VMEM((2, NMET * BY, NZ), F32),
            pltpu.VMEM((2, NMET * 8, NZ), F32),
            pltpu.VMEM((2, BY, NZ), F32),
            pltpu.VMEM((BX * PITCH, NZ), F32),
        ],
        compiler_params=pltpu.CompilerParams(vmem_limit_bytes=32 * 1024 * 1024),
    )(
        *(
            pltpu.with_memory_space_constraint(a, pltpu.VMEM)
            for a in (src, ya, yb, xa, xb, *z, ca, cb, *local)
        )
    )
    return advected.reshape(NMET, BX, BY, NZ), energy_out.reshape(BX, BY, NZ)


def solution(mesh):
    field = P("gx", "gy", None)
    stack = P(None, "gx", "gy", None)
    in_specs = (stack, P(), field, field, stack, field, field, field, field)
    out_specs = (stack, field)
    return jax.shard_map(body, mesh=mesh, in_specs=in_specs, out_specs=out_specs, check_vma=False)
```

```python
import jax
import jax.numpy as jnp
from jax import lax
from jax.experimental import pallas as pl
from jax.experimental.pallas import tpu as pltpu
from jax.sharding import PartitionSpec as P

F32 = jnp.float32
BF16 = jnp.bfloat16
BINS = 256
COMP = 17
NMET = 16
BX = 4
BY = 8
NZ = 128
CHUNKS = 4
GROUP = 4
YROWS = 112
ZROWS = 114
XROWS = 424
CROWS = 114
PITCH = 24
DENSITIES = [(w, q) for w in range(3) for q in range(3) if w + q < 4]
DPITCH = 40


def rows(start, count, stride=1):
    return pl.ds(start, count) if stride == 1 else pl.ds(start, count, stride)


def place(axis):
    index = lax.axis_index(axis)
    last = index == lax.axis_size(axis) - 1
    odd = index % 2
    alone_a = jnp.logical_and(odd == 0, last)
    alone_b = jnp.logical_or(index == 0, jnp.logical_and(odd == 1, last))
    return 1 - odd, alone_a, alone_b


def sources_kernel(
    masses_hbm, table_hbm, star_hbm, dens_hbm, metals_hbm, energy_hbm, cx_hbm, cy_hbm, cz_hbm,
    src_ref, ya_ref, yb_ref, xa_ref, xb_ref, za_ref, zb_ref,
    dens_ref, metals_ref, energy_ref, cx_ref, cy_ref, cz_ref,
    mass_buf, table_ref, star_ref, expand_ref, wide_ref, mass_sems, sems,
):
    small = [
        (table_hbm, table_ref), (star_hbm, star_ref), (dens_hbm, dens_ref), (metals_hbm, metals_ref),
        (cx_hbm, cx_ref), (cy_hbm, cy_ref), (cz_hbm, cz_ref), (energy_hbm, energy_ref),
    ]
    small_copies = [
        pltpu.make_async_copy(hbm, ref, sems.at[i]) for i, (hbm, ref) in enumerate(small)
    ]
    per = BINS // CHUNKS
    copies = [
        pltpu.make_async_copy(
            masses_hbm.at[pl.ds(c * per, per)], mass_buf.at[pl.ds(c * per, per)], mass_sems.at[c]
        )
        for c in range(CHUNKS)
    ]
    small_copies[0].start()
    for copy in copies:
        copy.start()
    for copy in small_copies[1:]:
        copy.start()

    width = BINS * BY
    group = lax.broadcasted_iota(jnp.int32, (8, NZ), 1) // BY
    same = (
        lax.broadcasted_iota(jnp.int32, (BY, NZ), 1) % BY
        == lax.broadcasted_iota(jnp.int32, (BY, NZ), 0)
    )
    upper = lax.broadcasted_iota(jnp.int32, (1, 16, NZ), 1) < BY
    small_copies[0].wait()
    turned = table_ref[...].astype(F32)
    turned = jnp.concatenate([turned, jnp.zeros((24 - COMP, BINS), F32)], axis=0)

    def expand(c):
        tiles = width // NZ // CHUNKS
        for t in range(c * tiles, (c + 1) * tiles):
            first = 16 * t
            half = first // NZ
            columns = slice(t * NZ, (t + 1) * NZ)
            for r in range(3):
                tile = turned[8 * r : 8 * r + 8, half * NZ : (half + 1) * NZ]
                wide_ref[8 * r : 8 * r + 8, columns] = jnp.take_along_axis(
                    tile, group + first % NZ, axis=1
                )
            for k in range(0, COMP + 1, 2):
                lines = [
                    jnp.where(same, jnp.broadcast_to(wide_ref[i : i + 1, columns], (BY, NZ)), 0.0)
                    for i in (k, k + 1)
                ]
                expand_ref[k * BY : k * BY + 16, columns] = jnp.concatenate(lines, axis=0).astype(BF16)

    expand(0)
    total = None
    for c in range(CHUNKS):
        copies[c].wait()
        part = mass_buf[c * per : (c + 1) * per]
        blocks = []
        for j in range(2):
            both = part[:, 16 * j : 16 * j + 16].reshape(per // 2, 2, 16, NZ)
            even, odd = both[:, 0], both[:, 1]
            blocks.append(jnp.where(upper, even, pltpu.roll(odd, 8, 1)).reshape(per * BY, NZ))
            blocks.append(jnp.where(upper, pltpu.roll(even, 8, 1), odd).reshape(per * BY, NZ))
        right = jnp.concatenate(blocks, axis=1)
        left = expand_ref[:, c * per * BY : (c + 1) * per * BY]
        prod = jnp.dot(left, right, preferred_element_type=F32)
        total = prod if total is None else total + prod
        if c + 1 < CHUNKS:
            expand(c + 1)
    for copy in small_copies[1:]:
        copy.wait()
    for x in range(BX):
        mask = star_ref[x * BY : x * BY + BY, :].astype(F32)
        for k in range(COMP):
            at = (k * BX + x) * BY
            piece = total[k * BY : k * BY + BY, x * NZ : (x + 1) * NZ]
            src_ref[at : at + BY, :] = piece * mask

    even_x, alone_xa, alone_xb = place("gx")
    even_y, alone_ya, alone_yb = place("gy")
    plane = BX * BY
    for out, rest, high in ((ya_ref, za_ref, even_y), (yb_ref, zb_ref, 1 - even_y)):
        near = jnp.where(high == 1, BY - 1, 0)
        step = jnp.where(high == 1, -1, 1)
        out[0:64, :] = src_ref[rows(near, 64, BY), :]
        for i, x in enumerate((0, BX - 1)):
            out[64 + 16 * i : 80 + 16 * i, :] = src_ref[rows(x * BY + near + step, 16, plane), :]
        out[96:100, :] = src_ref[rows(NMET * plane + near, 4, BY), :]
        out[100:104, :] = dens_ref[rows(near, 4, BY), :]
        out[104:108, :] = dens_ref[rows(near + step, 4, BY), :]
        out[108:112, :] = dens_ref[rows(near + 2 * step, 4, BY), :]
        rest[0:64, :] = metals_ref[rows(near, 64, BY), :]
        for x in range(1, BX - 1):
            at = 64 + 16 * (x - 1)
            rest[at : at + 16, :] = src_ref[rows(x * BY + near + step, 16, plane), :]
        rest[96:100, :] = cy_ref[rows(near, 4, BY), :]
        rest[100:ZROWS, :] = jnp.zeros((ZROWS - 100, NZ), F32)
    for out, high in ((xa_ref, even_x), (xb_ref, 1 - even_x)):
        near = jnp.where(high == 1, BX - 1, 0) * BY
        step = jnp.where(high == 1, -1, 1) * BY
        tile = 0
        pieces = [(src_ref, k * BX * BY + near) for k in range(COMP)]
        pieces += [(src_ref, k * BX * BY + near + step) for k in range(NMET)]
        pieces += [(metals_ref, k * BX * BY + near) for k in range(NMET)]
        pieces += [(dens_ref, near), (dens_ref, near + step), (dens_ref, near + 2 * step)]
        pieces += [(cx_ref, near)]
        for ref, at in pieces:
            out[tile * BY : tile * BY + BY, :] = ref[pl.ds(pl.multiple_of(at, BY), BY), :]
            tile += 1
    for out, alone in (
        (ya_ref, alone_ya), (yb_ref, alone_yb), (za_ref, alone_ya), (zb_ref, alone_yb),
        (xa_ref, alone_xa), (xb_ref, alone_xb),
    ):
        clear(out, alone)


def clear(ref, alone):
    @pl.when(alone)
    def _():
        ref[...] = jnp.zeros(ref.shape, F32)


def corner_kernel(ya_ref, yb_ref, xa_ref, xb_ref, ca_ref, cb_ref):
    del xa_ref, xb_ref
    even_x, alone_a, alone_b = place("gx")
    for out, high in ((ca_ref, even_x), (cb_ref, 1 - even_x)):
        near = jnp.where(high == 1, BX - 1, 0)
        step = jnp.where(high == 1, -1, 1)
        at = pl.multiple_of(jnp.where(high == 1, 80, 64), 16)
        for side, y_ref in enumerate((ya_ref, yb_ref)):
            base = side * 48
            out[base : base + 16, :] = y_ref[rows(near, 16, BX), :]
            out[base + 16 : base + 32, :] = y_ref[rows(near + step, 16, BX), :]
            out[base + 32 : base + 48, :] = y_ref[pl.ds(at, 16), :]
            base = 96 + side * 9
            out[base : base + 1, :] = y_ref[pl.ds(96 + near, 1), :]
            for i, (w, q) in enumerate(DENSITIES):
                out[base + 1 + i : base + 2 + i, :] = y_ref[pl.ds(100 + 4 * w + near + q * step, 1), :]
    clear(ca_ref, alone_a)
    clear(cb_ref, alone_b)


def sort_kernel(za_ref, zb_ref, zlow_ref, zhigh_ref):
    a_is_high = place("gy")[0] == 1
    a = za_ref[...]
    b = zb_ref[...]
    zlow_ref[...] = jnp.where(a_is_high, b, a)
    zhigh_ref[...] = jnp.where(a_is_high, a, b)


def finish_kernel(
    src_ref, ya_ref, yb_ref, xa_ref, xb_ref, zlow_ref, zhigh_ref, ca_ref, cb_ref,
    dens_ref, metals_ref, energy_ref, cx_ref, cy_ref, cz_ref,
    out_hbm, energy_out_hbm,
    out_ref, energy_out_ref, sems,
    se_ref, de_ref, rw_ref, ys_ref, ee_ref, mx_ref, my_ref, cxl_ref, cye_ref,
):
    even_x = place("gx")[0]
    even_y = place("gy")[0]
    lane = lax.broadcasted_iota(jnp.int32, (1, NZ), 1)
    not_first = lane > 0
    not_last = lane < NZ - 1

    def prev_z(v):
        return pltpu.roll(v, 1, 1)

    def next_z(v):
        return pltpu.roll(v, NZ - 1, 1)

    def masked_prev(v):
        return jnp.where(not_first, prev_z(v), 0.0)

    def masked_next(v):
        return jnp.where(not_last, next_z(v), 0.0)

    de_ref[...] = jnp.zeros(de_ref.shape, F32)

    for x in range(BX):
        at = x * BY
        d_at = (x + 3) * DPITCH + 16
        de_ref[d_at : d_at + BY, :] = dens_ref[at : at + BY, :]
        cye_ref[x * PITCH + 8 : x * PITCH + 16, :] = cy_ref[at : at + BY, :]
        for k in range(COMP):
            s_at = (k * 8 + x + 2) * PITCH + 8
            se_ref[s_at : s_at + BY, :] = src_ref[(k * BX + x) * BY : (k * BX + x + 1) * BY, :]

    for y_ref, high in ((ya_ref, even_y), (yb_ref, 1 - even_y)):
        is_high = high == 1
        r1 = jnp.where(is_high, 16, 7)
        r2 = jnp.where(is_high, 17, 6)
        for k in range(NMET):
            at = k * BX
            base = (k * 8 + 2) * PITCH
            se_ref[rows(base + r1, BX, PITCH), :] = y_ref[at : at + BX, :]
        for i, x in enumerate((0, BX - 1)):
            se_ref[rows((x + 2) * PITCH + r2, NMET, 8 * PITCH), :] = y_ref[64 + 16 * i : 80 + 16 * i, :]
        base = (NMET * 8 + 2) * PITCH
        se_ref[rows(base + r1, BX, PITCH), :] = y_ref[96:100, :]
        for w in range(3):
            d_row = jnp.where(is_high, 24 + w, 15 - w)
            de_ref[rows(3 * DPITCH + d_row, BX, DPITCH), :] = y_ref[100 + 4 * w : 104 + 4 * w, :]
    for side, z_ref in enumerate((zlow_ref, zhigh_ref)):
        for k in range(NMET):
            my_ref[side, k * 8 + 2 : k * 8 + 2 + BX, :] = z_ref[k * BX : k * BX + BX, :]
        for x in range(1, BX - 1):
            r2 = (6, 17)[side]
            se_ref[rows((x + 2) * PITCH + r2, NMET, 8 * PITCH), :] = z_ref[48 + 16 * x : 64 + 16 * x, :]
    cye_ref[rows(7, BX, PITCH), :] = zlow_ref[96:100, :]

    for x_ref, c_ref, high in ((xa_ref, ca_ref, even_x), (xb_ref, cb_ref, 1 - even_x)):
        is_high = high == 1
        p1 = jnp.where(is_high, 6, 1)
        p2 = jnp.where(is_high, 7, 0)
        for k in range(COMP):
            at = pl.multiple_of((k * 8 + p1) * PITCH + 8, 8)
            se_ref[pl.ds(at, BY), :] = x_ref[k * BY : k * BY + BY, :]
        for k in range(NMET):
            at = pl.multiple_of((k * 8 + p2) * PITCH + 8, 8)
            tile = COMP + k
            se_ref[pl.ds(at, BY), :] = x_ref[tile * BY : tile * BY + BY, :]
            tile = COMP + NMET + k
            mx_ref[high, k * BY : k * BY + BY, :] = x_ref[tile * BY : tile * BY + BY, :]
        for w in range(3):
            tile = COMP + 2 * NMET + w
            plane = jnp.where(is_high, 7 + w, 2 - w)
            at = pl.multiple_of(plane * DPITCH + 16, 8)
            de_ref[pl.ds(at, BY), :] = x_ref[tile * BY : tile * BY + BY, :]
        tile = COMP + 2 * NMET + 3
        cxl_ref[high] = x_ref[tile * BY : tile * BY + BY, :]
        for side, y_high in enumerate((even_y, 1 - even_y)):
            base = 48 * side
            y_is_high = y_high == 1
            r1 = jnp.where(y_is_high, 16, 7)
            r2 = jnp.where(y_is_high, 17, 6)
            se_ref[rows(p1 * PITCH + r1, NMET, 8 * PITCH), :] = c_ref[base : base + 16, :]
            se_ref[rows(p2 * PITCH + r1, NMET, 8 * PITCH), :] = c_ref[base + 16 : base + 32, :]
            se_ref[rows(p1 * PITCH + r2, NMET, 8 * PITCH), :] = c_ref[base + 32 : base + 48, :]
            base = 96 + 9 * side
            se_ref[pl.ds((NMET * 8 + p1) * PITCH + r1, 1), :] = c_ref[base : base + 1, :]
            for i, (w, q) in enumerate(DENSITIES):
                d_row = jnp.where(y_is_high, 24 + w, 15 - w)
                plane = jnp.where(is_high, 7 + q, 2 - q)
                de_ref[pl.ds(plane * DPITCH + d_row, 1), :] = c_ref[base + 1 + i : base + 2 + i, :]

    columns = []
    for p in range(10):
        at = p * DPITCH + 8
        columns.append(
            de_ref[at - 1 : at + 23, :] + de_ref[at : at + 24, :] + de_ref[at + 1 : at + 25, :]
        )
    for p in range(8):
        flat = columns[p] + columns[p + 1] + columns[p + 2]
        weight = flat + masked_prev(flat) + masked_next(flat)
        inside = weight > 0.0
        rw_ref[p * PITCH : (p + 1) * PITCH, :] = jnp.where(
            inside, 1.0 / jnp.where(inside, weight, 1.0), 0.0
        )

    copies = []
    for first in range(NMET, -1, -GROUP):
        group = [first] if first == NMET else range(first, first + GROUP)
        share_sums(group, se_ref, rw_ref, ys_ref)
        for k in group:
            for p in range(2, 6) if k == NMET else range(1, 7):
                dens = de_ref[(p + 1) * DPITCH + 16 : (p + 1) * DPITCH + 24, :]
                at = (k * 8 + p) * BY
                flat = (
                    ys_ref[at - BY : at, :] + ys_ref[at : at + BY, :] + ys_ref[at + BY : at + 2 * BY, :]
                )
                collected = flat + masked_prev(flat) + masked_next(flat)
                deposit = dens * collected
                if k == NMET:
                    cell = (p - 2) * BY
                    energy_out_ref[cell : cell + BY, :] = energy_ref[cell : cell + BY, :] + deposit
                    continue
                if p == 1:
                    metal = mx_ref[0, k * BY : k * BY + BY, :]
                elif p == 6:
                    metal = mx_ref[1, k * BY : k * BY + BY, :]
                else:
                    cell = (k * BX + p - 2) * BY
                    metal = metals_ref[cell : cell + BY, :]
                e_at = (k * 8 + p) * PITCH + 8
                ee_ref[e_at : e_at + BY, :] = metal + deposit
        if first == NMET:
            copies.append(pltpu.make_async_copy(energy_out_ref, energy_out_hbm, sems.at[0]))
            copies[-1].start()
            continue

        for side in range(2):
            row = (7, 16)[side]
            dens = de_ref[rows(DPITCH + row + 8, 8, DPITCH), :]
            inv = [rw_ref[rows(row - 1 + d, 8, PITCH), :] for d in range(3)]
            for k in group:
                value = None
                for d in range(3):
                    term = se_ref[rows(k * 8 * PITCH + row - 1 + d, 8, PITCH), :] * inv[d]
                    value = term if value is None else value + term
                flat = value + pltpu.roll(value, 1, 0) + pltpu.roll(value, 7, 0)
                deposit = dens * (flat + masked_prev(flat) + masked_next(flat))
                ee_ref[rows(k * 8 * PITCH + row, 8, PITCH), :] = (
                    my_ref[side, k * 8 : k * 8 + 8, :] + deposit
                )

        for x in range(BX):
            at = x * BY
            cx_up = cx_ref[at : at + BY, :]
            cx_low = cxl_ref[0] if x == 0 else cx_ref[at - BY : at, :]
            cy_up = cy_ref[at : at + BY, :]
            cy_low = cye_ref[x * PITCH + 7 : x * PITCH + 15, :]
            cz_up = cz_ref[at : at + BY, :]
            cz_low = masked_prev(cz_up)
            to_next = [-jnp.minimum(c, 0.0) for c in (cx_up, cy_up, cz_up)]
            from_prev = [jnp.maximum(c, 0.0) for c in (cx_low, cy_low, cz_low)]
            middle = 1.0
            for up, low in ((cx_up, cx_low), (cy_up, cy_low), (cz_up, cz_low)):
                middle = middle - jnp.maximum(up, 0.0) + jnp.minimum(low, 0.0)
            to_next[2] = jnp.where(not_last, to_next[2], 0.0)
            for k in group:
                e_at = (k * 8 + x + 2) * PITCH + 8
                own = ee_ref[e_at : e_at + BY, :]
                result = middle * own
                result = result + to_next[0] * ee_ref[e_at + PITCH : e_at + PITCH + BY, :]
                result = result + from_prev[0] * ee_ref[e_at - PITCH : e_at - PITCH + BY, :]
                result = result + to_next[1] * ee_ref[e_at + 1 : e_at + 1 + BY, :]
                result = result + from_prev[1] * ee_ref[e_at - 1 : e_at - 1 + BY, :]
                result = result + to_next[2] * next_z(own)
                result = result + from_prev[2] * prev_z(own)
                cell = (k * BX + x) * BY
                out_ref[cell : cell + BY, :] = result
        piece = pl.ds(first * BX * BY, GROUP * BX * BY)
        copies.append(
            pltpu.make_async_copy(out_ref.at[piece], out_hbm.at[piece], sems.at[len(copies)])
        )
        copies[-1].start()
    for copy in copies:
        copy.wait()


def share_sums(group, se_ref, rw_ref, ys_ref):
    for p in range(8):
        inv = [rw_ref[p * PITCH + 7 + d : p * PITCH + 15 + d, :] for d in range(3)]
        for k in group:
            if k == NMET and p in (0, 7):
                continue
            at = (k * 8 + p) * PITCH + 7
            value = None
            for d in range(3):
                term = se_ref[at + d : at + d + BY, :] * inv[d]
                value = term if value is None else value + term
            ys_ref[(k * 8 + p) * BY : (k * 8 + p) * BY + BY, :] = value


def swaps():
    nx = lax.axis_size("gx")
    ny = lax.axis_size("gy")
    rounds = []
    for along_x in (True, False):
        for first in (0, 1):
            pairs = []
            for x in range(nx):
                for y in range(ny):
                    place_, count = (x, nx) if along_x else (y, ny)
                    mate = place_ + 1 if place_ % 2 == first else place_ - 1
                    if 0 <= mate < count:
                        to = (mate, y) if along_x else (x, mate)
                    elif along_x and ny % 2 == 0:
                        to = (x, (y + ny // 2) % ny)
                    elif not along_x and nx % 2 == 0:
                        to = (x + 1 - 2 * (x % 2), y)
                    else:
                        to = (x, y)
                    pairs.append((x * ny + y, to[0] * ny + to[1]))
            rounds.append(pairs)
    return rounds


def swap(value, pairs):
    return lax.ppermute(value, ("gx", "gy"), pairs)


VM = pl.BlockSpec(memory_space=pltpu.VMEM)
HB = pl.BlockSpec(memory_space=pltpu.HBM)


def buffer(count):
    return pltpu.VMEM((count, NZ), F32)


def body(masses, table, star_mask, density, metals, energy, courant_x, courant_y, courant_z):
    cells = BX * BY
    masses = masses.reshape(BINS, cells, NZ)
    star_mask, density, energy, courant_x, courant_y, courant_z = (
        a.reshape(cells, NZ) for a in (star_mask, density, energy, courant_x, courant_y, courant_z)
    )
    metals = metals.reshape(NMET * cells, NZ)
    src, ya, yb, xa, xb, za, zb, *local = pl.pallas_call(
        sources_kernel,
        name="sources",
        out_shape=[buffer(COMP * cells)]
        + [buffer(count) for count in (YROWS, YROWS, XROWS, XROWS, ZROWS, ZROWS)]
        + [buffer(cells), buffer(NMET * cells)] + [buffer(cells)] * 4,
        in_specs=[HB] * 9,
        out_specs=[VM] * 13,
        scratch_shapes=[
            pltpu.VMEM((BINS, cells, NZ), BF16),
            pltpu.VMEM((COMP, BINS), BF16),
            pltpu.VMEM((cells, NZ), jnp.int32),
            pltpu.VMEM(((COMP + 1) * BY, BINS * BY), BF16),
            pltpu.VMEM((24, BINS * BY), F32),
            pltpu.SemaphoreType.DMA((CHUNKS,)),
            pltpu.SemaphoreType.DMA((8,)),
        ],
        compiler_params=pltpu.CompilerParams(vmem_limit_bytes=32 * 1024 * 1024),
    )(
        *(
            pltpu.with_memory_space_constraint(a, pltpu.HBM)
            for a in (
                masses, table.T, star_mask, density, metals, energy, courant_x, courant_y, courant_z
            )
        )
    )
    pairs_xa, pairs_xb, pairs_ya, pairs_yb = swaps()
    ya = swap(ya, pairs_ya)
    yb = swap(yb, pairs_yb)
    xa = swap(xa, pairs_xa)
    xb = swap(xb, pairs_xb)
    za = swap(za, pairs_ya)
    zb = swap(zb, pairs_yb)
    ca, cb = pl.pallas_call(
        corner_kernel,
        name="corners",
        out_shape=[buffer(CROWS), buffer(CROWS)],
        in_specs=[VM] * 4,
        out_specs=[VM, VM],
        compiler_params=pltpu.CompilerParams(vmem_limit_bytes=4 * 1024 * 1024),
    )(*(pltpu.with_memory_space_constraint(a, pltpu.VMEM) for a in (ya, yb, xa, xb)))
    ca = swap(ca, pairs_xa)
    cb = swap(cb, pairs_xb)
    z = pl.pallas_call(
        sort_kernel,
        name="sort",
        out_shape=[buffer(ZROWS), buffer(ZROWS)],
        in_specs=[VM] * 2,
        out_specs=[VM] * 2,
        compiler_params=pltpu.CompilerParams(vmem_limit_bytes=4 * 1024 * 1024),
    )(*(pltpu.with_memory_space_constraint(a, pltpu.VMEM) for a in (za, zb)))
    advected, energy_out = pl.pallas_call(
        finish_kernel,
        name="finish",
        out_shape=[
            jax.ShapeDtypeStruct((NMET * cells, NZ), F32),
            jax.ShapeDtypeStruct((cells, NZ), F32),
        ],
        in_specs=[VM] * 15,
        out_specs=[HB, HB],
        scratch_shapes=[
            pltpu.VMEM((NMET * cells, NZ), F32),
            pltpu.VMEM((cells, NZ), F32),
            pltpu.SemaphoreType.DMA((1 + NMET // GROUP,)),
            pltpu.VMEM((COMP * 8 * PITCH, NZ), F32),
            pltpu.VMEM((10 * DPITCH, NZ), F32),
            pltpu.VMEM((8 * PITCH, NZ), F32),
            pltpu.VMEM((COMP * 8 * BY, NZ), F32),
            pltpu.VMEM((NMET * 8 * PITCH, NZ), F32),
            pltpu.VMEM((2, NMET * BY, NZ), F32),
            pltpu.VMEM((2, NMET * 8, NZ), F32),
            pltpu.VMEM((2, BY, NZ), F32),
            pltpu.VMEM((BX * PITCH, NZ), F32),
        ],
        compiler_params=pltpu.CompilerParams(vmem_limit_bytes=32 * 1024 * 1024),
    )(
        *(
            pltpu.with_memory_space_constraint(a, pltpu.VMEM)
            for a in (src, ya, yb, xa, xb, *z, ca, cb, *local)
        )
    )
    return advected.reshape(NMET, BX, BY, NZ), energy_out.reshape(BX, BY, NZ)


def solution(mesh):
    field = P("gx", "gy", None)
    stack = P(None, "gx", "gy", None)
    in_specs = (stack, P(), field, field, stack, field, field, field, field)
    out_specs = (stack, field)
    return jax.shard_map(body, mesh=mesh, in_specs=in_specs, out_specs=out_specs, check_vma=False)
```

```python
import jax
import jax.numpy as jnp
from jax import lax
from jax.experimental import pallas as pl
from jax.experimental.pallas import tpu as pltpu
from jax.sharding import PartitionSpec as P

F32 = jnp.float32
BF16 = jnp.bfloat16
BINS = 256
COMP = 17
NMET = 16
BX = 4
BY = 8
NZ = 128
CHUNKS = 8
GROUP = 4
YROWS = 112
ZROWS = 114
XROWS = 424
CROWS = 114
PITCH = 24
DENSITIES = [(w, q) for w in range(3) for q in range(3) if w + q < 4]
DPITCH = 40


def rows(start, count, stride=1):
    return pl.ds(start, count) if stride == 1 else pl.ds(start, count, stride)


def place(axis):
    index = lax.axis_index(axis)
    last = index == lax.axis_size(axis) - 1
    odd = index % 2
    alone_a = jnp.logical_and(odd == 0, last)
    alone_b = jnp.logical_or(index == 0, jnp.logical_and(odd == 1, last))
    return 1 - odd, alone_a, alone_b


def sources_kernel(
    masses_hbm, table_hbm, star_hbm, dens_hbm, metals_hbm, energy_hbm, cx_hbm, cy_hbm, cz_hbm,
    src_ref, ya_ref, yb_ref, xa_ref, xb_ref, za_ref, zb_ref,
    dens_ref, metals_ref, energy_ref, cx_ref, cy_ref, cz_ref,
    mass_buf, table_ref, star_ref, expand_ref, wide_ref, mass_sems, sems,
):
    small = [
        (table_hbm, table_ref), (star_hbm, star_ref), (dens_hbm, dens_ref), (metals_hbm, metals_ref),
        (cx_hbm, cx_ref), (cy_hbm, cy_ref), (cz_hbm, cz_ref), (energy_hbm, energy_ref),
    ]
    small_copies = [
        pltpu.make_async_copy(hbm, ref, sems.at[i]) for i, (hbm, ref) in enumerate(small)
    ]
    per = BINS // CHUNKS
    copies = [
        pltpu.make_async_copy(
            masses_hbm.at[pl.ds(c * per, per)], mass_buf.at[pl.ds(c * per, per)], mass_sems.at[c]
        )
        for c in range(CHUNKS)
    ]
    small_copies[0].start()
    for copy in copies:
        copy.start()
    for copy in small_copies[1:]:
        copy.start()

    width = BINS * BY
    group = lax.broadcasted_iota(jnp.int32, (8, NZ), 1) // BY
    same = (
        lax.broadcasted_iota(jnp.int32, (BY, NZ), 1) % BY
        == lax.broadcasted_iota(jnp.int32, (BY, NZ), 0)
    )
    upper = lax.broadcasted_iota(jnp.int32, (1, 16, NZ), 1) < BY
    small_copies[0].wait()
    turned = table_ref[...].astype(F32)
    turned = jnp.concatenate([turned, jnp.zeros((24 - COMP, BINS), F32)], axis=0)

    def expand(c):
        tiles = width // NZ // CHUNKS
        for t in range(c * tiles, (c + 1) * tiles):
            first = 16 * t
            half = first // NZ
            columns = slice(t * NZ, (t + 1) * NZ)
            for r in range(3):
                tile = turned[8 * r : 8 * r + 8, half * NZ : (half + 1) * NZ]
                wide_ref[8 * r : 8 * r + 8, columns] = jnp.take_along_axis(
                    tile, group + first % NZ, axis=1
                )
            for k in range(0, COMP + 1, 2):
                lines = [
                    jnp.where(same, jnp.broadcast_to(wide_ref[i : i + 1, columns], (BY, NZ)), 0.0)
                    for i in (k, k + 1)
                ]
                expand_ref[k * BY : k * BY + 16, columns] = jnp.concatenate(lines, axis=0).astype(BF16)

    expand(0)
    total = None
    for c in range(CHUNKS):
        copies[c].wait()
        part = mass_buf[c * per : (c + 1) * per]
        blocks = []
        for j in range(2):
            both = part[:, 16 * j : 16 * j + 16].reshape(per // 2, 2, 16, NZ)
            even, odd = both[:, 0], both[:, 1]
            blocks.append(jnp.where(upper, even, pltpu.roll(odd, 8, 1)).reshape(per * BY, NZ))
            blocks.append(jnp.where(upper, pltpu.roll(even, 8, 1), odd).reshape(per * BY, NZ))
        right = jnp.concatenate(blocks, axis=1)
        left = expand_ref[:, c * per * BY : (c + 1) * per * BY]
        prod = jnp.dot(left, right, preferred_element_type=F32)
        total = prod if total is None else total + prod
        if c + 1 < CHUNKS:
            expand(c + 1)
    for copy in small_copies[1:]:
        copy.wait()
    for x in range(BX):
        mask = star_ref[x * BY : x * BY + BY, :].astype(F32)
        for k in range(COMP):
            at = (k * BX + x) * BY
            piece = total[k * BY : k * BY + BY, x * NZ : (x + 1) * NZ]
            src_ref[at : at + BY, :] = piece * mask

    even_x, alone_xa, alone_xb = place("gx")
    even_y, alone_ya, alone_yb = place("gy")
    plane = BX * BY
    for out, rest, high in ((ya_ref, za_ref, even_y), (yb_ref, zb_ref, 1 - even_y)):
        near = jnp.where(high == 1, BY - 1, 0)
        step = jnp.where(high == 1, -1, 1)
        out[0:64, :] = src_ref[rows(near, 64, BY), :]
        for i, x in enumerate((0, BX - 1)):
            out[64 + 16 * i : 80 + 16 * i, :] = src_ref[rows(x * BY + near + step, 16, plane), :]
        out[96:100, :] = src_ref[rows(NMET * plane + near, 4, BY), :]
        out[100:104, :] = dens_ref[rows(near, 4, BY), :]
        out[104:108, :] = dens_ref[rows(near + step, 4, BY), :]
        out[108:112, :] = dens_ref[rows(near + 2 * step, 4, BY), :]
        rest[0:64, :] = metals_ref[rows(near, 64, BY), :]
        for x in range(1, BX - 1):
            at = 64 + 16 * (x - 1)
            rest[at : at + 16, :] = src_ref[rows(x * BY + near + step, 16, plane), :]
        rest[96:100, :] = cy_ref[rows(near, 4, BY), :]
        rest[100:ZROWS, :] = jnp.zeros((ZROWS - 100, NZ), F32)
    for out, high in ((xa_ref, even_x), (xb_ref, 1 - even_x)):
        near = jnp.where(high == 1, BX - 1, 0) * BY
        step = jnp.where(high == 1, -1, 1) * BY
        tile = 0
        pieces = [(src_ref, k * BX * BY + near) for k in range(COMP)]
        pieces += [(src_ref, k * BX * BY + near + step) for k in range(NMET)]
        pieces += [(metals_ref, k * BX * BY + near) for k in range(NMET)]
        pieces += [(dens_ref, near), (dens_ref, near + step), (dens_ref, near + 2 * step)]
        pieces += [(cx_ref, near)]
        for ref, at in pieces:
            out[tile * BY : tile * BY + BY, :] = ref[pl.ds(pl.multiple_of(at, BY), BY), :]
            tile += 1
    for out, alone in (
        (ya_ref, alone_ya), (yb_ref, alone_yb), (za_ref, alone_ya), (zb_ref, alone_yb),
        (xa_ref, alone_xa), (xb_ref, alone_xb),
    ):
        clear(out, alone)


def clear(ref, alone):
    @pl.when(alone)
    def _():
        ref[...] = jnp.zeros(ref.shape, F32)


def corner_kernel(ya_ref, yb_ref, xa_ref, xb_ref, ca_ref, cb_ref):
    del xa_ref, xb_ref
    even_x, alone_a, alone_b = place("gx")
    for out, high in ((ca_ref, even_x), (cb_ref, 1 - even_x)):
        near = jnp.where(high == 1, BX - 1, 0)
        step = jnp.where(high == 1, -1, 1)
        at = pl.multiple_of(jnp.where(high == 1, 80, 64), 16)
        for side, y_ref in enumerate((ya_ref, yb_ref)):
            base = side * 48
            out[base : base + 16, :] = y_ref[rows(near, 16, BX), :]
            out[base + 16 : base + 32, :] = y_ref[rows(near + step, 16, BX), :]
            out[base + 32 : base + 48, :] = y_ref[pl.ds(at, 16), :]
            base = 96 + side * 9
            out[base : base + 1, :] = y_ref[pl.ds(96 + near, 1), :]
            for i, (w, q) in enumerate(DENSITIES):
                out[base + 1 + i : base + 2 + i, :] = y_ref[pl.ds(100 + 4 * w + near + q * step, 1), :]
    clear(ca_ref, alone_a)
    clear(cb_ref, alone_b)


def sort_kernel(za_ref, zb_ref, zlow_ref, zhigh_ref):
    a_is_high = place("gy")[0] == 1
    a = za_ref[...]
    b = zb_ref[...]
    zlow_ref[...] = jnp.where(a_is_high, b, a)
    zhigh_ref[...] = jnp.where(a_is_high, a, b)


def finish_kernel(
    src_ref, ya_ref, yb_ref, xa_ref, xb_ref, zlow_ref, zhigh_ref, ca_ref, cb_ref,
    dens_ref, metals_ref, energy_ref, cx_ref, cy_ref, cz_ref,
    out_hbm, energy_out_hbm,
    out_ref, energy_out_ref, sems,
    se_ref, de_ref, rw_ref, ys_ref, ee_ref, mx_ref, my_ref, cxl_ref, cye_ref,
):
    even_x = place("gx")[0]
    even_y = place("gy")[0]
    lane = lax.broadcasted_iota(jnp.int32, (1, NZ), 1)
    not_first = lane > 0
    not_last = lane < NZ - 1

    def prev_z(v):
        return pltpu.roll(v, 1, 1)

    def next_z(v):
        return pltpu.roll(v, NZ - 1, 1)

    def masked_prev(v):
        return jnp.where(not_first, prev_z(v), 0.0)

    def masked_next(v):
        return jnp.where(not_last, next_z(v), 0.0)

    de_ref[...] = jnp.zeros(de_ref.shape, F32)

    for x in range(BX):
        at = x * BY
        d_at = (x + 3) * DPITCH + 16
        de_ref[d_at : d_at + BY, :] = dens_ref[at : at + BY, :]
        cye_ref[x * PITCH + 8 : x * PITCH + 16, :] = cy_ref[at : at + BY, :]
        for k in range(COMP):
            s_at = (k * 8 + x + 2) * PITCH + 8
            se_ref[s_at : s_at + BY, :] = src_ref[(k * BX + x) * BY : (k * BX + x + 1) * BY, :]

    for y_ref, high in ((ya_ref, even_y), (yb_ref, 1 - even_y)):
        is_high = high == 1
        r1 = jnp.where(is_high, 16, 7)
        r2 = jnp.where(is_high, 17, 6)
        for k in range(NMET):
            at = k * BX
            base = (k * 8 + 2) * PITCH
            se_ref[rows(base + r1, BX, PITCH), :] = y_ref[at : at + BX, :]
        for i, x in enumerate((0, BX - 1)):
            se_ref[rows((x + 2) * PITCH + r2, NMET, 8 * PITCH), :] = y_ref[64 + 16 * i : 80 + 16 * i, :]
        base = (NMET * 8 + 2) * PITCH
        se_ref[rows(base + r1, BX, PITCH), :] = y_ref[96:100, :]
        for w in range(3):
            d_row = jnp.where(is_high, 24 + w, 15 - w)
            de_ref[rows(3 * DPITCH + d_row, BX, DPITCH), :] = y_ref[100 + 4 * w : 104 + 4 * w, :]
    for side, z_ref in enumerate((zlow_ref, zhigh_ref)):
        for k in range(NMET):
            my_ref[side, k * 8 + 2 : k * 8 + 2 + BX, :] = z_ref[k * BX : k * BX + BX, :]
        for x in range(1, BX - 1):
            r2 = (6, 17)[side]
            se_ref[rows((x + 2) * PITCH + r2, NMET, 8 * PITCH), :] = z_ref[48 + 16 * x : 64 + 16 * x, :]
    cye_ref[rows(7, BX, PITCH), :] = zlow_ref[96:100, :]

    for x_ref, c_ref, high in ((xa_ref, ca_ref, even_x), (xb_ref, cb_ref, 1 - even_x)):
        is_high = high == 1
        p1 = jnp.where(is_high, 6, 1)
        p2 = jnp.where(is_high, 7, 0)
        for k in range(COMP):
            at = pl.multiple_of((k * 8 + p1) * PITCH + 8, 8)
            se_ref[pl.ds(at, BY), :] = x_ref[k * BY : k * BY + BY, :]
        for k in range(NMET):
            at = pl.multiple_of((k * 8 + p2) * PITCH + 8, 8)
            tile = COMP + k
            se_ref[pl.ds(at, BY), :] = x_ref[tile * BY : tile * BY + BY, :]
            tile = COMP + NMET + k
            mx_ref[high, k * BY : k * BY + BY, :] = x_ref[tile * BY : tile * BY + BY, :]
        for w in range(3):
            tile = COMP + 2 * NMET + w
            plane = jnp.where(is_high, 7 + w, 2 - w)
            at = pl.multiple_of(plane * DPITCH + 16, 8)
            de_ref[pl.ds(at, BY), :] = x_ref[tile * BY : tile * BY + BY, :]
        tile = COMP + 2 * NMET + 3
        cxl_ref[high] = x_ref[tile * BY : tile * BY + BY, :]
        for side, y_high in enumerate((even_y, 1 - even_y)):
            base = 48 * side
            y_is_high = y_high == 1
            r1 = jnp.where(y_is_high, 16, 7)
            r2 = jnp.where(y_is_high, 17, 6)
            se_ref[rows(p1 * PITCH + r1, NMET, 8 * PITCH), :] = c_ref[base : base + 16, :]
            se_ref[rows(p2 * PITCH + r1, NMET, 8 * PITCH), :] = c_ref[base + 16 : base + 32, :]
            se_ref[rows(p1 * PITCH + r2, NMET, 8 * PITCH), :] = c_ref[base + 32 : base + 48, :]
            base = 96 + 9 * side
            se_ref[pl.ds((NMET * 8 + p1) * PITCH + r1, 1), :] = c_ref[base : base + 1, :]
            for i, (w, q) in enumerate(DENSITIES):
                d_row = jnp.where(y_is_high, 24 + w, 15 - w)
                plane = jnp.where(is_high, 7 + q, 2 - q)
                de_ref[pl.ds(plane * DPITCH + d_row, 1), :] = c_ref[base + 1 + i : base + 2 + i, :]

    columns = []
    for p in range(10):
        at = p * DPITCH + 8
        columns.append(
            de_ref[at - 1 : at + 23, :] + de_ref[at : at + 24, :] + de_ref[at + 1 : at + 25, :]
        )
    for p in range(8):
        flat = columns[p] + columns[p + 1] + columns[p + 2]
        weight = flat + masked_prev(flat) + masked_next(flat)
        inside = weight > 0.0
        rw_ref[p * PITCH : (p + 1) * PITCH, :] = jnp.where(
            inside, 1.0 / jnp.where(inside, weight, 1.0), 0.0
        )

    copies = []
    for first in range(NMET, -1, -GROUP):
        group = [first] if first == NMET else range(first, first + GROUP)
        share_sums(group, se_ref, rw_ref, ys_ref)
        for k in group:
            for p in range(2, 6) if k == NMET else range(1, 7):
                dens = de_ref[(p + 1) * DPITCH + 16 : (p + 1) * DPITCH + 24, :]
                at = (k * 8 + p) * BY
                flat = (
                    ys_ref[at - BY : at, :] + ys_ref[at : at + BY, :] + ys_ref[at + BY : at + 2 * BY, :]
                )
                collected = flat + masked_prev(flat) + masked_next(flat)
                deposit = dens * collected
                if k == NMET:
                    cell = (p - 2) * BY
                    energy_out_ref[cell : cell + BY, :] = energy_ref[cell : cell + BY, :] + deposit
                    continue
                if p == 1:
                    metal = mx_ref[0, k * BY : k * BY + BY, :]
                elif p == 6:
                    metal = mx_ref[1, k * BY : k * BY + BY, :]
                else:
                    cell = (k * BX + p - 2) * BY
                    metal = metals_ref[cell : cell + BY, :]
                e_at = (k * 8 + p) * PITCH + 8
                ee_ref[e_at : e_at + BY, :] = metal + deposit
        if first == NMET:
            copies.append(pltpu.make_async_copy(energy_out_ref, energy_out_hbm, sems.at[0]))
            copies[-1].start()
            continue

        for side in range(2):
            row = (7, 16)[side]
            dens = de_ref[rows(DPITCH + row + 8, 8, DPITCH), :]
            inv = [rw_ref[rows(row - 1 + d, 8, PITCH), :] for d in range(3)]
            for k in group:
                value = None
                for d in range(3):
                    term = se_ref[rows(k * 8 * PITCH + row - 1 + d, 8, PITCH), :] * inv[d]
                    value = term if value is None else value + term
                flat = value + pltpu.roll(value, 1, 0) + pltpu.roll(value, 7, 0)
                deposit = dens * (flat + masked_prev(flat) + masked_next(flat))
                ee_ref[rows(k * 8 * PITCH + row, 8, PITCH), :] = (
                    my_ref[side, k * 8 : k * 8 + 8, :] + deposit
                )

        for x in range(BX):
            at = x * BY
            cx_up = cx_ref[at : at + BY, :]
            cx_low = cxl_ref[0] if x == 0 else cx_ref[at - BY : at, :]
            cy_up = cy_ref[at : at + BY, :]
            cy_low = cye_ref[x * PITCH + 7 : x * PITCH + 15, :]
            cz_up = cz_ref[at : at + BY, :]
            cz_low = masked_prev(cz_up)
            to_next = [-jnp.minimum(c, 0.0) for c in (cx_up, cy_up, cz_up)]
            from_prev = [jnp.maximum(c, 0.0) for c in (cx_low, cy_low, cz_low)]
            middle = 1.0
            for up, low in ((cx_up, cx_low), (cy_up, cy_low), (cz_up, cz_low)):
                middle = middle - jnp.maximum(up, 0.0) + jnp.minimum(low, 0.0)
            to_next[2] = jnp.where(not_last, to_next[2], 0.0)
            for k in group:
                e_at = (k * 8 + x + 2) * PITCH + 8
                own = ee_ref[e_at : e_at + BY, :]
                result = middle * own
                result = result + to_next[0] * ee_ref[e_at + PITCH : e_at + PITCH + BY, :]
                result = result + from_prev[0] * ee_ref[e_at - PITCH : e_at - PITCH + BY, :]
                result = result + to_next[1] * ee_ref[e_at + 1 : e_at + 1 + BY, :]
                result = result + from_prev[1] * ee_ref[e_at - 1 : e_at - 1 + BY, :]
                result = result + to_next[2] * next_z(own)
                result = result + from_prev[2] * prev_z(own)
                cell = (k * BX + x) * BY
                out_ref[cell : cell + BY, :] = result
        piece = pl.ds(first * BX * BY, GROUP * BX * BY)
        copies.append(
            pltpu.make_async_copy(out_ref.at[piece], out_hbm.at[piece], sems.at[len(copies)])
        )
        copies[-1].start()
    for copy in copies:
        copy.wait()


def share_sums(group, se_ref, rw_ref, ys_ref):
    for p in range(8):
        inv = [rw_ref[p * PITCH + 7 + d : p * PITCH + 15 + d, :] for d in range(3)]
        for k in group:
            if k == NMET and p in (0, 7):
                continue
            at = (k * 8 + p) * PITCH + 7
            value = None
            for d in range(3):
                term = se_ref[at + d : at + d + BY, :] * inv[d]
                value = term if value is None else value + term
            ys_ref[(k * 8 + p) * BY : (k * 8 + p) * BY + BY, :] = value


def swaps():
    nx = lax.axis_size("gx")
    ny = lax.axis_size("gy")
    rounds = []
    for along_x in (True, False):
        for first in (0, 1):
            pairs = []
            for x in range(nx):
                for y in range(ny):
                    place_, count = (x, nx) if along_x else (y, ny)
                    mate = place_ + 1 if place_ % 2 == first else place_ - 1
                    if 0 <= mate < count:
                        to = (mate, y) if along_x else (x, mate)
                    elif along_x and ny % 2 == 0:
                        to = (x, (y + ny // 2) % ny)
                    elif not along_x and nx % 2 == 0:
                        to = (x + 1 - 2 * (x % 2), y)
                    else:
                        to = (x, y)
                    pairs.append((x * ny + y, to[0] * ny + to[1]))
            rounds.append(pairs)
    return rounds


def swap(value, pairs):
    return lax.ppermute(value, ("gx", "gy"), pairs)


VM = pl.BlockSpec(memory_space=pltpu.VMEM)
HB = pl.BlockSpec(memory_space=pltpu.HBM)


def buffer(count):
    return pltpu.VMEM((count, NZ), F32)


def body(masses, table, star_mask, density, metals, energy, courant_x, courant_y, courant_z):
    cells = BX * BY
    masses = masses.reshape(BINS, cells, NZ)
    star_mask, density, energy, courant_x, courant_y, courant_z = (
        a.reshape(cells, NZ) for a in (star_mask, density, energy, courant_x, courant_y, courant_z)
    )
    metals = metals.reshape(NMET * cells, NZ)
    src, ya, yb, xa, xb, za, zb, *local = pl.pallas_call(
        sources_kernel,
        name="sources",
        out_shape=[buffer(COMP * cells)]
        + [buffer(count) for count in (YROWS, YROWS, XROWS, XROWS, ZROWS, ZROWS)]
        + [buffer(cells), buffer(NMET * cells)] + [buffer(cells)] * 4,
        in_specs=[HB] * 9,
        out_specs=[VM] * 13,
        scratch_shapes=[
            pltpu.VMEM((BINS, cells, NZ), BF16),
            pltpu.VMEM((COMP, BINS), BF16),
            pltpu.VMEM((cells, NZ), jnp.int32),
            pltpu.VMEM(((COMP + 1) * BY, BINS * BY), BF16),
            pltpu.VMEM((24, BINS * BY), F32),
            pltpu.SemaphoreType.DMA((CHUNKS,)),
            pltpu.SemaphoreType.DMA((8,)),
        ],
        compiler_params=pltpu.CompilerParams(vmem_limit_bytes=32 * 1024 * 1024),
    )(
        *(
            pltpu.with_memory_space_constraint(a, pltpu.HBM)
            for a in (
                masses, table.T, star_mask, density, metals, energy, courant_x, courant_y, courant_z
            )
        )
    )
    pairs_xa, pairs_xb, pairs_ya, pairs_yb = swaps()
    ya = swap(ya, pairs_ya)
    yb = swap(yb, pairs_yb)
    xa = swap(xa, pairs_xa)
    xb = swap(xb, pairs_xb)
    za = swap(za, pairs_ya)
    zb = swap(zb, pairs_yb)
    ca, cb = pl.pallas_call(
        corner_kernel,
        name="corners",
        out_shape=[buffer(CROWS), buffer(CROWS)],
        in_specs=[VM] * 4,
        out_specs=[VM, VM],
        compiler_params=pltpu.CompilerParams(vmem_limit_bytes=4 * 1024 * 1024),
    )(*(pltpu.with_memory_space_constraint(a, pltpu.VMEM) for a in (ya, yb, xa, xb)))
    ca = swap(ca, pairs_xa)
    cb = swap(cb, pairs_xb)
    z = pl.pallas_call(
        sort_kernel,
        name="sort",
        out_shape=[buffer(ZROWS), buffer(ZROWS)],
        in_specs=[VM] * 2,
        out_specs=[VM] * 2,
        compiler_params=pltpu.CompilerParams(vmem_limit_bytes=4 * 1024 * 1024),
    )(*(pltpu.with_memory_space_constraint(a, pltpu.VMEM) for a in (za, zb)))
    advected, energy_out = pl.pallas_call(
        finish_kernel,
        name="finish",
        out_shape=[
            jax.ShapeDtypeStruct((NMET * cells, NZ), F32),
            jax.ShapeDtypeStruct((cells, NZ), F32),
        ],
        in_specs=[VM] * 15,
        out_specs=[HB, HB],
        scratch_shapes=[
            pltpu.VMEM((NMET * cells, NZ), F32),
            pltpu.VMEM((cells, NZ), F32),
            pltpu.SemaphoreType.DMA((1 + NMET // GROUP,)),
            pltpu.VMEM((COMP * 8 * PITCH, NZ), F32),
            pltpu.VMEM((10 * DPITCH, NZ), F32),
            pltpu.VMEM((8 * PITCH, NZ), F32),
            pltpu.VMEM((COMP * 8 * BY, NZ), F32),
            pltpu.VMEM((NMET * 8 * PITCH, NZ), F32),
            pltpu.VMEM((2, NMET * BY, NZ), F32),
            pltpu.VMEM((2, NMET * 8, NZ), F32),
            pltpu.VMEM((2, BY, NZ), F32),
            pltpu.VMEM((BX * PITCH, NZ), F32),
        ],
        compiler_params=pltpu.CompilerParams(vmem_limit_bytes=32 * 1024 * 1024),
    )(
        *(
            pltpu.with_memory_space_constraint(a, pltpu.VMEM)
            for a in (src, ya, yb, xa, xb, *z, ca, cb, *local)
        )
    )
    return advected.reshape(NMET, BX, BY, NZ), energy_out.reshape(BX, BY, NZ)


def solution(mesh):
    field = P("gx", "gy", None)
    stack = P(None, "gx", "gy", None)
    in_specs = (stack, P(), field, field, stack, field, field, field, field)
    out_specs = (stack, field)
    return jax.shard_map(body, mesh=mesh, in_specs=in_specs, out_specs=out_specs, check_vma=False)
```

```python
import functools

import jax
import jax.numpy as jnp
from jax import lax
from jax.experimental import pallas as pl
from jax.experimental.pallas import tpu as pltpu
from jax.sharding import PartitionSpec as P

F32 = jnp.float32
BF16 = jnp.bfloat16
BINS = 256
COMP = 17
NMET = 16
BX = 4
BY = 8
NZ = 128
CHUNKS = 8
GROUP = 4
YROWS = 112
ZROWS = 114
XROWS = 424
CROWS = 114
PITCH = 24
DENSITIES = [(w, q) for w in range(3) for q in range(3) if w + q < 4]
DPITCH = 40


def rows(start, count, stride=1):
    return pl.ds(start, count) if stride == 1 else pl.ds(start, count, stride)


def place(axis):
    index = lax.axis_index(axis)
    last = index == lax.axis_size(axis) - 1
    odd = index % 2
    alone_a = jnp.logical_and(odd == 0, last)
    alone_b = jnp.logical_or(index == 0, jnp.logical_and(odd == 1, last))
    return 1 - odd, alone_a, alone_b


def sources_kernel(
    masses_hbm, table_hbm, star_hbm, dens_hbm, metals_hbm, energy_hbm, cx_hbm, cy_hbm, cz_hbm,
    src_ref, ya_ref, yb_ref, xa_ref, xb_ref, za_ref, zb_ref,
    dens_ref, metals_ref, energy_ref, cx_ref, cy_ref, cz_ref,
    mass_buf, table_ref, star_ref, expand_ref, wide_ref, mass_sems, sems,
):
    small = [
        (table_hbm, table_ref), (star_hbm, star_ref), (dens_hbm, dens_ref), (metals_hbm, metals_ref),
        (cx_hbm, cx_ref), (cy_hbm, cy_ref), (cz_hbm, cz_ref), (energy_hbm, energy_ref),
    ]
    small_copies = [
        pltpu.make_async_copy(hbm, ref, sems.at[i]) for i, (hbm, ref) in enumerate(small)
    ]
    per = BINS // CHUNKS
    copies = [
        pltpu.make_async_copy(
            masses_hbm.at[pl.ds(c * per, per)], mass_buf.at[pl.ds(c * per, per)], mass_sems.at[c]
        )
        for c in range(CHUNKS)
    ]
    small_copies[0].start()
    for copy in copies:
        copy.start()
    for copy in small_copies[1:]:
        copy.start()

    width = BINS * BY
    group = lax.broadcasted_iota(jnp.int32, (8, NZ), 1) // BY
    same = (
        lax.broadcasted_iota(jnp.int32, (BY, NZ), 1) % BY
        == lax.broadcasted_iota(jnp.int32, (BY, NZ), 0)
    )
    upper = lax.broadcasted_iota(jnp.int32, (1, 16, NZ), 1) < BY
    small_copies[0].wait()
    turned = table_ref[...].astype(F32)
    turned = jnp.concatenate([turned, jnp.zeros((24 - COMP, BINS), F32)], axis=0)

    def expand(c):
        tiles = width // NZ // CHUNKS
        for t in range(c * tiles, (c + 1) * tiles):
            first = 16 * t
            half = first // NZ
            columns = slice(t * NZ, (t + 1) * NZ)
            for r in range(3):
                tile = turned[8 * r : 8 * r + 8, half * NZ : (half + 1) * NZ]
                wide_ref[8 * r : 8 * r + 8, columns] = jnp.take_along_axis(
                    tile, group + first % NZ, axis=1
                )
            for k in range(0, COMP + 1, 2):
                lines = [
                    jnp.where(same, jnp.broadcast_to(wide_ref[i : i + 1, columns], (BY, NZ)), 0.0)
                    for i in (k, k + 1)
                ]
                expand_ref[k * BY : k * BY + 16, columns] = jnp.concatenate(lines, axis=0).astype(BF16)

    expand(0)
    total = None
    for c in range(CHUNKS):
        copies[c].wait()
        part = mass_buf[c * per : (c + 1) * per]
        blocks = []
        for j in range(2):
            both = part[:, 16 * j : 16 * j + 16].reshape(per // 2, 2, 16, NZ)
            even, odd = both[:, 0], both[:, 1]
            blocks.append(jnp.where(upper, even, pltpu.roll(odd, 8, 1)).reshape(per * BY, NZ))
            blocks.append(jnp.where(upper, pltpu.roll(even, 8, 1), odd).reshape(per * BY, NZ))
        right = jnp.concatenate(blocks, axis=1)
        left = expand_ref[:, c * per * BY : (c + 1) * per * BY]
        prod = jnp.dot(left, right, preferred_element_type=F32)
        total = prod if total is None else total + prod
        if c + 1 < CHUNKS:
            expand(c + 1)
    for copy in small_copies[1:]:
        copy.wait()
    for x in range(BX):
        mask = star_ref[x * BY : x * BY + BY, :].astype(F32)
        for k in range(COMP):
            at = (k * BX + x) * BY
            piece = total[k * BY : k * BY + BY, x * NZ : (x + 1) * NZ]
            src_ref[at : at + BY, :] = piece * mask

    even_x, alone_xa, alone_xb = place("gx")
    even_y, alone_ya, alone_yb = place("gy")
    plane = BX * BY
    for out, rest, high in ((ya_ref, za_ref, even_y), (yb_ref, zb_ref, 1 - even_y)):
        near = jnp.where(high == 1, BY - 1, 0)
        step = jnp.where(high == 1, -1, 1)
        out[0:64, :] = src_ref[rows(near, 64, BY), :]
        for i, x in enumerate((0, BX - 1)):
            out[64 + 16 * i : 80 + 16 * i, :] = src_ref[rows(x * BY + near + step, 16, plane), :]
        out[96:100, :] = src_ref[rows(NMET * plane + near, 4, BY), :]
        out[100:104, :] = dens_ref[rows(near, 4, BY), :]
        out[104:108, :] = dens_ref[rows(near + step, 4, BY), :]
        out[108:112, :] = dens_ref[rows(near + 2 * step, 4, BY), :]
        rest[0:64, :] = metals_ref[rows(near, 64, BY), :]
        for x in range(1, BX - 1):
            at = 64 + 16 * (x - 1)
            rest[at : at + 16, :] = src_ref[rows(x * BY + near + step, 16, plane), :]
        rest[96:100, :] = cy_ref[rows(near, 4, BY), :]
        rest[100:ZROWS, :] = jnp.zeros((ZROWS - 100, NZ), F32)
    for out, high in ((xa_ref, even_x), (xb_ref, 1 - even_x)):
        near = jnp.where(high == 1, BX - 1, 0) * BY
        step = jnp.where(high == 1, -1, 1) * BY
        tile = 0
        pieces = [(src_ref, k * BX * BY + near) for k in range(COMP)]
        pieces += [(src_ref, k * BX * BY + near + step) for k in range(NMET)]
        pieces += [(metals_ref, k * BX * BY + near) for k in range(NMET)]
        pieces += [(dens_ref, near), (dens_ref, near + step), (dens_ref, near + 2 * step)]
        pieces += [(cx_ref, near)]
        for ref, at in pieces:
            out[tile * BY : tile * BY + BY, :] = ref[pl.ds(pl.multiple_of(at, BY), BY), :]
            tile += 1
    for out, alone in (
        (ya_ref, alone_ya), (yb_ref, alone_yb), (za_ref, alone_ya), (zb_ref, alone_yb),
        (xa_ref, alone_xa), (xb_ref, alone_xb),
    ):
        clear(out, alone)


def clear(ref, alone):
    @pl.when(alone)
    def _():
        ref[...] = jnp.zeros(ref.shape, F32)


def corner_kernel(ya_ref, yb_ref, xa_ref, xb_ref, ca_ref, cb_ref):
    del xa_ref, xb_ref
    even_x, alone_a, alone_b = place("gx")
    for out, high in ((ca_ref, even_x), (cb_ref, 1 - even_x)):
        near = jnp.where(high == 1, BX - 1, 0)
        step = jnp.where(high == 1, -1, 1)
        at = pl.multiple_of(jnp.where(high == 1, 80, 64), 16)
        for side, y_ref in enumerate((ya_ref, yb_ref)):
            base = side * 48
            out[base : base + 16, :] = y_ref[rows(near, 16, BX), :]
            out[base + 16 : base + 32, :] = y_ref[rows(near + step, 16, BX), :]
            out[base + 32 : base + 48, :] = y_ref[pl.ds(at, 16), :]
            base = 96 + side * 9
            out[base : base + 1, :] = y_ref[pl.ds(96 + near, 1), :]
            for i, (w, q) in enumerate(DENSITIES):
                out[base + 1 + i : base + 2 + i, :] = y_ref[pl.ds(100 + 4 * w + near + q * step, 1), :]
    clear(ca_ref, alone_a)
    clear(cb_ref, alone_b)


def layout_kernel(
    src_ref, ya_ref, yb_ref, xa_ref, xb_ref, za_ref, zb_ref, dens_ref, cy_ref,
    se_ref, de_ref, mx_ref, my_ref, cxl_ref, cye_ref,
):
    even_x = place("gx")[0]
    even_y = place("gy")[0]
    a = za_ref[...]
    b = zb_ref[...]
    low = jnp.where(even_y == 1, b, a)
    high_part = jnp.where(even_y == 1, a, b)
    de_ref[...] = jnp.zeros(de_ref.shape, F32)

    for x in range(BX):
        at = x * BY
        d_at = (x + 3) * DPITCH + 16
        de_ref[d_at : d_at + BY, :] = dens_ref[at : at + BY, :]
        cye_ref[x * PITCH + 8 : x * PITCH + 16, :] = cy_ref[at : at + BY, :]
        for k in range(COMP):
            s_at = (k * 8 + x + 2) * PITCH + 8
            se_ref[s_at : s_at + BY, :] = src_ref[(k * BX + x) * BY : (k * BX + x + 1) * BY, :]

    for y_ref, high in ((ya_ref, even_y), (yb_ref, 1 - even_y)):
        is_high = high == 1
        r1 = jnp.where(is_high, 16, 7)
        r2 = jnp.where(is_high, 17, 6)
        for k in range(NMET):
            at = k * BX
            base = (k * 8 + 2) * PITCH
            se_ref[rows(base + r1, BX, PITCH), :] = y_ref[at : at + BX, :]
        for i, x in enumerate((0, BX - 1)):
            se_ref[rows((x + 2) * PITCH + r2, NMET, 8 * PITCH), :] = y_ref[64 + 16 * i : 80 + 16 * i, :]
        base = (NMET * 8 + 2) * PITCH
        se_ref[rows(base + r1, BX, PITCH), :] = y_ref[96:100, :]
        for w in range(3):
            d_row = jnp.where(is_high, 24 + w, 15 - w)
            de_ref[rows(3 * DPITCH + d_row, BX, DPITCH), :] = y_ref[100 + 4 * w : 104 + 4 * w, :]
    for side, part in enumerate((low, high_part)):
        for k in range(NMET):
            my_ref[side, k * 8 + 2 : k * 8 + 2 + BX, :] = part[k * BX : k * BX + BX, :]
        for x in range(1, BX - 1):
            r2 = (6, 17)[side]
            se_ref[rows((x + 2) * PITCH + r2, NMET, 8 * PITCH), :] = part[48 + 16 * x : 64 + 16 * x, :]
    cye_ref[rows(7, BX, PITCH), :] = low[96:100, :]

    for x_ref, high in ((xa_ref, even_x), (xb_ref, 1 - even_x)):
        is_high = high == 1
        p1 = jnp.where(is_high, 6, 1)
        p2 = jnp.where(is_high, 7, 0)
        for k in range(COMP):
            at = pl.multiple_of((k * 8 + p1) * PITCH + 8, 8)
            se_ref[pl.ds(at, BY), :] = x_ref[k * BY : k * BY + BY, :]
        for k in range(NMET):
            at = pl.multiple_of((k * 8 + p2) * PITCH + 8, 8)
            tile = COMP + k
            se_ref[pl.ds(at, BY), :] = x_ref[tile * BY : tile * BY + BY, :]
            tile = COMP + NMET + k
            mx_ref[high, k * BY : k * BY + BY, :] = x_ref[tile * BY : tile * BY + BY, :]
        for w in range(3):
            tile = COMP + 2 * NMET + w
            plane = jnp.where(is_high, 7 + w, 2 - w)
            at = pl.multiple_of(plane * DPITCH + 16, 8)
            de_ref[pl.ds(at, BY), :] = x_ref[tile * BY : tile * BY + BY, :]
        tile = COMP + 2 * NMET + 3
        cxl_ref[high] = x_ref[tile * BY : tile * BY + BY, :]


def finish_kernel(
    se_in_ref, de_in_ref, mx_ref, my_ref, cxl_ref, cye_ref, ca_ref, cb_ref,
    metals_ref, energy_ref, cx_ref, cy_ref, cz_ref,
    out_hbm, energy_out_hbm, se_ref, de_ref,
    out_ref, energy_out_ref, sems,
    rw_ref, ys_ref, ee_ref,
):
    del se_in_ref, de_in_ref
    even_x = place("gx")[0]
    even_y = place("gy")[0]
    lane = lax.broadcasted_iota(jnp.int32, (1, NZ), 1)
    not_first = lane > 0
    not_last = lane < NZ - 1

    def prev_z(v):
        return pltpu.roll(v, 1, 1)

    def next_z(v):
        return pltpu.roll(v, NZ - 1, 1)

    def masked_prev(v):
        return jnp.where(not_first, prev_z(v), 0.0)

    def masked_next(v):
        return jnp.where(not_last, next_z(v), 0.0)

    for c_ref, high in ((ca_ref, even_x), (cb_ref, 1 - even_x)):
        is_high = high == 1
        p1 = jnp.where(is_high, 6, 1)
        p2 = jnp.where(is_high, 7, 0)
        for side, y_high in enumerate((even_y, 1 - even_y)):
            base = 48 * side
            y_is_high = y_high == 1
            r1 = jnp.where(y_is_high, 16, 7)
            r2 = jnp.where(y_is_high, 17, 6)
            se_ref[rows(p1 * PITCH + r1, NMET, 8 * PITCH), :] = c_ref[base : base + 16, :]
            se_ref[rows(p2 * PITCH + r1, NMET, 8 * PITCH), :] = c_ref[base + 16 : base + 32, :]
            se_ref[rows(p1 * PITCH + r2, NMET, 8 * PITCH), :] = c_ref[base + 32 : base + 48, :]
            base = 96 + 9 * side
            se_ref[pl.ds((NMET * 8 + p1) * PITCH + r1, 1), :] = c_ref[base : base + 1, :]
            for i, (w, q) in enumerate(DENSITIES):
                d_row = jnp.where(y_is_high, 24 + w, 15 - w)
                plane = jnp.where(is_high, 7 + q, 2 - q)
                de_ref[pl.ds(plane * DPITCH + d_row, 1), :] = c_ref[base + 1 + i : base + 2 + i, :]

    columns = []
    for p in range(10):
        at = p * DPITCH + 8
        columns.append(
            de_ref[at - 1 : at + 23, :] + de_ref[at : at + 24, :] + de_ref[at + 1 : at + 25, :]
        )
    for p in range(8):
        flat = columns[p] + columns[p + 1] + columns[p + 2]
        weight = flat + masked_prev(flat) + masked_next(flat)
        inside = weight > 0.0
        rw_ref[p * PITCH : (p + 1) * PITCH, :] = jnp.where(
            inside, 1.0 / jnp.where(inside, weight, 1.0), 0.0
        )

    copies = []
    for first in range(NMET, -1, -GROUP):
        group = [first] if first == NMET else range(first, first + GROUP)
        share_sums(group, se_ref, rw_ref, ys_ref)
        for k in group:
            for p in range(2, 6) if k == NMET else range(1, 7):
                dens = de_ref[(p + 1) * DPITCH + 16 : (p + 1) * DPITCH + 24, :]
                at = (k * 8 + p) * BY
                flat = (
                    ys_ref[at - BY : at, :] + ys_ref[at : at + BY, :] + ys_ref[at + BY : at + 2 * BY, :]
                )
                collected = flat + masked_prev(flat) + masked_next(flat)
                deposit = dens * collected
                if k == NMET:
                    cell = (p - 2) * BY
                    energy_out_ref[cell : cell + BY, :] = energy_ref[cell : cell + BY, :] + deposit
                    continue
                if p == 1:
                    metal = mx_ref[0, k * BY : k * BY + BY, :]
                elif p == 6:
                    metal = mx_ref[1, k * BY : k * BY + BY, :]
                else:
                    cell = (k * BX + p - 2) * BY
                    metal = metals_ref[cell : cell + BY, :]
                e_at = (k * 8 + p) * PITCH + 8
                ee_ref[e_at : e_at + BY, :] = metal + deposit
        if first == NMET:
            copies.append(pltpu.make_async_copy(energy_out_ref, energy_out_hbm, sems.at[0]))
            copies[-1].start()
            continue

        for side in range(2):
            row = (7, 16)[side]
            dens = de_ref[rows(DPITCH + row + 8, 8, DPITCH), :]
            inv = [rw_ref[rows(row - 1 + d, 8, PITCH), :] for d in range(3)]
            for k in group:
                value = None
                for d in range(3):
                    term = se_ref[rows(k * 8 * PITCH + row - 1 + d, 8, PITCH), :] * inv[d]
                    value = term if value is None else value + term
                flat = value + pltpu.roll(value, 1, 0) + pltpu.roll(value, 7, 0)
                deposit = dens * (flat + masked_prev(flat) + masked_next(flat))
                ee_ref[rows(k * 8 * PITCH + row, 8, PITCH), :] = (
                    my_ref[side, k * 8 : k * 8 + 8, :] + deposit
                )

        for x in range(BX):
            at = x * BY
            cx_up = cx_ref[at : at + BY, :]
            cx_low = cxl_ref[0] if x == 0 else cx_ref[at - BY : at, :]
            cy_up = cy_ref[at : at + BY, :]
            cy_low = cye_ref[x * PITCH + 7 : x * PITCH + 15, :]
            cz_up = cz_ref[at : at + BY, :]
            cz_low = masked_prev(cz_up)
            to_next = [-jnp.minimum(c, 0.0) for c in (cx_up, cy_up, cz_up)]
            from_prev = [jnp.maximum(c, 0.0) for c in (cx_low, cy_low, cz_low)]
            middle = 1.0
            for up, low in ((cx_up, cx_low), (cy_up, cy_low), (cz_up, cz_low)):
                middle = middle - jnp.maximum(up, 0.0) + jnp.minimum(low, 0.0)
            to_next[2] = jnp.where(not_last, to_next[2], 0.0)
            for k in group:
                e_at = (k * 8 + x + 2) * PITCH + 8
                own = ee_ref[e_at : e_at + BY, :]
                result = middle * own
                result = result + to_next[0] * ee_ref[e_at + PITCH : e_at + PITCH + BY, :]
                result = result + from_prev[0] * ee_ref[e_at - PITCH : e_at - PITCH + BY, :]
                result = result + to_next[1] * ee_ref[e_at + 1 : e_at + 1 + BY, :]
                result = result + from_prev[1] * ee_ref[e_at - 1 : e_at - 1 + BY, :]
                result = result + to_next[2] * next_z(own)
                result = result + from_prev[2] * prev_z(own)
                cell = (k * BX + x) * BY
                out_ref[cell : cell + BY, :] = result
        piece = pl.ds(first * BX * BY, GROUP * BX * BY)
        copies.append(
            pltpu.make_async_copy(out_ref.at[piece], out_hbm.at[piece], sems.at[len(copies)])
        )
        copies[-1].start()
    for copy in copies:
        copy.wait()


def share_sums(group, se_ref, rw_ref, ys_ref):
    for p in range(8):
        inv = [rw_ref[p * PITCH + 7 + d : p * PITCH + 15 + d, :] for d in range(3)]
        for k in group:
            if k == NMET and p in (0, 7):
                continue
            at = (k * 8 + p) * PITCH + 7
            value = None
            for d in range(3):
                term = se_ref[at + d : at + d + BY, :] * inv[d]
                value = term if value is None else value + term
            ys_ref[(k * 8 + p) * BY : (k * 8 + p) * BY + BY, :] = value


def swaps():
    nx = lax.axis_size("gx")
    ny = lax.axis_size("gy")
    rounds = []
    for along_x in (True, False):
        for first in (0, 1):
            pairs = []
            for x in range(nx):
                for y in range(ny):
                    place_, count = (x, nx) if along_x else (y, ny)
                    mate = place_ + 1 if place_ % 2 == first else place_ - 1
                    if 0 <= mate < count:
                        to = (mate, y) if along_x else (x, mate)
                    elif along_x and ny % 2 == 0:
                        to = (x, (y + ny // 2) % ny)
                    elif not along_x and nx % 2 == 0:
                        to = (x + 1 - 2 * (x % 2), y)
                    else:
                        to = (x, y)
                    pairs.append((x * ny + y, to[0] * ny + to[1]))
            rounds.append(pairs)
    return rounds


def swap(value, pairs):
    return lax.ppermute(value, ("gx", "gy"), pairs)


VM = pl.BlockSpec(memory_space=pltpu.VMEM)
HB = pl.BlockSpec(memory_space=pltpu.HBM)


def buffer(count):
    return pltpu.VMEM((count, NZ), F32)


def body(masses, table, star_mask, density, metals, energy, courant_x, courant_y, courant_z):
    cells = BX * BY
    masses = masses.reshape(BINS, cells, NZ)
    star_mask, density, energy, courant_x, courant_y, courant_z = (
        a.reshape(cells, NZ) for a in (star_mask, density, energy, courant_x, courant_y, courant_z)
    )
    metals = metals.reshape(NMET * cells, NZ)
    src, ya, yb, xa, xb, za, zb, *local = pl.pallas_call(
        sources_kernel,
        name="sources",
        out_shape=[buffer(COMP * cells)]
        + [buffer(count) for count in (YROWS, YROWS, XROWS, XROWS, ZROWS, ZROWS)]
        + [buffer(cells), buffer(NMET * cells)] + [buffer(cells)] * 4,
        in_specs=[HB] * 9,
        out_specs=[VM] * 13,
        scratch_shapes=[
            pltpu.VMEM((BINS, cells, NZ), BF16),
            pltpu.VMEM((COMP, BINS), BF16),
            pltpu.VMEM((cells, NZ), jnp.int32),
            pltpu.VMEM(((COMP + 1) * BY, BINS * BY), BF16),
            pltpu.VMEM((24, BINS * BY), F32),
            pltpu.SemaphoreType.DMA((CHUNKS,)),
            pltpu.SemaphoreType.DMA((8,)),
        ],
        compiler_params=pltpu.CompilerParams(vmem_limit_bytes=32 * 1024 * 1024),
    )(
        *(
            pltpu.with_memory_space_constraint(a, pltpu.HBM)
            for a in (
                masses, table.T, star_mask, density, metals, energy, courant_x, courant_y, courant_z
            )
        )
    )
    pairs_xa, pairs_xb, pairs_ya, pairs_yb = swaps()
    ya = swap(ya, pairs_ya)
    yb = swap(yb, pairs_yb)
    xa = swap(xa, pairs_xa)
    xb = swap(xb, pairs_xb)
    za = swap(za, pairs_ya)
    zb = swap(zb, pairs_yb)
    ca, cb = pl.pallas_call(
        corner_kernel,
        name="corners",
        out_shape=[buffer(CROWS), buffer(CROWS)],
        in_specs=[VM] * 4,
        out_specs=[VM, VM],
        compiler_params=pltpu.CompilerParams(vmem_limit_bytes=4 * 1024 * 1024),
    )(*(pltpu.with_memory_space_constraint(a, pltpu.VMEM) for a in (ya, yb, xa, xb)))
    ca = swap(ca, pairs_xa)
    cb = swap(cb, pairs_xb)
    dens, metals, energy, cx, cy, cz = local
    in_vmem = functools.partial(pltpu.with_memory_space_constraint, memory_space=pltpu.VMEM)
    shape_se, shape_de = buffer(COMP * 8 * PITCH), buffer(10 * DPITCH)
    operands = [src, ya, yb, xa, xb, za, zb, dens, cy]
    laid = pl.pallas_call(
        layout_kernel,
        name="layout",
        out_shape=[
            shape_se,
            shape_de,
            pltpu.VMEM((2, NMET * BY, NZ), F32),
            pltpu.VMEM((2, NMET * 8, NZ), F32),
            pltpu.VMEM((2, BY, NZ), F32),
            buffer(BX * PITCH),
        ],
        in_specs=[VM] * len(operands),
        out_specs=[VM] * 6,
        compiler_params=pltpu.CompilerParams(vmem_limit_bytes=16 * 1024 * 1024),
    )(*map(in_vmem, operands))
    operands = [*laid, ca, cb, metals, energy, cx, cy, cz]
    advected, energy_out, _, _ = pl.pallas_call(
        finish_kernel,
        name="finish",
        out_shape=[
            jax.ShapeDtypeStruct((NMET * cells, NZ), F32),
            jax.ShapeDtypeStruct((cells, NZ), F32),
            shape_se,
            shape_de,
        ],
        in_specs=[VM] * len(operands),
        out_specs=[HB, HB, VM, VM],
        input_output_aliases={0: 2, 1: 3},
        scratch_shapes=[
            pltpu.VMEM((NMET * cells, NZ), F32),
            pltpu.VMEM((cells, NZ), F32),
            pltpu.SemaphoreType.DMA((1 + NMET // GROUP,)),
            pltpu.VMEM((8 * PITCH, NZ), F32),
            pltpu.VMEM((COMP * 8 * BY, NZ), F32),
            pltpu.VMEM((NMET * 8 * PITCH, NZ), F32),
        ],
        compiler_params=pltpu.CompilerParams(vmem_limit_bytes=32 * 1024 * 1024),
    )(*map(in_vmem, operands))
    return advected.reshape(NMET, BX, BY, NZ), energy_out.reshape(BX, BY, NZ)


def solution(mesh):
    field = P("gx", "gy", None)
    stack = P(None, "gx", "gy", None)
    in_specs = (stack, P(), field, field, stack, field, field, field, field)
    out_specs = (stack, field)
    return jax.shard_map(body, mesh=mesh, in_specs=in_specs, out_specs=out_specs, check_vma=False)
```

```python
import functools

import jax
import jax.numpy as jnp
from jax import lax
from jax.experimental import pallas as pl
from jax.experimental.pallas import tpu as pltpu
from jax.sharding import PartitionSpec as P

F32 = jnp.float32
BF16 = jnp.bfloat16
BINS = 256
COMP = 17
NMET = 16
BX = 4
BY = 8
NZ = 128
CHUNKS = 8
GROUP = 4
YROWS = 112
ZROWS = 114
XROWS = 424
CROWS = 114
PITCH = 24
DENSITIES = [(w, q) for w in range(3) for q in range(3) if w + q < 4]
DPITCH = 40


def rows(start, count, stride=1):
    return pl.ds(start, count) if stride == 1 else pl.ds(start, count, stride)


def place(axis):
    index = lax.axis_index(axis)
    last = index == lax.axis_size(axis) - 1
    odd = index % 2
    alone_a = jnp.logical_and(odd == 0, last)
    alone_b = jnp.logical_or(index == 0, jnp.logical_and(odd == 1, last))
    return 1 - odd, alone_a, alone_b


def sources_kernel(
    masses_hbm, table_hbm, star_hbm, dens_hbm, metals_hbm, energy_hbm, cx_hbm, cy_hbm, cz_hbm,
    src_ref, ya_ref, yb_ref, xa_ref, xb_ref, za_ref, zb_ref,
    dens_ref, metals_ref, energy_ref, cx_ref, cy_ref, cz_ref,
    mass_buf, table_ref, star_ref, expand_ref, wide_ref, mass_sems, sems,
):
    small = [
        (table_hbm, table_ref), (star_hbm, star_ref), (dens_hbm, dens_ref), (metals_hbm, metals_ref),
        (cx_hbm, cx_ref), (cy_hbm, cy_ref), (cz_hbm, cz_ref), (energy_hbm, energy_ref),
    ]
    small_copies = [
        pltpu.make_async_copy(
            hbm, ref if i < 2 else ref.at[pl.ds(0, hbm.shape[0])], sems.at[i]
        )
        for i, (hbm, ref) in enumerate(small)
    ]
    per = BINS // CHUNKS
    copies = [
        pltpu.make_async_copy(
            masses_hbm.at[pl.ds(c * per, per)], mass_buf.at[pl.ds(c * per, per)], mass_sems.at[c]
        )
        for c in range(CHUNKS)
    ]
    small_copies[0].start()
    for copy in copies:
        copy.start()
    for copy in small_copies[1:]:
        copy.start()

    width = BINS * BY
    group = lax.broadcasted_iota(jnp.int32, (8, NZ), 1) // BY
    same = (
        lax.broadcasted_iota(jnp.int32, (BY, NZ), 1) % BY
        == lax.broadcasted_iota(jnp.int32, (BY, NZ), 0)
    )
    upper = lax.broadcasted_iota(jnp.int32, (1, 16, NZ), 1) < BY
    small_copies[0].wait()
    turned = table_ref[...].astype(F32)
    turned = jnp.concatenate([turned, jnp.zeros((24 - COMP, BINS), F32)], axis=0)

    def expand(c):
        tiles = width // NZ // CHUNKS
        for t in range(c * tiles, (c + 1) * tiles):
            first = 16 * t
            half = first // NZ
            columns = slice(t * NZ, (t + 1) * NZ)
            for r in range(3):
                tile = turned[8 * r : 8 * r + 8, half * NZ : (half + 1) * NZ]
                wide_ref[8 * r : 8 * r + 8, columns] = jnp.take_along_axis(
                    tile, group + first % NZ, axis=1
                )
            for k in range(0, COMP + 1, 2):
                lines = [
                    jnp.where(same, jnp.broadcast_to(wide_ref[i : i + 1, columns], (BY, NZ)), 0.0)
                    for i in (k, k + 1)
                ]
                expand_ref[k * BY : k * BY + 16, columns] = jnp.concatenate(lines, axis=0).astype(BF16)

    expand(0)
    total = None
    for c in range(CHUNKS):
        copies[c].wait()
        part = mass_buf[c * per : (c + 1) * per]
        blocks = []
        for j in range(2):
            both = part[:, 16 * j : 16 * j + 16].reshape(per // 2, 2, 16, NZ)
            even, odd = both[:, 0], both[:, 1]
            blocks.append(jnp.where(upper, even, pltpu.roll(odd, 8, 1)).reshape(per * BY, NZ))
            blocks.append(jnp.where(upper, pltpu.roll(even, 8, 1), odd).reshape(per * BY, NZ))
        right = jnp.concatenate(blocks, axis=1)
        left = expand_ref[:, c * per * BY : (c + 1) * per * BY]
        prod = jnp.dot(left, right, preferred_element_type=F32)
        total = prod if total is None else total + prod
        if c + 1 < CHUNKS:
            expand(c + 1)
    for copy in small_copies[1:]:
        copy.wait()
    for x in range(BX):
        mask = star_ref[x * BY : x * BY + BY, :].astype(F32)
        for k in range(COMP):
            at = (k * BX + x) * BY
            piece = total[k * BY : k * BY + BY, x * NZ : (x + 1) * NZ]
            src_ref[at : at + BY, :] = piece * mask

    even_x, alone_xa, alone_xb = place("gx")
    even_y, alone_ya, alone_yb = place("gy")
    plane = BX * BY
    for out, rest, high in ((ya_ref, za_ref, even_y), (yb_ref, zb_ref, 1 - even_y)):
        near = jnp.where(high == 1, BY - 1, 0)
        step = jnp.where(high == 1, -1, 1)
        out[0:64, :] = src_ref[rows(near, 64, BY), :]
        for i, x in enumerate((0, BX - 1)):
            out[64 + 16 * i : 80 + 16 * i, :] = src_ref[rows(x * BY + near + step, 16, plane), :]
        out[96:100, :] = src_ref[rows(NMET * plane + near, 4, BY), :]
        out[100:104, :] = dens_ref[rows(near, 4, BY), :]
        out[104:108, :] = dens_ref[rows(near + step, 4, BY), :]
        out[108:112, :] = dens_ref[rows(near + 2 * step, 4, BY), :]
        rest[0:64, :] = metals_ref[rows(near, 64, BY), :]
        for x in range(1, BX - 1):
            at = 64 + 16 * (x - 1)
            rest[at : at + 16, :] = src_ref[rows(x * BY + near + step, 16, plane), :]
        rest[96:100, :] = cy_ref[rows(near, 4, BY), :]
        rest[100:ZROWS, :] = jnp.zeros((ZROWS - 100, NZ), F32)
    for out, high in ((xa_ref, even_x), (xb_ref, 1 - even_x)):
        near = jnp.where(high == 1, BX - 1, 0) * BY
        step = jnp.where(high == 1, -1, 1) * BY
        tile = 0
        pieces = [(src_ref, k * BX * BY + near) for k in range(COMP)]
        pieces += [(src_ref, k * BX * BY + near + step) for k in range(NMET)]
        pieces += [(metals_ref, k * BX * BY + near) for k in range(NMET)]
        pieces += [(dens_ref, near), (dens_ref, near + step), (dens_ref, near + 2 * step)]
        pieces += [(cx_ref, near)]
        for ref, at in pieces:
            out[tile * BY : tile * BY + BY, :] = ref[pl.ds(pl.multiple_of(at, BY), BY), :]
            tile += 1
    for out, alone in (
        (ya_ref, alone_ya), (yb_ref, alone_yb), (za_ref, alone_ya), (zb_ref, alone_yb),
        (xa_ref, alone_xa), (xb_ref, alone_xb),
    ):
        clear(out, alone)


def clear(ref, alone):
    @pl.when(alone)
    def _():
        ref[...] = jnp.zeros(ref.shape, F32)


def corner_kernel(ya_ref, yb_ref, xa_ref, xb_ref, ca_ref, cb_ref):
    del xa_ref, xb_ref
    even_x, alone_a, alone_b = place("gx")
    for out, high in ((ca_ref, even_x), (cb_ref, 1 - even_x)):
        near = jnp.where(high == 1, BX - 1, 0)
        step = jnp.where(high == 1, -1, 1)
        at = pl.multiple_of(jnp.where(high == 1, 80, 64), 16)
        for side, y_ref in enumerate((ya_ref, yb_ref)):
            base = side * 48
            out[base : base + 16, :] = y_ref[rows(near, 16, BX), :]
            out[base + 16 : base + 32, :] = y_ref[rows(near + step, 16, BX), :]
            out[base + 32 : base + 48, :] = y_ref[pl.ds(at, 16), :]
            base = 96 + side * 9
            out[base : base + 1, :] = y_ref[pl.ds(96 + near, 1), :]
            for i, (w, q) in enumerate(DENSITIES):
                out[base + 1 + i : base + 2 + i, :] = y_ref[pl.ds(100 + 4 * w + near + q * step, 1), :]
    clear(ca_ref, alone_a)
    clear(cb_ref, alone_b)


def layout_kernel(
    src_ref, ya_ref, yb_ref, xa_ref, xb_ref, za_ref, zb_ref, dens_ref, cy_ref,
    se_ref, de_ref, mx_ref, my_ref, cxl_ref, cye_ref,
):
    even_x = place("gx")[0]
    even_y = place("gy")[0]
    a = za_ref[...]
    b = zb_ref[...]
    low = jnp.where(even_y == 1, b, a)
    high_part = jnp.where(even_y == 1, a, b)
    de_ref[...] = jnp.zeros(de_ref.shape, F32)

    for x in range(BX):
        at = x * BY
        d_at = (x + 3) * DPITCH + 16
        de_ref[d_at : d_at + BY, :] = dens_ref[at : at + BY, :]
        cye_ref[x * PITCH + 8 : x * PITCH + 16, :] = cy_ref[at : at + BY, :]
        for k in range(COMP):
            s_at = (k * 8 + x + 2) * PITCH + 8
            se_ref[s_at : s_at + BY, :] = src_ref[(k * BX + x) * BY : (k * BX + x + 1) * BY, :]

    for y_ref, high in ((ya_ref, even_y), (yb_ref, 1 - even_y)):
        is_high = high == 1
        r1 = jnp.where(is_high, 16, 7)
        r2 = jnp.where(is_high, 17, 6)
        for k in range(NMET):
            at = k * BX
            base = (k * 8 + 2) * PITCH
            se_ref[rows(base + r1, BX, PITCH), :] = y_ref[at : at + BX, :]
        for i, x in enumerate((0, BX - 1)):
            se_ref[rows((x + 2) * PITCH + r2, NMET, 8 * PITCH), :] = y_ref[64 + 16 * i : 80 + 16 * i, :]
        base = (NMET * 8 + 2) * PITCH
        se_ref[rows(base + r1, BX, PITCH), :] = y_ref[96:100, :]
        for w in range(3):
            d_row = jnp.where(is_high, 24 + w, 15 - w)
            de_ref[rows(3 * DPITCH + d_row, BX, DPITCH), :] = y_ref[100 + 4 * w : 104 + 4 * w, :]
    for side, part in enumerate((low, high_part)):
        for k in range(NMET):
            my_ref[side, k * 8 + 2 : k * 8 + 2 + BX, :] = part[k * BX : k * BX + BX, :]
        for x in range(1, BX - 1):
            r2 = (6, 17)[side]
            se_ref[rows((x + 2) * PITCH + r2, NMET, 8 * PITCH), :] = part[48 + 16 * x : 64 + 16 * x, :]
    cye_ref[rows(7, BX, PITCH), :] = low[96:100, :]

    for x_ref, high in ((xa_ref, even_x), (xb_ref, 1 - even_x)):
        is_high = high == 1
        p1 = jnp.where(is_high, 6, 1)
        p2 = jnp.where(is_high, 7, 0)
        for k in range(COMP):
            at = pl.multiple_of((k * 8 + p1) * PITCH + 8, 8)
            se_ref[pl.ds(at, BY), :] = x_ref[k * BY : k * BY + BY, :]
        for k in range(NMET):
            at = pl.multiple_of((k * 8 + p2) * PITCH + 8, 8)
            tile = COMP + k
            se_ref[pl.ds(at, BY), :] = x_ref[tile * BY : tile * BY + BY, :]
            tile = COMP + NMET + k
            mx_ref[high, k * BY : k * BY + BY, :] = x_ref[tile * BY : tile * BY + BY, :]
        for w in range(3):
            tile = COMP + 2 * NMET + w
            plane = jnp.where(is_high, 7 + w, 2 - w)
            at = pl.multiple_of(plane * DPITCH + 16, 8)
            de_ref[pl.ds(at, BY), :] = x_ref[tile * BY : tile * BY + BY, :]
        tile = COMP + 2 * NMET + 3
        cxl_ref[high] = x_ref[tile * BY : tile * BY + BY, :]


def finish_kernel(
    se_in_ref, de_in_ref, mx_ref, my_ref, cxl_ref, cye_ref, ca_ref, cb_ref,
    metals_ref, energy_ref, cx_ref, cy_ref, cz_ref,
    out_hbm, energy_out_hbm, se_ref, de_ref,
    out_ref, energy_out_ref, sems,
    rw_ref, ys_ref, ee_ref,
):
    del se_in_ref, de_in_ref
    even_x = place("gx")[0]
    even_y = place("gy")[0]
    lane = lax.broadcasted_iota(jnp.int32, (1, NZ), 1)
    not_first = lane > 0
    not_last = lane < NZ - 1

    def prev_z(v):
        return pltpu.roll(v, 1, 1)

    def next_z(v):
        return pltpu.roll(v, NZ - 1, 1)

    def masked_prev(v):
        return jnp.where(not_first, prev_z(v), 0.0)

    def masked_next(v):
        return jnp.where(not_last, next_z(v), 0.0)

    for c_ref, high in ((ca_ref, even_x), (cb_ref, 1 - even_x)):
        is_high = high == 1
        p1 = jnp.where(is_high, 6, 1)
        p2 = jnp.where(is_high, 7, 0)
        for side, y_high in enumerate((even_y, 1 - even_y)):
            base = 48 * side
            y_is_high = y_high == 1
            r1 = jnp.where(y_is_high, 16, 7)
            r2 = jnp.where(y_is_high, 17, 6)
            se_ref[rows(p1 * PITCH + r1, NMET, 8 * PITCH), :] = c_ref[base : base + 16, :]
            se_ref[rows(p2 * PITCH + r1, NMET, 8 * PITCH), :] = c_ref[base + 16 : base + 32, :]
            se_ref[rows(p1 * PITCH + r2, NMET, 8 * PITCH), :] = c_ref[base + 32 : base + 48, :]
            base = 96 + 9 * side
            se_ref[pl.ds((NMET * 8 + p1) * PITCH + r1, 1), :] = c_ref[base : base + 1, :]
            for i, (w, q) in enumerate(DENSITIES):
                d_row = jnp.where(y_is_high, 24 + w, 15 - w)
                plane = jnp.where(is_high, 7 + q, 2 - q)
                de_ref[pl.ds(plane * DPITCH + d_row, 1), :] = c_ref[base + 1 + i : base + 2 + i, :]

    columns = []
    for p in range(10):
        at = p * DPITCH + 8
        columns.append(
            de_ref[at - 1 : at + 23, :] + de_ref[at : at + 24, :] + de_ref[at + 1 : at + 25, :]
        )
    for p in range(8):
        flat = columns[p] + columns[p + 1] + columns[p + 2]
        weight = flat + masked_prev(flat) + masked_next(flat)
        inside = weight > 0.0
        rw_ref[p * PITCH : (p + 1) * PITCH, :] = jnp.where(
            inside, 1.0 / jnp.where(inside, weight, 1.0), 0.0
        )

    copies = []
    for first in range(NMET, -1, -GROUP):
        group = [first] if first == NMET else range(first, first + GROUP)
        share_sums(group, se_ref, rw_ref, ys_ref)
        for k in group:
            for p in range(2, 6) if k == NMET else range(1, 7):
                dens = de_ref[(p + 1) * DPITCH + 16 : (p + 1) * DPITCH + 24, :]
                at = (k * 8 + p) * BY
                flat = (
                    ys_ref[at - BY : at, :] + ys_ref[at : at + BY, :] + ys_ref[at + BY : at + 2 * BY, :]
                )
                collected = flat + masked_prev(flat) + masked_next(flat)
                deposit = dens * collected
                if k == NMET:
                    cell = (p - 2) * BY
                    energy_out_ref[cell : cell + BY, :] = energy_ref[cell : cell + BY, :] + deposit
                    continue
                if p == 1:
                    metal = mx_ref[0, k * BY : k * BY + BY, :]
                elif p == 6:
                    metal = mx_ref[1, k * BY : k * BY + BY, :]
                else:
                    cell = (k * BX + p - 2) * BY
                    metal = metals_ref[cell : cell + BY, :]
                e_at = (k * 8 + p) * PITCH + 8
                ee_ref[e_at : e_at + BY, :] = metal + deposit
        if first == NMET:
            copies.append(pltpu.make_async_copy(energy_out_ref, energy_out_hbm, sems.at[0]))
            copies[-1].start()
            continue

        for side in range(2):
            row = (7, 16)[side]
            dens = de_ref[rows(DPITCH + row + 8, 8, DPITCH), :]
            inv = [rw_ref[rows(row - 1 + d, 8, PITCH), :] for d in range(3)]
            for k in group:
                value = None
                for d in range(3):
                    term = se_ref[rows(k * 8 * PITCH + row - 1 + d, 8, PITCH), :] * inv[d]
                    value = term if value is None else value + term
                flat = value + pltpu.roll(value, 1, 0) + pltpu.roll(value, 7, 0)
                deposit = dens * (flat + masked_prev(flat) + masked_next(flat))
                ee_ref[rows(k * 8 * PITCH + row, 8, PITCH), :] = (
                    my_ref[side, k * 8 : k * 8 + 8, :] + deposit
                )

        for x in range(BX):
            at = x * BY
            cx_up = cx_ref[at : at + BY, :]
            cx_low = cxl_ref[0] if x == 0 else cx_ref[at - BY : at, :]
            cy_up = cy_ref[at : at + BY, :]
            cy_low = cye_ref[x * PITCH + 7 : x * PITCH + 15, :]
            cz_up = cz_ref[at : at + BY, :]
            cz_low = masked_prev(cz_up)
            to_next = [-jnp.minimum(c, 0.0) for c in (cx_up, cy_up, cz_up)]
            from_prev = [jnp.maximum(c, 0.0) for c in (cx_low, cy_low, cz_low)]
            middle = 1.0
            for up, low in ((cx_up, cx_low), (cy_up, cy_low), (cz_up, cz_low)):
                middle = middle - jnp.maximum(up, 0.0) + jnp.minimum(low, 0.0)
            to_next[2] = jnp.where(not_last, to_next[2], 0.0)
            for k in group:
                e_at = (k * 8 + x + 2) * PITCH + 8
                own = ee_ref[e_at : e_at + BY, :]
                result = middle * own
                result = result + to_next[0] * ee_ref[e_at + PITCH : e_at + PITCH + BY, :]
                result = result + from_prev[0] * ee_ref[e_at - PITCH : e_at - PITCH + BY, :]
                result = result + to_next[1] * ee_ref[e_at + 1 : e_at + 1 + BY, :]
                result = result + from_prev[1] * ee_ref[e_at - 1 : e_at - 1 + BY, :]
                result = result + to_next[2] * next_z(own)
                result = result + from_prev[2] * prev_z(own)
                cell = (k * BX + x) * BY
                out_ref[cell : cell + BY, :] = result
        piece = pl.ds(first * BX * BY, GROUP * BX * BY)
        copies.append(
            pltpu.make_async_copy(out_ref.at[piece], out_hbm.at[piece], sems.at[len(copies)])
        )
        copies[-1].start()
    for copy in copies:
        copy.wait()


def share_sums(group, se_ref, rw_ref, ys_ref):
    for p in range(8):
        inv = [rw_ref[p * PITCH + 7 + d : p * PITCH + 15 + d, :] for d in range(3)]
        for k in group:
            if k == NMET and p in (0, 7):
                continue
            at = (k * 8 + p) * PITCH + 7
            value = None
            for d in range(3):
                term = se_ref[at + d : at + d + BY, :] * inv[d]
                value = term if value is None else value + term
            ys_ref[(k * 8 + p) * BY : (k * 8 + p) * BY + BY, :] = value


def swaps():
    nx = lax.axis_size("gx")
    ny = lax.axis_size("gy")
    rounds = []
    for along_x in (True, False):
        for first in (0, 1):
            pairs = []
            for x in range(nx):
                for y in range(ny):
                    place_, count = (x, nx) if along_x else (y, ny)
                    mate = place_ + 1 if place_ % 2 == first else place_ - 1
                    if 0 <= mate < count:
                        to = (mate, y) if along_x else (x, mate)
                    elif along_x and ny % 2 == 0:
                        to = (x, (y + ny // 2) % ny)
                    elif not along_x and nx % 2 == 0:
                        to = (x + 1 - 2 * (x % 2), y)
                    else:
                        to = (x, y)
                    pairs.append((x * ny + y, to[0] * ny + to[1]))
            rounds.append(pairs)
    return rounds


def swap(value, pairs):
    return lax.ppermute(value, ("gx", "gy"), pairs)


VM = pl.BlockSpec(memory_space=pltpu.VMEM)
HB = pl.BlockSpec(memory_space=pltpu.HBM)


def buffer(count):
    return pltpu.VMEM((count, NZ), F32)


def body(masses, table, star_mask, density, metals, energy, courant_x, courant_y, courant_z):
    cells = BX * BY
    masses = masses.reshape(BINS, cells, NZ)
    star_mask, density, energy, courant_x, courant_y, courant_z = (
        a.reshape(cells, NZ) for a in (star_mask, density, energy, courant_x, courant_y, courant_z)
    )
    metals = metals.reshape(NMET * cells, NZ)
    src, ya, yb, xa, xb, za, zb, *local = pl.pallas_call(
        sources_kernel,
        name="sources",
        out_shape=[buffer(COMP * cells + BY)]
        + [buffer(count) for count in (YROWS, YROWS, XROWS, XROWS, ZROWS, ZROWS)]
        + [buffer(cells + BY), buffer(NMET * cells + BY)] + [buffer(cells + BY)] * 4,
        in_specs=[HB] * 9,
        out_specs=[VM] * 13,
        scratch_shapes=[
            pltpu.VMEM((BINS, cells, NZ), BF16),
            pltpu.VMEM((COMP, BINS), BF16),
            pltpu.VMEM((cells, NZ), jnp.int32),
            pltpu.VMEM(((COMP + 1) * BY, BINS * BY), BF16),
            pltpu.VMEM((24, BINS * BY), F32),
            pltpu.SemaphoreType.DMA((CHUNKS,)),
            pltpu.SemaphoreType.DMA((8,)),
        ],
        compiler_params=pltpu.CompilerParams(vmem_limit_bytes=32 * 1024 * 1024),
    )(
        *(
            pltpu.with_memory_space_constraint(a, pltpu.HBM)
            for a in (
                masses, table.T, star_mask, density, metals, energy, courant_x, courant_y, courant_z
            )
        )
    )
    pairs_xa, pairs_xb, pairs_ya, pairs_yb = swaps()
    ya = swap(ya, pairs_ya)
    yb = swap(yb, pairs_yb)
    xa = swap(xa, pairs_xa)
    xb = swap(xb, pairs_xb)
    za = swap(za, pairs_ya)
    zb = swap(zb, pairs_yb)
    ca, cb = pl.pallas_call(
        corner_kernel,
        name="corners",
        out_shape=[buffer(CROWS), buffer(CROWS)],
        in_specs=[VM] * 4,
        out_specs=[VM, VM],
        compiler_params=pltpu.CompilerParams(vmem_limit_bytes=4 * 1024 * 1024),
    )(*(pltpu.with_memory_space_constraint(a, pltpu.VMEM) for a in (ya, yb, xa, xb)))
    ca = swap(ca, pairs_xa)
    cb = swap(cb, pairs_xb)
    dens, metals, energy, cx, cy, cz = local
    in_vmem = functools.partial(pltpu.with_memory_space_constraint, memory_space=pltpu.VMEM)
    shape_se, shape_de = buffer(COMP * 8 * PITCH), buffer(10 * DPITCH)
    operands = [src, ya, yb, xa, xb, za, zb, dens, cy]
    laid = pl.pallas_call(
        layout_kernel,
        name="layout",
        out_shape=[
            shape_se,
            shape_de,
            pltpu.VMEM((2, NMET * BY, NZ), F32),
            pltpu.VMEM((2, NMET * 8, NZ), F32),
            pltpu.VMEM((2, BY, NZ), F32),
            buffer(BX * PITCH),
        ],
        in_specs=[VM] * len(operands),
        out_specs=[VM] * 6,
        compiler_params=pltpu.CompilerParams(vmem_limit_bytes=16 * 1024 * 1024),
    )(*map(in_vmem, operands))
    operands = [*laid, ca, cb, metals, energy, cx, cy, cz]
    advected, energy_out, _, _ = pl.pallas_call(
        finish_kernel,
        name="finish",
        out_shape=[
            jax.ShapeDtypeStruct((NMET * cells, NZ), F32),
            jax.ShapeDtypeStruct((cells, NZ), F32),
            shape_se,
            shape_de,
        ],
        in_specs=[VM] * len(operands),
        out_specs=[HB, HB, VM, VM],
        input_output_aliases={0: 2, 1: 3},
        scratch_shapes=[
            pltpu.VMEM((NMET * cells, NZ), F32),
            pltpu.VMEM((cells, NZ), F32),
            pltpu.SemaphoreType.DMA((1 + NMET // GROUP,)),
            pltpu.VMEM((8 * PITCH, NZ), F32),
            pltpu.VMEM((COMP * 8 * BY, NZ), F32),
            pltpu.VMEM((NMET * 8 * PITCH, NZ), F32),
        ],
        compiler_params=pltpu.CompilerParams(vmem_limit_bytes=32 * 1024 * 1024),
    )(*map(in_vmem, operands))
    return advected.reshape(NMET, BX, BY, NZ), energy_out.reshape(BX, BY, NZ)


def solution(mesh):
    field = P("gx", "gy", None)
    stack = P(None, "gx", "gy", None)
    in_specs = (stack, P(), field, field, stack, field, field, field, field)
    out_specs = (stack, field)
    return jax.shard_map(body, mesh=mesh, in_specs=in_specs, out_specs=out_specs, check_vma=False)
```
